32 devices in a mesh: groups: 2 (over x), ex: 16 (over z, y, core).
Axes of the slice: x: 2, y: 2, z: 4, core: 2. Of those that a mesh axis runs over, the one named last changes fastest.
Arguments:
- inputs: bfloat16 [8192, 4096], P('ex', 'groups'), parts along dimension 1, may hold values from -6 to 6
- out_grads: bfloat16 [28672, 4096], P('ex', 'groups'), parts along dimension 1, may hold values from -6 to 6
- proj_in: bfloat16 [8192, 64], P('ex'), may hold values from -0.0625 to 0.0625
- proj_out: bfloat16 [28672, 64], P('ex'), may hold values from -0.03125 to 0.03125
- queries: bfloat16 [128, 4096], P('ex'), may hold values from -0.01171875 to 0.01171875
Outputs:
- scores: float32 [64, 128], P(('groups', 'ex')), parts along dimension 0
The draws below stay inside these ranges and needn't reach their ends.
There are 2 independent parts, one for each index of `groups`. The reference program is written for one: setup_inputs(seed, part) draws one part's arguments, and reference() takes and returns one part's arrays. A program takes and returns all parts, laid end to end along the dimension named above; an argument that names none is the same for every part. Nothing has to cross between parts.
All inputs are finite; a program needn't handle non-finite values.
Results may differ from the reference program's by a relative error of at most 0.0029.
Values may be sent and summed in bfloat16 or wider, within the bound.
No kernel may reach another device: no remote copies, remote signals or barrier semaphores. Data moves between devices by JAX's collectives and lax.ppermute only.
A program may use at most 64 MiB of HBM per device.

```python
import jax
import jax.numpy as jnp
from jax import lax

D = 8192
FF = 28672
RANK = 64
SEQ = 64
TOKENS = 2048
QUERIES = 128


def strengthened(entries, key, source, target, blocks, factor):
    def block_of(dim):
        return (jnp.arange(entries.shape[dim]) // (entries.shape[dim] // blocks)).reshape((-1,) + (1,) * (entries.ndim - 1 - dim))

    one_side = jax.random.permutation(key, blocks)[block_of(target)]
    far = (block_of(target) + blocks // 2) % blocks
    return jnp.where((block_of(source) == one_side) | (block_of(source) == far), factor * entries, entries)


def steps_of(stream_key, dims, shards, low, top_value):
    loudness, own = 1.0, jax.random.fold_in(stream_key, 6)
    for axis_at, shards_of in shards:
        steps = jnp.exp(jax.random.uniform(jax.random.fold_in(own, axis_at), (shards_of,), jnp.float32, low / len(shards), top_value / len(shards)))
        loudness = loudness * jnp.repeat(steps, dims[axis_at] // shards_of).reshape([-1 if axis == axis_at else 1 for axis in range(len(dims))])
    return loudness


def gaussian(stream_key, extent, scale, most, shards=(), held_as=jnp.bfloat16):
    factor_of = steps_of(stream_key, extent, shards, -0.22, 0.18) if shards else 1.0
    drawn = jax.random.normal(stream_key, extent, jnp.float32) * scale * factor_of
    return jnp.minimum(jnp.maximum(drawn, -most), most).astype(held_as)


def heavy_noise(stream_key, shape, deviation, reach, cuts, heavy, held_as=jnp.bfloat16):
    entries = deviation * jax.random.normal(stream_key, shape, jnp.float32)
    if cuts:
        entries = entries * steps_of(stream_key, shape, cuts, -0.22, 0.18)
    return jnp.clip(strengthened(entries, jax.random.fold_in(stream_key, 3), *heavy), -reach, reach).astype(held_as)


def setup_inputs(seed: int = 0, part: int = 0) -> dict:
    keys = jax.random.split(jax.random.key(seed), 6)
    part_keys = jax.random.split(jax.random.fold_in(keys[5], part), 6)
    inputs = heavy_noise(part_keys[0], (D, TOKENS), 1.0, 6.0, ((0, 16),), (0, 1, 16, 2.0))
    out_grads = heavy_noise(part_keys[1], (FF, TOKENS), 1.0, 6.0, ((0, 16),), (0, 1, 16, 2.0))
    proj_in = gaussian(keys[2], (D, RANK), D ** -0.5, 0.0625, ((0, 16),))
    proj_out = gaussian(keys[3], (FF, RANK), FF ** -0.5, 0.03125, ((0, 16),))
    queries = gaussian(keys[4], (QUERIES, RANK * RANK), (RANK * RANK * SEQ) ** -0.5, 0.01171875, ((0, 16),))
    return dict(inputs=inputs, out_grads=out_grads, proj_in=proj_in, proj_out=proj_out, queries=queries)


def reference(inputs, out_grads, proj_in, proj_out, queries):
    low_in = jnp.dot(inputs.T, proj_in, preferred_element_type=jnp.float32)
    low_out = jnp.dot(out_grads.T, proj_out, preferred_element_type=jnp.float32)
    count = low_in.shape[0] // SEQ
    per_in = low_in.reshape(count, SEQ, RANK)
    per_out = low_out.reshape(count, SEQ, RANK)
    grads = jnp.einsum("nsi,nsj->nij", per_out, per_in, precision=lax.Precision.HIGHEST)
    grads = grads.reshape(count, RANK * RANK).astype(jnp.bfloat16)
    return jnp.dot(grads, queries.T, preferred_element_type=jnp.float32)
```

```python
import functools

import jax
import jax.numpy as jnp
from jax import lax
from jax.experimental import pallas as pl
from jax.experimental.pallas import tpu as pltpu
from jax.sharding import PartitionSpec as P

SEQ = 64
VMEM_BYTES = 48 * 1024 * 1024
ROWS_BY_ROWS = (((0,), (0,)), ((), ()))
LANES_BY_LANES = (((1,), (1,)), ((), ()))


def project_kernel(
    other_core, width, x_hbm, w_hbm, p_in_hbm, p_out_hbm, out_ref, x_buf, w_buf, p_in, p_out, p_sems, x_sems, w_sems
):
    here = lax.axis_index("ex")
    blocks = out_ref.shape[0]
    rank = p_in.shape[1]
    copies = [
        pltpu.make_async_copy(p_in_hbm, p_in, p_sems.at[0]),
        pltpu.make_async_copy(p_out_hbm, p_out, p_sems.at[1]),
    ]
    for block in range(blocks):
        owner = lax.bitwise_xor(here, 2 * block + other_core)
        columns = pl.ds(pl.multiple_of(owner * width, width), width)
        place = pl.ds((block % 2) * width, width)
        copies.append(pltpu.make_async_copy(x_hbm.at[:, columns], x_buf.at[block // 2, :, place], x_sems.at[block]))
        copies.append(pltpu.make_async_copy(w_hbm.at[:, columns], w_buf.at[block // 2, :, place], w_sems.at[block]))
    for copy in copies:
        copy.start()
    copies[0].wait()
    copies[1].wait()
    p_in_t = p_in[...].T
    p_out_t = p_out[...].T
    for pair in range(blocks // 2):
        for copy in copies[2 + 4 * pair : 6 + 4 * pair]:
            copy.wait()
        low_in = jnp.dot(p_in_t, x_buf[pair], preferred_element_type=jnp.float32)
        low_out = jnp.dot(p_out_t, w_buf[pair], preferred_element_type=jnp.float32)
        for side in range(2):
            out_ref[2 * pair + side, :rank, :] = low_in[:, side * width : (side + 1) * width]
            out_ref[2 * pair + side, rank:, :] = low_out[:, side * width : (side + 1) * width]


def project(other_core, inputs, out_grads, proj_in, proj_out, devices):
    width = inputs.shape[1] // devices
    blocks = devices // 2
    rank = proj_in.shape[1]
    features, units = inputs.shape[0], out_grads.shape[0]
    hbm = pl.BlockSpec(memory_space=pltpu.HBM)
    return pl.pallas_call(
        functools.partial(project_kernel, other_core, width),
        out_shape=jax.ShapeDtypeStruct((blocks, 2 * rank, width), jnp.float32),
        in_specs=[hbm] * 4,
        out_specs=pl.BlockSpec(memory_space=pltpu.VMEM),
        scratch_shapes=[
            pltpu.VMEM((blocks // 2, features, 2 * width), jnp.bfloat16),
            pltpu.VMEM((blocks // 2, units, 2 * width), jnp.bfloat16),
            pltpu.VMEM(proj_in.shape, jnp.bfloat16),
            pltpu.VMEM(proj_out.shape, jnp.bfloat16),
            pltpu.SemaphoreType.DMA((2,)),
            pltpu.SemaphoreType.DMA((blocks,)),
            pltpu.SemaphoreType.DMA((blocks,)),
        ],
        compiler_params=pltpu.CompilerParams(vmem_limit_bytes=VMEM_BYTES),
        cost_estimate=pl.CostEstimate(
            flops=2 * (features + units) * rank * blocks * width,
            bytes_accessed=2 * (features + units) * blocks * width,
            transcendentals=0,
        ),
    )(inputs, out_grads, proj_in, proj_out)


def add_kernel(kept_ref, came_ref, *out_refs):
    for block, out_ref in enumerate(out_refs):
        out_ref[...] = (kept_ref[block] + came_ref[block]).astype(out_ref.dtype)


def add_halves(kept, came, types):
    return pl.pallas_call(
        add_kernel,
        out_shape=[jax.ShapeDtypeStruct(kept.shape[1:], dtype) for dtype in types],
        compiler_params=pltpu.CompilerParams(vmem_limit_bytes=VMEM_BYTES),
    )(kept, came)


def score_kernel(rank, *refs):
    *parts, queries_ref, out_ref, total_ref, grads_ref = refs
    total = parts[0][...]
    for part in parts[1:]:
        total = total + part[...].astype(jnp.float32)
    total_ref[...] = total
    tokens = total.shape[1]
    examples = tokens // SEQ
    low_in = total_ref[:rank, :]
    even = total_ref[pl.ds(rank, rank // 2, stride=2), :]
    odd = total_ref[pl.ds(rank + 1, rank // 2, stride=2), :]
    token = lax.broadcasted_iota(jnp.int32, (rank, tokens), 1)
    for n in range(examples):
        mine = jnp.where((token >= n * SEQ) & (token < (n + 1) * SEQ), low_in, 0.0)
        for side, rows in enumerate((even, odd)):
            grads_ref[n, :, side * rank : (side + 1) * rank] = lax.dot_general(
                rows, mine, LANES_BY_LANES, precision=lax.Precision.HIGHEST, preferred_element_type=jnp.float32
            )
    ones = jnp.ones((8, 2 * rank), jnp.float32)
    step = min(128, queries_ref.shape[0])
    for first in range(0, queries_ref.shape[0], step):
        sums = [jnp.zeros((step, 2 * rank), jnp.float32) for _ in range(examples)]
        for k in range(rank // 2):
            query = queries_ref[first : first + step, k * 2 * rank : (k + 1) * 2 * rank].astype(jnp.float32)
            for n in range(examples):
                sums[n] = sums[n] + query * grads_ref[n, k : k + 1, :]
        for n in range(examples):
            row = lax.dot_general(
                ones, sums[n], LANES_BY_LANES, precision=lax.Precision.HIGHEST, preferred_element_type=jnp.float32
            )
            out_ref[n : n + 1, first : first + step] = row[0:1, :]


def score(parts, queries, rank):
    tokens = parts[0].shape[1]
    examples = tokens // SEQ
    return pl.pallas_call(
        functools.partial(score_kernel, rank),
        out_shape=jax.ShapeDtypeStruct((examples, queries.shape[0]), jnp.float32),
        scratch_shapes=[
            pltpu.VMEM((2 * rank, tokens), jnp.float32),
            pltpu.VMEM((examples, rank // 2, 2 * rank), jnp.float32),
        ],
        compiler_params=pltpu.CompilerParams(vmem_limit_bytes=VMEM_BYTES),
    )(*parts, queries)


def shards(inputs, out_grads, proj_in, proj_out, queries):
    devices = lax.axis_size("ex")
    chips = devices // 2
    rank = proj_in.shape[1]
    every_query = lax.all_gather(queries, "ex", axis=0, tiled=True)

    def swap(array, distance):
        return lax.ppermute(array, "ex", [(i, i ^ distance) for i in range(devices)])

    given = project(1, inputs, out_grads, proj_in, proj_out, devices)
    came = swap(given, 1)
    kept = project(0, inputs, out_grads, proj_in, proj_out, devices)
    types = [jnp.float32 if block < chips // 2 else jnp.bfloat16 for block in range(chips)]
    sums = add_halves(kept, came, types)
    parts = [sums[0]] + [swap(sums[block], 2 * block) for block in range(1, chips)]
    return score(parts, every_query, rank)


def solution(mesh):
    return jax.shard_map(
        shards,
        mesh=mesh,
        in_specs=(
            P("ex", "groups"),
            P("ex", "groups"),
            P("ex", None),
            P("ex", None),
            P("ex", None),
        ),
        out_specs=P(("groups", "ex"), None),
        check_vma=False,
    )
```

```python
import functools

import jax
import jax.numpy as jnp
from jax import lax
from jax.experimental import pallas as pl
from jax.experimental.pallas import tpu as pltpu
from jax.sharding import PartitionSpec as P

SEQ = 64
VMEM_BYTES = 48 * 1024 * 1024
LANES_BY_LANES = (((1,), (1,)), ((), ()))


def project_kernel(
    other_core, width, x_hbm, w_hbm, p_in_hbm, p_out_hbm, out_ref, x_buf, w_buf, p_in, p_out, p_sems, x_sems, w_sems
):
    core = lax.rem(lax.axis_index("ex") + other_core, 2)
    blocks = out_ref.shape[0]
    rank = p_in.shape[0]
    copies = [
        pltpu.make_async_copy(p_in_hbm, p_in, p_sems.at[0]),
        pltpu.make_async_copy(p_out_hbm, p_out, p_sems.at[1]),
    ]
    for block in range(blocks):
        columns = pl.ds(pl.multiple_of((2 * block + core) * width, width), width)
        place = pl.ds((block % 2) * width, width)
        copies.append(pltpu.make_async_copy(x_hbm.at[:, columns], x_buf.at[block // 2, :, place], x_sems.at[block]))
        copies.append(pltpu.make_async_copy(w_hbm.at[:, columns], w_buf.at[block // 2, :, place], w_sems.at[block]))
    for copy in copies:
        copy.start()
    copies[0].wait()
    copies[1].wait()
    for pair in range(blocks // 2):
        for copy in copies[2 + 4 * pair : 6 + 4 * pair]:
            copy.wait()
        low_in = jnp.dot(p_in[...], x_buf[pair], preferred_element_type=jnp.float32)
        low_out = jnp.dot(p_out[...], w_buf[pair], preferred_element_type=jnp.float32)
        for side in range(2):
            out_ref[2 * pair + side, :rank, :] = low_in[:, side * width : (side + 1) * width]
            out_ref[2 * pair + side, rank:, :] = low_out[:, side * width : (side + 1) * width]


def project(other_core, inputs, out_grads, proj_in_t, proj_out_t, devices):
    width = inputs.shape[1] // devices
    blocks = devices // 2
    rank = proj_in_t.shape[0]
    features, units = inputs.shape[0], out_grads.shape[0]
    hbm = pl.BlockSpec(memory_space=pltpu.HBM)
    return pl.pallas_call(
        functools.partial(project_kernel, other_core, width),
        out_shape=jax.ShapeDtypeStruct((blocks, 2 * rank, width), jnp.float32),
        in_specs=[hbm] * 4,
        out_specs=pl.BlockSpec(memory_space=pltpu.VMEM),
        scratch_shapes=[
            pltpu.VMEM((blocks // 2, features, 2 * width), jnp.bfloat16),
            pltpu.VMEM((blocks // 2, units, 2 * width), jnp.bfloat16),
            pltpu.VMEM(proj_in_t.shape, jnp.bfloat16),
            pltpu.VMEM(proj_out_t.shape, jnp.bfloat16),
            pltpu.SemaphoreType.DMA((2,)),
            pltpu.SemaphoreType.DMA((blocks,)),
            pltpu.SemaphoreType.DMA((blocks,)),
        ],
        compiler_params=pltpu.CompilerParams(vmem_limit_bytes=VMEM_BYTES),
        cost_estimate=pl.CostEstimate(
            flops=2 * (features + units) * rank * blocks * width,
            bytes_accessed=2 * (features + units) * blocks * width,
            transcendentals=0,
        ),
    )(inputs, out_grads, proj_in_t, proj_out_t)


def add_kernel(rank, kept_ref, came_ref, out_ref):
    total = kept_ref[...] + came_ref[...]
    low_in = total[:, :rank, :]
    high = low_in.astype(jnp.bfloat16)
    out_ref[:, :rank, :] = high
    out_ref[:, rank : 2 * rank, :] = total[:, rank:, :].astype(jnp.bfloat16)
    out_ref[:, 2 * rank :, :] = (low_in - high.astype(jnp.float32)).astype(jnp.bfloat16)


def add_halves(kept, came, rank):
    blocks, _, width = kept.shape
    return pl.pallas_call(
        functools.partial(add_kernel, rank),
        out_shape=jax.ShapeDtypeStruct((blocks, 3 * rank, width), jnp.bfloat16),
        compiler_params=pltpu.CompilerParams(vmem_limit_bytes=VMEM_BYTES),
    )(kept, came)


def score_kernel(parts_ref, own_ref, other_ref, out_ref, out_t_ref, grads_ref, sums_ref):
    rank = parts_ref.shape[1] // 3
    tokens = parts_ref.shape[2]
    examples = tokens // SEQ
    core = lax.rem(lax.axis_index("ex"), 2)
    total = jnp.sum(parts_ref[...].astype(jnp.float32), axis=0)
    low_in = total[:rank, :] + total[2 * rank :, :]
    out_t_ref[...] = total[rank : 2 * rank, :]
    even = out_t_ref[pl.ds(0, rank // 2, stride=2), :]
    odd = out_t_ref[pl.ds(1, rank // 2, stride=2), :]
    token = lax.broadcasted_iota(jnp.int32, (rank, tokens), 1)
    for n in range(examples):
        mine = jnp.where((token >= n * SEQ) & (token < (n + 1) * SEQ), low_in, 0.0)
        for side, rows in enumerate((even, odd)):
            grads_ref[n, :, side * rank : (side + 1) * rank] = lax.dot_general(
                rows, mine, LANES_BY_LANES, precision=lax.Precision.HIGHEST, preferred_element_type=jnp.float32
            )
    chips, held = sums_ref.shape[1], sums_ref.shape[3]
    for offset, queries_ref in enumerate((own_ref, other_ref)):
        place = lax.rem(core + offset, 2)
        step = min(8, chips)
        for first in range(0, chips, step):
            sums = [jnp.zeros((step * held, 2 * rank), jnp.float32) for _ in range(examples)]
            for k in range(rank // 2):
                query = queries_ref[first * held : (first + step) * held, k * 2 * rank : (k + 1) * 2 * rank]
                query = query.astype(jnp.float32)
                for n in range(examples):
                    sums[n] = sums[n] + query * grads_ref[n, k : k + 1, :]
            for n in range(examples):
                sums_ref[n, first : first + step, place] = sums[n].reshape(step, held, 2 * rank)
    ones = jnp.ones((8, 2 * rank), jnp.float32)
    for n in range(examples):
        row = lax.dot_general(
            ones,
            sums_ref[n].reshape(chips * 2 * held, 2 * rank),
            LANES_BY_LANES,
            precision=lax.Precision.HIGHEST,
            preferred_element_type=jnp.float32,
        )
        out_ref[n : n + 1, :] = row[0:1, :]


def score(parts, own_queries, other_queries):
    chips, rows, tokens = parts.shape
    rank = rows // 3
    examples = tokens // SEQ
    held = own_queries.shape[0] // chips
    return pl.pallas_call(
        score_kernel,
        out_shape=jax.ShapeDtypeStruct((examples, 2 * own_queries.shape[0]), jnp.float32),
        scratch_shapes=[
            pltpu.VMEM((rank, tokens), jnp.float32),
            pltpu.VMEM((examples, rank // 2, 2 * rank), jnp.float32),
            pltpu.VMEM((examples, chips, 2, held, 2 * rank), jnp.float32),
        ],
        compiler_params=pltpu.CompilerParams(vmem_limit_bytes=VMEM_BYTES),
    )(parts, own_queries, other_queries)


def shards(inputs, out_grads, proj_in, proj_out, queries):
    devices = lax.axis_size("ex")
    rank = proj_in.shape[1]
    same_core = [list(range(core, devices, 2)) for core in range(2)]
    other_core = [(i, i ^ 1) for i in range(devices)]
    own_queries = lax.all_gather(queries, "ex", axis=0, tiled=True, axis_index_groups=same_core)
    inputs = pltpu.with_memory_space_constraint(inputs, pltpu.HBM)
    out_grads = pltpu.with_memory_space_constraint(out_grads, pltpu.HBM)
    given = project(1, inputs, out_grads, proj_in.T, proj_out.T, devices)
    came = lax.ppermute(given, "ex", other_core)
    kept = project(0, inputs, out_grads, proj_in.T, proj_out.T, devices)
    sums = add_halves(kept, came, rank)
    parts = lax.all_to_all(sums, "ex", split_axis=0, concat_axis=0, tiled=True, axis_index_groups=same_core)
    own_queries, parts = lax.optimization_barrier((own_queries, parts))
    other_queries = lax.ppermute(own_queries, "ex", other_core)
    return score(parts, own_queries, other_queries)


def solution(mesh):
    return jax.shard_map(
        shards,
        mesh=mesh,
        in_specs=(
            P("ex", "groups"),
            P("ex", "groups"),
            P("ex", None),
            P("ex", None),
            P("ex", None),
        ),
        out_specs=P(("groups", "ex"), None),
        check_vma=False,
    )
```

```python
import functools

import jax
import jax.numpy as jnp
from jax import lax
from jax.experimental import pallas as pl
from jax.experimental.pallas import tpu as pltpu
from jax.sharding import PartitionSpec as P

SEQ = 64
VMEM_BYTES = 32 * 1024 * 1024
LANES_BY_LANES = (((1,), (1,)), ((), ()))
HBM_SPEC = pl.BlockSpec(memory_space=pltpu.HBM)
VMEM_SPEC = pl.BlockSpec(memory_space=pltpu.VMEM)
PARAMS = pltpu.CompilerParams(vmem_limit_bytes=VMEM_BYTES)


def slab_copies(flip, width, x_hbm, w_hbm, x_buf, w_buf, sems):
    here = lax.axis_index("ex")
    copies = []
    for block in range(2 * x_buf.shape[0]):
        owner = lax.bitwise_xor(here, 4 * block + flip)
        columns = pl.ds(pl.multiple_of(owner * width, width), width)
        place = pl.ds((block % 2) * width, width)
        copies.append(pltpu.make_async_copy(x_hbm.at[:, columns], x_buf.at[block // 2, :, place], sems.at[0, block]))
        copies.append(pltpu.make_async_copy(w_hbm.at[:, columns], w_buf.at[block // 2, :, place], sems.at[1, block]))
    return copies


def project_slab(slab, width, p_in, p_out, x_buf, w_buf, low_ref):
    rank = p_in.shape[0]
    low_in = jnp.dot(p_in[...], x_buf[slab], preferred_element_type=jnp.float32)
    low_out = jnp.dot(p_out[...], w_buf[slab], preferred_element_type=jnp.float32)
    for side in range(2):
        low_ref[2 * slab + side, :rank, :] = low_in[:, side * width : (side + 1) * width]
        low_ref[2 * slab + side, rank:, :] = low_out[:, side * width : (side + 1) * width]


def first_kernel(
    flip, next_flip, x_hbm, w_hbm, p_in_hbm, p_out_hbm, low_ref, p_in, p_out, x_next, w_next, x_buf, w_buf, p_sems, sems, next_sems
):
    width = low_ref.shape[2]
    p_copies = [
        pltpu.make_async_copy(p_in_hbm, p_in, p_sems.at[0]),
        pltpu.make_async_copy(p_out_hbm, p_out, p_sems.at[1]),
    ]
    copies = slab_copies(flip, width, x_hbm, w_hbm, x_buf, w_buf, sems)
    next_copies = slab_copies(next_flip, width, x_hbm, w_hbm, x_next, w_next, next_sems)
    for copy in p_copies + copies + next_copies:
        copy.start()
    for copy in p_copies:
        copy.wait()
    for slab in range(x_buf.shape[0]):
        for copy in copies[4 * slab : 4 * slab + 4]:
            copy.wait()
        project_slab(slab, width, p_in, p_out, x_buf, w_buf, low_ref)
    for copy in next_copies:
        copy.wait()


def middle_kernel(next_flip, x_hbm, w_hbm, p_in, p_out, x_buf, w_buf, low_ref, x_next, w_next, next_sems):
    width = low_ref.shape[2]
    next_copies = slab_copies(next_flip, width, x_hbm, w_hbm, x_next, w_next, next_sems)
    for copy in next_copies:
        copy.start()
    for slab in range(x_buf.shape[0]):
        project_slab(slab, width, p_in, p_out, x_buf, w_buf, low_ref)
    for copy in next_copies:
        copy.wait()


def last_kernel(p_in, p_out, x_buf, w_buf, low_ref):
    for slab in range(x_buf.shape[0]):
        project_slab(slab, low_ref.shape[2], p_in, p_out, x_buf, w_buf, low_ref)


class Projection:
    def __init__(self, inputs, out_grads, proj_in_t, proj_out_t, devices):
        self.hbm = [pltpu.with_memory_space_constraint(a, pltpu.HBM) for a in (inputs, out_grads)]
        self.proj = [pltpu.with_memory_space_constraint(a, pltpu.HBM) for a in (proj_in_t, proj_out_t)]
        self.blocks = devices // 4
        width = inputs.shape[1] // devices
        rank = proj_in_t.shape[0]
        self.low = jax.ShapeDtypeStruct((self.blocks, 2 * rank, width), jnp.float32)
        sizes = (inputs.shape[0], out_grads.shape[0])
        self.slabs = [(self.blocks // 2, size, 2 * width) for size in sizes]
        self.slab_types = [jax.ShapeDtypeStruct(slab, jnp.bfloat16) for slab in self.slabs]
        self.cost = pl.CostEstimate(
            flops=2 * sum(sizes) * rank * self.blocks * width,
            bytes_accessed=2 * sum(sizes) * self.blocks * width,
            transcendentals=0,
        )
        self.sems = pltpu.SemaphoreType.DMA((2, self.blocks))

    def first(self, flip, next_flip):
        proj_types = [jax.ShapeDtypeStruct(a.shape, a.dtype) for a in self.proj]
        low, p_in, p_out, x_next, w_next = pl.pallas_call(
            functools.partial(first_kernel, flip, next_flip),
            out_shape=[self.low] + proj_types + self.slab_types,
            in_specs=[HBM_SPEC] * 4,
            out_specs=[VMEM_SPEC] * 5,
            scratch_shapes=[pltpu.VMEM(slab, jnp.bfloat16) for slab in self.slabs]
            + [pltpu.SemaphoreType.DMA((2,)), self.sems, self.sems],
            compiler_params=PARAMS,
            cost_estimate=self.cost,
        )(*self.hbm, *self.proj)
        return low, (p_in, p_out), (x_next, w_next)

    def middle(self, next_flip, proj, slabs):
        low, x_next, w_next = pl.pallas_call(
            functools.partial(middle_kernel, next_flip),
            out_shape=[self.low] + self.slab_types,
            in_specs=[HBM_SPEC] * 2 + [VMEM_SPEC] * 4,
            out_specs=[VMEM_SPEC] * 3,
            scratch_shapes=[self.sems],
            compiler_params=PARAMS,
            cost_estimate=self.cost,
        )(*self.hbm, *proj, *slabs)
        return low, (x_next, w_next)

    def last(self, proj, slabs):
        return pl.pallas_call(
            last_kernel,
            out_shape=self.low,
            in_specs=[VMEM_SPEC] * 4,
            out_specs=VMEM_SPEC,
            compiler_params=PARAMS,
            cost_estimate=self.cost,
        )(*proj, *slabs)


def put_split(out_ref, low):
    rank = low.shape[0] // 2
    low_in = low[:rank, :]
    high = low_in.astype(jnp.bfloat16)
    out_ref[:rank, :] = high
    out_ref[rank : 2 * rank, :] = low[rank:, :].astype(jnp.bfloat16)
    out_ref[2 * rank :, :] = (low_in - high.astype(jnp.float32)).astype(jnp.bfloat16)


def get_split(ref):
    rank = ref.shape[0] // 3
    low_in = ref[:rank, :].astype(jnp.float32) + ref[2 * rank :, :].astype(jnp.float32)
    return jnp.concatenate([low_in, ref[rank : 2 * rank, :].astype(jnp.float32)], axis=0)


def add_given_kernel(kept_ref, came_ref, out_ref):
    for block in range(out_ref.shape[0]):
        put_split(out_ref.at[block], kept_ref[block] + came_ref[block])


def add_given(kept, came):
    blocks, rows, width = kept.shape
    return pl.pallas_call(
        add_given_kernel,
        out_shape=jax.ShapeDtypeStruct((blocks, rows // 2 * 3, width), jnp.bfloat16),
        compiler_params=PARAMS,
    )(kept, came)


def add_kept_kernel(kept_ref, came_ref, across_ref, *out_refs):
    for block, out_ref in enumerate(out_refs):
        total = kept_ref[block] + came_ref[block] + get_split(across_ref.at[block])
        if out_ref.dtype == jnp.float32:
            out_ref[...] = total
        else:
            put_split(out_ref, total)


def add_kept(kept, came, across):
    blocks, rows, width = kept.shape
    wide = jax.ShapeDtypeStruct((rows, width), jnp.float32)
    split = jax.ShapeDtypeStruct((rows // 2 * 3, width), jnp.bfloat16)
    return pl.pallas_call(
        add_kept_kernel,
        out_shape=[wide if 2 * block < blocks else split for block in range(blocks)],
        compiler_params=PARAMS,
    )(kept, came, across)


def stack_kernel(left_ref, right_ref, out_ref):
    out_ref[: left_ref.shape[0]] = left_ref[...]
    out_ref[left_ref.shape[0] :] = right_ref[...]


def stack(left, right):
    return pl.pallas_call(
        stack_kernel,
        out_shape=jax.ShapeDtypeStruct((2 * left.shape[0],) + left.shape[1:], left.dtype),
        compiler_params=PARAMS,
    )(left, right)


def score_kernel(parts_count, distances, *refs):
    part_refs, query_refs = refs[:parts_count], refs[parts_count : parts_count + 4]
    out_ref, out_t_ref, grads_ref, sums_ref = refs[parts_count + 4 :]
    rank, tokens = out_t_ref.shape
    examples = tokens // SEQ
    here = lax.axis_index("ex")
    core, chip = lax.rem(here, 2), lax.div(here, 2)
    total = part_refs[0][...]
    for part_ref in part_refs[1:]:
        total = total + (part_ref[...] if part_ref.dtype == jnp.float32 else get_split(part_ref))
    out_t_ref[...] = total[rank:, :]
    even = out_t_ref[pl.ds(0, rank // 2, stride=2), :]
    odd = out_t_ref[pl.ds(1, rank // 2, stride=2), :]
    token = lax.broadcasted_iota(jnp.int32, (rank, tokens), 1)
    for n in range(examples):
        mine = jnp.where((token >= n * SEQ) & (token < (n + 1) * SEQ), total[:rank, :], 0.0)
        for side, rows in enumerate((even, odd)):
            grads_ref[n, :, side * rank : (side + 1) * rank] = lax.dot_general(
                rows, mine, LANES_BY_LANES, precision=lax.Precision.HIGHEST, preferred_element_type=jnp.float32
            )
    chips, held = sums_ref.shape[1], sums_ref.shape[3]
    for index, queries_ref in enumerate(query_refs):
        place = lax.rem(core + index // 2, 2)
        count = queries_ref.shape[0]
        step = min(4, count)
        for first in range(0, count, step):
            sums = [jnp.zeros((step * held, 2 * rank), jnp.float32) for _ in range(examples)]
            for k in range(rank // 2):
                query = queries_ref[first : first + step, :, k * 2 * rank : (k + 1) * 2 * rank].astype(jnp.float32)
                query = query.reshape(step * held, 2 * rank)
                for n in range(examples):
                    sums[n] = sums[n] + query * grads_ref[n, k : k + 1, :]
            for part in range(step):
                source = lax.bitwise_xor(chip, distances[index % 2][first + part])
                for n in range(examples):
                    sums_ref[n, source, place] = sums[n][part * held : (part + 1) * held, :]
    ones = jnp.ones((8, 2 * rank), jnp.float32)
    for n in range(examples):
        row = lax.dot_general(
            ones,
            sums_ref[n].reshape(chips * 2 * held, 2 * rank),
            LANES_BY_LANES,
            precision=lax.Precision.HIGHEST,
            preferred_element_type=jnp.float32,
        )
        out_ref[n : n + 1, :] = row[0:1, :]


def score(parts, queries, distances, rank):
    tokens = parts[0].shape[1]
    examples = tokens // SEQ
    chips = len(distances[0]) + len(distances[1])
    held = queries[0].shape[1]
    return pl.pallas_call(
        functools.partial(score_kernel, len(parts), distances),
        out_shape=jax.ShapeDtypeStruct((examples, 2 * chips * held), jnp.float32),
        scratch_shapes=[
            pltpu.VMEM((rank, tokens), jnp.float32),
            pltpu.VMEM((examples, rank // 2, 2 * rank), jnp.float32),
            pltpu.VMEM((examples, chips, 2, held, 2 * rank), jnp.float32),
        ],
        compiler_params=PARAMS,
    )(*parts, *queries)


def shards(inputs, out_grads, proj_in, proj_out, queries):
    devices = lax.axis_size("ex")
    chips = devices // 2
    rank = proj_in.shape[1]

    def swap(array, distance):
        return lax.ppermute(array, "ex", [(i, i ^ distance) for i in range(devices)])

    together = lax.optimization_barrier

    steps = [1 << bit for bit in reversed(range(chips.bit_length() - 1))]
    held, distances = queries[None], [0]
    came_held = swap(held, 2 * steps[0])

    projection = Projection(inputs, out_grads, proj_in.T, proj_out.T, devices)
    low_11, proj, slabs = projection.first(3, 2)
    came_11 = swap(low_11, 1)
    low_10, slabs = projection.middle(1, proj, slabs)
    came_held, low_10 = together((came_held, low_10))
    across = add_given(low_10, came_11)
    for last, step in zip(steps, steps[1:-1]):
        held, distances = stack(held, came_held), distances + [distance ^ last for distance in distances]
        came_held = swap(held, 2 * step)
    held, across, slabs = together((held, across, slabs))
    across = swap(across, 2)
    low_01, slabs = projection.middle(0, proj, slabs)
    came_01 = swap(low_01, 1)
    came_held, low_01, across = together((came_held, low_01, across))
    held, distances = stack(held, came_held), distances + [distance ^ steps[-2] for distance in distances]
    held, slabs = together((held, slabs))
    came_held = swap(held, 2 * steps[-1])
    low_00 = projection.last(proj, slabs)
    sums = add_kept(low_00, came_01, across)
    order = list(range(chips // 4, chips // 2)) + list(range(1, chips // 4))
    came = {distance: swap(sums[distance], 4 * distance) for distance in order}
    held, came_held, came[order[0]] = together((held, came_held, came[order[0]]))
    parts = [sums[0]] + [came[distance] for distance in sorted(came)]
    every = [held, came_held]
    every = every + [swap(array, 1) for array in every]
    return score(parts, every, (distances, [distance ^ steps[-1] for distance in distances]), rank)


def solution(mesh):
    return jax.shard_map(
        shards,
        mesh=mesh,
        in_specs=(
            P("ex", "groups"),
            P("ex", "groups"),
            P("ex", None),
            P("ex", None),
            P("ex", None),
        ),
        out_specs=P(("groups", "ex"), None),
        check_vma=False,
    )
```

```python
import functools

import jax
import jax.numpy as jnp
from jax import lax
from jax.experimental import pallas as pl
from jax.experimental.pallas import tpu as pltpu
from jax.sharding import PartitionSpec as P

SEQ = 64
VMEM_BYTES = 32 * 1024 * 1024
LANES_BY_LANES = (((1,), (1,)), ((), ()))
HBM_SPEC = pl.BlockSpec(memory_space=pltpu.HBM)
VMEM_SPEC = pl.BlockSpec(memory_space=pltpu.VMEM)
PARAMS = pltpu.CompilerParams(vmem_limit_bytes=VMEM_BYTES)


def project_kernel(
    x_hbm, w_hbm, p_in_hbm, p_out_hbm, given_ref, kept_ref, x_buf, w_buf, p_in, p_out, low, p_sems, x_sems, w_sems
):
    here = lax.axis_index("ex")
    chips = given_ref.shape[0]
    rank, width = given_ref.shape[1] // 2, given_ref.shape[2]
    copies = [
        pltpu.make_async_copy(p_in_hbm, p_in, p_sems.at[0]),
        pltpu.make_async_copy(p_out_hbm, p_out, p_sems.at[1]),
    ]
    sides = []
    for top, hbm, buf, sems, matrix in ((0, x_hbm, x_buf, x_sems, p_in), (rank, w_hbm, w_buf, w_sems, p_out)):
        rows = buf.shape[0] // sems.shape[0]
        for chunk in range(sems.shape[0]):
            part = pl.ds(chunk * rows, rows)
            copy = pltpu.make_async_copy(hbm.at[part, :], buf.at[part, :], sems.at[chunk])
            sides.append((slice(top, top + rank), part, buf, matrix, copy, chunk == 0))
            copies.append(copy)
    for copy in copies:
        copy.start()
    for copy in copies[:2]:
        copy.wait()
    step = min(1024, low.shape[1])
    for lines, part, buf, matrix, copy, first in sides:
        copy.wait()
        for column in range(0, low.shape[1], step):
            columns = slice(column, column + step)
            product = jnp.dot(matrix[:, part], buf[part, columns], preferred_element_type=jnp.float32)
            low[lines, columns] = product if first else low[lines, columns] + product
    core = lax.rem(here, 2)
    chip = lax.div(here, 2)
    for distance in range(chips):
        place = lax.bitwise_xor(chip, distance)
        both = low[:, pl.ds(pl.multiple_of(place * 2 * width, 2 * width), 2 * width)]
        left, right = both[:, :width], both[:, width:]
        given_ref[distance] = jnp.where(core == 0, right, left)
        kept_ref[distance] = jnp.where(core == 0, left, right)


def project(inputs, out_grads, proj_in_t, proj_out_t, devices):
    arrays = [pltpu.with_memory_space_constraint(a, pltpu.HBM) for a in (inputs, out_grads, proj_in_t, proj_out_t)]
    width = inputs.shape[1] // devices
    rank = proj_in_t.shape[0]
    half = jax.ShapeDtypeStruct((devices // 2, 2 * rank, width), jnp.float32)
    chunks = [a.shape[0] // 256 if a.shape[0] % 256 == 0 else 1 for a in (inputs, out_grads)]
    return pl.pallas_call(
        project_kernel,
        out_shape=[half] * 2,
        in_specs=[HBM_SPEC] * 4,
        out_specs=[VMEM_SPEC] * 2,
        scratch_shapes=[pltpu.VMEM(a.shape, jnp.bfloat16) for a in arrays]
        + [pltpu.VMEM((2 * rank, inputs.shape[1]), jnp.float32), pltpu.SemaphoreType.DMA((2,))]
        + [pltpu.SemaphoreType.DMA((count,)) for count in chunks],
        compiler_params=PARAMS,
        cost_estimate=pl.CostEstimate(
            flops=2 * rank * (inputs.size + out_grads.size),
            bytes_accessed=2 * (inputs.size + out_grads.size),
            transcendentals=0,
        ),
    )(*arrays)


def add_kernel(kept_ref, came_ref, *out_refs):
    for block, out_ref in enumerate(out_refs):
        out_ref[...] = (kept_ref[block] + came_ref[block]).astype(out_ref.dtype)


def add_halves(kept, came, types):
    return pl.pallas_call(
        add_kernel,
        out_shape=[jax.ShapeDtypeStruct(kept.shape[1:], dtype) for dtype in types],
        compiler_params=PARAMS,
    )(kept, came)


def stack_kernel(*refs):
    *in_refs, out_ref = refs
    first = 0
    for in_ref in in_refs:
        out_ref[first : first + in_ref.shape[0]] = in_ref[...]
        first += in_ref.shape[0]


def stack(arrays):
    count = sum(array.shape[0] for array in arrays)
    return pl.pallas_call(
        stack_kernel,
        out_shape=jax.ShapeDtypeStruct((count,) + arrays[0].shape[1:], arrays[0].dtype),
        compiler_params=PARAMS,
    )(*arrays)


def score_kernel(parts_count, distances, *refs):
    part_refs, query_refs = refs[:parts_count], refs[parts_count : parts_count + len(distances)]
    out_ref, out_t_ref, grads_ref, sums_ref = refs[parts_count + len(distances) :]
    rank, tokens = out_t_ref.shape
    examples = tokens // SEQ
    here = lax.axis_index("ex")
    core, chip = lax.rem(here, 2), lax.div(here, 2)
    total = part_refs[0][...]
    for part_ref in part_refs[1:]:
        total = total + part_ref[...].astype(jnp.float32)
    out_t_ref[...] = total[rank:, :]
    even = out_t_ref[pl.ds(0, rank // 2, stride=2), :]
    odd = out_t_ref[pl.ds(1, rank // 2, stride=2), :]
    token = lax.broadcasted_iota(jnp.int32, (rank, tokens), 1)
    for n in range(examples):
        mine = jnp.where((token >= n * SEQ) & (token < (n + 1) * SEQ), total[:rank, :], 0.0)
        for side, rows in enumerate((even, odd)):
            grads_ref[n, :, side * rank : (side + 1) * rank] = lax.dot_general(
                rows, mine, LANES_BY_LANES, precision=lax.Precision.HIGHEST, preferred_element_type=jnp.float32
            )
    chips, held = sums_ref.shape[1], sums_ref.shape[3]
    for index, queries_ref in enumerate(query_refs):
        place = lax.rem(core + distances[index][0], 2)
        count = queries_ref.shape[0]
        step = 4 if count % 4 == 0 else 2
        for first in range(0, count, step):
            sums = [jnp.zeros((step * held, 2 * rank), jnp.float32) for _ in range(examples)]
            for k in range(rank // 2):
                query = queries_ref[first : first + step, :, k * 2 * rank : (k + 1) * 2 * rank].astype(jnp.float32)
                query = query.reshape(step * held, 2 * rank)
                for n in range(examples):
                    sums[n] = sums[n] + query * grads_ref[n, k : k + 1, :]
            for part in range(step):
                source = lax.bitwise_xor(chip, distances[index][1][first + part])
                for n in range(examples):
                    sums_ref[n, source, place] = sums[n][part * held : (part + 1) * held, :]
    ones = jnp.ones((8, 2 * rank), jnp.float32)
    for n in range(examples):
        row = lax.dot_general(
            ones,
            sums_ref[n].reshape(chips * 2 * held, 2 * rank),
            LANES_BY_LANES,
            precision=lax.Precision.HIGHEST,
            preferred_element_type=jnp.float32,
        )
        out_ref[n : n + 1, :] = row[0:1, :]


def score(parts, queries, distances, rank):
    tokens = parts[0].shape[1]
    examples = tokens // SEQ
    chips = sum(len(chip_distances) for _, chip_distances in distances) // 2
    held = queries[0].shape[1]
    return pl.pallas_call(
        functools.partial(score_kernel, len(parts), distances),
        out_shape=jax.ShapeDtypeStruct((examples, 2 * chips * held), jnp.float32),
        scratch_shapes=[
            pltpu.VMEM((rank, tokens), jnp.float32),
            pltpu.VMEM((examples, rank // 2, 2 * rank), jnp.float32),
            pltpu.VMEM((examples, chips, 2, held, 2 * rank), jnp.float32),
        ],
        compiler_params=PARAMS,
    )(*parts, *queries)


def shards(inputs, out_grads, proj_in, proj_out, queries):
    devices = lax.axis_size("ex")
    chips = devices // 2
    middle = chips // 2
    rank = proj_in.shape[1]
    together = lax.optimization_barrier

    def swap(array, chip=0, core=0):
        distance = 2 * chip + core
        return lax.ppermute(array, "ex", [(i, i ^ distance) for i in range(devices)])

    query = queries[None]
    y_queries = [query, swap(query, chip=1)]
    z_queries = [swap(query, chip=chip) for chip in [middle] + list(range(2, middle, 2))]
    given, kept = project(inputs, out_grads, proj_in.T, proj_out.T, devices)
    y_queries, z_queries, given, kept = together((y_queries, z_queries, given, kept))
    came = swap(given, core=1)
    here_queries = stack(z_queries)
    there_queries = swap(here_queries, chip=1)
    early = stack(y_queries + [here_queries])
    early_other = swap(early, core=1)
    came, early_other = together((came, early_other))

    types = [jnp.float32 if chip < middle else jnp.bfloat16 for chip in range(chips)]
    parts = list(add_halves(kept, came, types))
    parts[middle:] = [swap(parts[chip], chip=chip) for chip in range(middle, chips)]
    first = slice(1, middle + middle // 2)
    there_queries, parts[first] = together((there_queries, parts[first]))
    corner = stack([here_queries[:1], there_queries[:1]])
    late = [there_queries] + [swap(corner, chip=chip) for chip in range(2, middle, 2)]
    parts[1:middle] = [swap(parts[chip], chip=chip) for chip in range(1, middle)]
    late, parts[1 : middle - 1], parts[middle + middle // 2 :] = together((late, parts[1 : middle - 1], parts[middle + middle // 2 :]))
    late = stack(late)
    late_other = swap(late, core=1)
    z_chips = [middle] + list(range(2, middle, 2))
    early_chips = [0, 1] + z_chips
    late_chips = [chip + 1 for chip in z_chips] + [middle + chip + y for chip in z_chips[1:] for y in range(2)]
    held = [early, early_other, late, late_other]
    return score(parts, held, [(0, early_chips), (1, early_chips), (0, late_chips), (1, late_chips)], rank)


def solution(mesh):
    return jax.shard_map(
        shards,
        mesh=mesh,
        in_specs=(
            P("ex", "groups"),
            P("ex", "groups"),
            P("ex", None),
            P("ex", None),
            P("ex", None),
        ),
        out_specs=P(("groups", "ex"), None),
        check_vma=False,
    )
```

```python
import functools

import jax
import jax.numpy as jnp
from jax import lax
from jax.experimental import pallas as pl
from jax.experimental.pallas import tpu as pltpu
from jax.sharding import PartitionSpec as P

SEQ = 64
VMEM_BYTES = 32 * 1024 * 1024
LANES_BY_LANES = (((1,), (1,)), ((), ()))
HBM_SPEC = pl.BlockSpec(memory_space=pltpu.HBM)
VMEM_SPEC = pl.BlockSpec(memory_space=pltpu.VMEM)
PARAMS = pltpu.CompilerParams(vmem_limit_bytes=VMEM_BYTES)


def project_kernel(flip, x_hbm, w_hbm, p_in_hbm, p_out_hbm, *refs):
    here = lax.axis_index("ex")
    core, chip = lax.rem(here, 2), lax.div(here, 2)
    *given_refs, kept_ref, x_buf, w_buf, p_in, p_out, p_sems, sems = refs
    depth = kept_ref.shape[0]
    rank, width = kept_ref.shape[1] // 2, kept_ref.shape[2]
    copies = [
        pltpu.make_async_copy(p_in_hbm, p_in, p_sems.at[0]),
        pltpu.make_async_copy(p_out_hbm, p_out, p_sems.at[1]),
    ]
    for z in range(depth):
        place = lax.bitwise_xor(chip, 2 * z + flip)
        columns = pl.ds(pl.multiple_of(place * 2 * width, 2 * width), 2 * width)
        copies.append(pltpu.make_async_copy(x_hbm.at[:, columns], x_buf.at[z], sems.at[0, z]))
        copies.append(pltpu.make_async_copy(w_hbm.at[:, columns], w_buf.at[z], sems.at[1, z]))
    for copy in copies:
        copy.start()
    for copy in copies[:2]:
        copy.wait()
    for z in range(depth):
        for copy in copies[2 + 2 * z : 4 + 2 * z]:
            copy.wait()
        low_in = jnp.dot(p_in[...], x_buf[z], preferred_element_type=jnp.float32)
        low_out = jnp.dot(p_out[...], w_buf[z], preferred_element_type=jnp.float32)
        for rows, low in ((slice(0, rank), low_in), (slice(rank, 2 * rank), low_out)):
            left, right = low[:, :width], low[:, width:]
            given_ref = given_refs[z * len(given_refs) // depth]
            given_ref[z % given_ref.shape[0], rows, :] = jnp.where(core == 0, right, left)
            kept_ref[z, rows, :] = jnp.where(core == 0, left, right)


def project(flip, arrays, devices, splits):
    inputs, out_grads, proj_in_t, proj_out_t = arrays
    depth = devices // 4
    width = inputs.shape[1] // devices
    rank = proj_in_t.shape[0]
    kept = jax.ShapeDtypeStruct((depth, 2 * rank, width), jnp.float32)
    given = jax.ShapeDtypeStruct((depth // splits, 2 * rank, width), jnp.float32)
    *given, kept = pl.pallas_call(
        functools.partial(project_kernel, flip),
        out_shape=[given] * splits + [kept],
        in_specs=[HBM_SPEC] * 4,
        out_specs=[VMEM_SPEC] * (splits + 1),
        scratch_shapes=[
            pltpu.VMEM((depth, inputs.shape[0], 2 * width), jnp.bfloat16),
            pltpu.VMEM((depth, out_grads.shape[0], 2 * width), jnp.bfloat16),
            pltpu.VMEM(proj_in_t.shape, jnp.bfloat16),
            pltpu.VMEM(proj_out_t.shape, jnp.bfloat16),
            pltpu.SemaphoreType.DMA((2,)),
            pltpu.SemaphoreType.DMA((2, depth)),
        ],
        compiler_params=PARAMS,
        cost_estimate=pl.CostEstimate(
            flops=rank * (inputs.size + out_grads.size),
            bytes_accessed=inputs.size + out_grads.size,
            transcendentals=0,
        ),
    )(*arrays)
    return given, kept


def put_split(out_ref, low):
    rank = low.shape[0] // 2
    low_in = low[:rank, :]
    high = low_in.astype(jnp.bfloat16)
    out_ref[:rank, :] = high
    out_ref[rank : 2 * rank, :] = low[rank:, :].astype(jnp.bfloat16)
    out_ref[2 * rank :, :] = (low_in - high.astype(jnp.float32)).astype(jnp.bfloat16)


def get_split(ref):
    rank = ref.shape[0] // 3
    low_in = ref[:rank, :].astype(jnp.float32) + ref[2 * rank :, :].astype(jnp.float32)
    return jnp.concatenate([low_in, ref[rank : 2 * rank, :].astype(jnp.float32)], axis=0)


def add_given_kernel(kept_ref, came_ref, out_ref):
    for block in range(out_ref.shape[0]):
        put_split(out_ref.at[block], kept_ref[block] + came_ref[block])


def add_given(kept, came):
    blocks, rows, width = kept.shape
    return pl.pallas_call(
        add_given_kernel,
        out_shape=jax.ShapeDtypeStruct((blocks, rows // 2 * 3, width), jnp.bfloat16),
        compiler_params=PARAMS,
    )(kept, came)


def add_kept_kernel(kept_ref, across_ref, *refs):
    came_refs, out_refs = refs[:2], refs[2:]
    half = came_refs[0].shape[0]
    for block, out_ref in enumerate(out_refs):
        total = kept_ref[block] + came_refs[block // half][block % half] + get_split(across_ref.at[block])
        out_ref[...] = total.astype(out_ref.dtype)


def add_kept(kept, came, across):
    blocks, rows, width = kept.shape
    wide = jax.ShapeDtypeStruct((rows, width), jnp.float32)
    rounded = jax.ShapeDtypeStruct((rows, width), jnp.bfloat16)
    return pl.pallas_call(
        add_kept_kernel,
        out_shape=[wide if 2 * block < blocks else rounded for block in range(blocks)],
        compiler_params=PARAMS,
    )(kept, across, *came)


def stack_kernel(left_ref, right_ref, out_ref):
    out_ref[: left_ref.shape[0]] = left_ref[...]
    out_ref[left_ref.shape[0] :] = right_ref[...]


def stack(left, right):
    return pl.pallas_call(
        stack_kernel,
        out_shape=jax.ShapeDtypeStruct((2 * left.shape[0],) + left.shape[1:], left.dtype),
        compiler_params=PARAMS,
    )(left, right)


def add_scores(queries_ref, chips, place, grads, sums_ref):
    examples, half_rank, lanes = grads.shape
    held = queries_ref.shape[1]
    step = 4 if len(chips) % 4 == 0 else 2
    here = lax.div(lax.axis_index("ex"), 2)
    for first in range(0, len(chips), step):
        sums = [jnp.zeros((step * held, lanes), jnp.float32) for _ in range(examples)]
        for k in range(half_rank):
            query = queries_ref[first : first + step, :, k * lanes : (k + 1) * lanes].astype(jnp.float32)
            query = query.reshape(step * held, lanes)
            for n in range(examples):
                sums[n] = sums[n] + query * grads[n, k : k + 1, :]
        for part in range(step):
            source = lax.bitwise_xor(here, chips[first + part])
            for n in range(examples):
                sums_ref[n, source, place] = sums[n][part * held : (part + 1) * held, :]


def first_score_kernel(parts_count, held, *refs):
    part_refs, query_refs = refs[:parts_count], refs[parts_count : parts_count + len(held)]
    grads_ref, sums_ref, out_t_ref = refs[parts_count + len(held) :]
    rank, tokens = out_t_ref.shape
    core = lax.rem(lax.axis_index("ex"), 2)
    total = part_refs[0][...]
    for part_ref in part_refs[1:]:
        total = total + part_ref[...].astype(jnp.float32)
    out_t_ref[...] = total[rank:, :]
    even = out_t_ref[pl.ds(0, rank // 2, stride=2), :]
    odd = out_t_ref[pl.ds(1, rank // 2, stride=2), :]
    token = lax.broadcasted_iota(jnp.int32, (rank, tokens), 1)
    for n in range(tokens // SEQ):
        mine = jnp.where((token >= n * SEQ) & (token < (n + 1) * SEQ), total[:rank, :], 0.0)
        for side, rows in enumerate((even, odd)):
            grads_ref[n, :, side * rank : (side + 1) * rank] = lax.dot_general(
                rows, mine, LANES_BY_LANES, precision=lax.Precision.HIGHEST, preferred_element_type=jnp.float32
            )
    sums_ref[...] = jnp.zeros_like(sums_ref)
    for queries_ref, (other, chips) in zip(query_refs, held):
        add_scores(queries_ref, chips, lax.rem(core + other, 2), grads_ref, sums_ref)


def last_score_kernel(chips, grads_ref, before_ref, queries_ref, out_ref, sums_ref):
    core = lax.rem(lax.axis_index("ex"), 2)
    sums_ref[...] = before_ref[...]
    add_scores(queries_ref, chips, lax.rem(core + 1, 2), grads_ref, sums_ref)
    examples, *rows, lanes = sums_ref.shape
    ones = jnp.ones((8, lanes), jnp.float32)
    for n in range(examples):
        row = lax.dot_general(
            ones,
            sums_ref[n].reshape(out_ref.shape[1], lanes),
            LANES_BY_LANES,
            precision=lax.Precision.HIGHEST,
            preferred_element_type=jnp.float32,
        )
        out_ref[n : n + 1, :] = row[0:1, :]


def first_scores(parts, queries, held, rank):
    tokens = parts[0].shape[1]
    examples = tokens // SEQ
    chips = 2 * queries[0].shape[0]
    return pl.pallas_call(
        functools.partial(first_score_kernel, len(parts), held),
        out_shape=[
            jax.ShapeDtypeStruct((examples, rank // 2, 2 * rank), jnp.float32),
            jax.ShapeDtypeStruct((examples, chips, 2, queries[0].shape[1], 2 * rank), jnp.float32),
        ],
        scratch_shapes=[pltpu.VMEM((rank, tokens), jnp.float32)],
        compiler_params=PARAMS,
    )(*parts, *queries)


def last_scores(grads, sums, queries, chips):
    examples, all_chips, cores, held, _ = sums.shape
    return pl.pallas_call(
        functools.partial(last_score_kernel, chips),
        out_shape=jax.ShapeDtypeStruct((examples, all_chips * cores * held), jnp.float32),
        scratch_shapes=[pltpu.VMEM(sums.shape, jnp.float32)],
        compiler_params=PARAMS,
    )(grads, sums, queries)


def shards(inputs, out_grads, proj_in, proj_out, queries):
    devices = lax.axis_size("ex")
    chips = devices // 2
    depth = chips // 2
    rank = proj_in.shape[1]
    together = lax.optimization_barrier

    def swap(array, chip=0, core=0):
        distance = 2 * chip + core
        return lax.ppermute(array, "ex", [(i, i ^ distance) for i in range(devices)])

    steps = [1 << bit for bit in reversed(range(chips.bit_length() - 1))]
    held, reach = queries[None], [0]
    came_held = swap(held, chip=steps[0])
    arrays = [pltpu.with_memory_space_constraint(a, pltpu.HBM) for a in (inputs, out_grads, proj_in.T, proj_out.T)]
    given, kept = project(1, arrays, devices, 1)
    came_held, given, kept = together((came_held, given, kept))
    came = swap(given[0], core=1)
    for last, step in zip(steps, steps[1:-1]):
        held, reach = stack(held, came_held), reach + [chip ^ last for chip in reach]
        came_held = swap(held, chip=step)
    message = add_given(kept, came)
    message, arrays = together((message, arrays))
    across = swap(message, chip=1)
    given, kept = project(0, arrays, devices, 2)
    came_held, given, kept = together((came_held, given, kept))
    came = [swap(array, core=1) for array in given]
    held, reach = stack(held, came_held), reach + [chip ^ steps[-2] for chip in reach]
    came_held = swap(held, chip=1)
    other_held = swap(held, core=1)
    across, came = together((across, came))

    sums = add_kept(kept, came, across)
    parts = list(sums)
    for z in list(range(depth // 2, depth)) + list(range(1, depth // 2)):
        parts[z] = swap(parts[z], chip=2 * z)
    came_held, other_held, parts = together((came_held, other_held, parts))
    other_came = swap(came_held, core=1)
    reach_y = [chip ^ 1 for chip in reach]
    grads, scores = first_scores(parts, [held, other_held, came_held], [(0, reach), (1, reach), (0, reach_y)], rank)
    return last_scores(grads, scores, other_came, reach_y)


def solution(mesh):
    return jax.shard_map(
        shards,
        mesh=mesh,
        in_specs=(
            P("ex", "groups"),
            P("ex", "groups"),
            P("ex", None),
            P("ex", None),
            P("ex", None),
        ),
        out_specs=P(("groups", "ex"), None),
        check_vma=False,
    )
```

```python
import functools

import jax
import jax.numpy as jnp
from jax import lax
from jax.experimental import pallas as pl
from jax.experimental.pallas import tpu as pltpu
from jax.sharding import PartitionSpec as P

SEQ = 64
VMEM_BYTES = 32 * 1024 * 1024
AHEAD = 3
LANES_BY_LANES = (((1,), (1,)), ((), ()))
HBM_SPEC = pl.BlockSpec(memory_space=pltpu.HBM)
VMEM_SPEC = pl.BlockSpec(memory_space=pltpu.VMEM)
PARAMS = pltpu.CompilerParams(vmem_limit_bytes=VMEM_BYTES)


def project_kernel(x_hbm, w_hbm, p_in_hbm, p_out_hbm, *refs):
    given_y, given_here, kept_y, kept_here, x_buf, w_buf, p_in, p_out, low, p_sems, x_sems, w_sems = refs
    here = lax.axis_index("ex")
    core, chip = lax.rem(here, 2), lax.div(here, 2)
    depth = kept_y.shape[0]
    rank, width = kept_y.shape[1] // 2, kept_y.shape[2]
    matrices = [
        pltpu.make_async_copy(p_in_hbm, p_in, p_sems.at[0]),
        pltpu.make_async_copy(p_out_hbm, p_out, p_sems.at[1]),
    ]
    chunks = []
    for top, hbm, buf, sems, matrix in ((0, x_hbm, x_buf, x_sems, p_in), (rank, w_hbm, w_buf, w_sems, p_out)):
        rows = buf.shape[0] // sems.shape[0]
        for chunk in range(sems.shape[0]):
            part = pl.ds(chunk * rows, rows)
            copy = pltpu.make_async_copy(hbm.at[part, :], buf.at[part, :], sems.at[chunk])
            chunks.append((slice(top, top + rank), part, buf, matrix, copy, chunk == 0))
    for copy in matrices + [chunk[4] for chunk in chunks[:AHEAD]]:
        copy.start()
    for copy in matrices:
        copy.wait()
    step = min(1024, low.shape[1])
    for index, (lines, part, buf, matrix, copy, first) in enumerate(chunks):
        copy.wait()
        if index + AHEAD < len(chunks):
            chunks[index + AHEAD][4].start()
        for column in range(0, low.shape[1], step):
            columns = slice(column, column + step)
            product = jnp.dot(matrix[:, part], buf[part, columns], preferred_element_type=jnp.float32)
            low[lines, columns] = product if first else low[lines, columns] + product
    for flip, given_ref, kept_ref in ((1, given_y, kept_y), (0, given_here, kept_here)):
        for z in range(depth):
            place = lax.bitwise_xor(chip, 2 * z + flip)
            both = low[:, pl.ds(pl.multiple_of(place * 2 * width, 2 * width), 2 * width)]
            left, right = both[:, :width], both[:, width:]
            given_ref[z] = jnp.where(core == 0, right, left)
            kept_ref[z] = jnp.where(core == 0, left, right)


def project(inputs, out_grads, proj_in_t, proj_out_t, devices):
    arrays = [pltpu.with_memory_space_constraint(a, pltpu.HBM) for a in (inputs, out_grads, proj_in_t, proj_out_t)]
    width = inputs.shape[1] // devices
    rank = proj_in_t.shape[0]
    low = jax.ShapeDtypeStruct((devices // 4, 2 * rank, width), jnp.float32)
    chunks = [a.shape[0] // 256 if a.shape[0] % 256 == 0 else 1 for a in (inputs, out_grads)]
    return pl.pallas_call(
        project_kernel,
        out_shape=[low] * 4,
        in_specs=[HBM_SPEC] * 4,
        out_specs=[VMEM_SPEC] * 4,
        scratch_shapes=[pltpu.VMEM(a.shape, jnp.bfloat16) for a in arrays]
        + [pltpu.VMEM((2 * rank, inputs.shape[1]), jnp.float32), pltpu.SemaphoreType.DMA((2,))]
        + [pltpu.SemaphoreType.DMA((count,)) for count in chunks],
        compiler_params=PARAMS,
        cost_estimate=pl.CostEstimate(
            flops=2 * rank * (inputs.size + out_grads.size),
            bytes_accessed=2 * (inputs.size + out_grads.size),
            transcendentals=0,
        ),
    )(*arrays)


def put_split(out_ref, low):
    rank = low.shape[0] // 2
    low_in = low[:rank, :]
    high = low_in.astype(jnp.bfloat16)
    out_ref[:rank, :] = high
    out_ref[rank : 2 * rank, :] = low[rank:, :].astype(jnp.bfloat16)
    out_ref[2 * rank :, :] = (low_in - high.astype(jnp.float32)).astype(jnp.bfloat16)


def get_split(ref):
    rank = ref.shape[0] // 3
    low_in = ref[:rank, :].astype(jnp.float32) + ref[2 * rank :, :].astype(jnp.float32)
    return jnp.concatenate([low_in, ref[rank : 2 * rank, :].astype(jnp.float32)], axis=0)


def add_given_kernel(kept_ref, came_ref, out_ref):
    for block in range(out_ref.shape[0]):
        put_split(out_ref.at[block], kept_ref[block] + came_ref[block])


def add_given(kept, came):
    blocks, rows, width = kept.shape
    return pl.pallas_call(
        add_given_kernel,
        out_shape=jax.ShapeDtypeStruct((blocks, rows // 2 * 3, width), jnp.bfloat16),
        compiler_params=PARAMS,
    )(kept, came)


def add_kept_kernel(kept_ref, came_ref, across_ref, *out_refs):
    for block, out_ref in enumerate(out_refs):
        total = kept_ref[block] + came_ref[block] + get_split(across_ref.at[block])
        out_ref[...] = total.astype(out_ref.dtype)


def add_kept(kept, came, across):
    blocks, rows, width = kept.shape
    wide = jax.ShapeDtypeStruct((rows, width), jnp.float32)
    rounded = jax.ShapeDtypeStruct((rows, width), jnp.bfloat16)
    return pl.pallas_call(
        add_kept_kernel,
        out_shape=[wide if 2 * block < blocks else rounded for block in range(blocks)],
        compiler_params=PARAMS,
    )(kept, came, across)


def stack_kernel(left_ref, right_ref, out_ref):
    out_ref[: left_ref.shape[0]] = left_ref[...]
    out_ref[left_ref.shape[0] :] = right_ref[...]


def stack(left, right):
    return pl.pallas_call(
        stack_kernel,
        out_shape=jax.ShapeDtypeStruct((2 * left.shape[0],) + left.shape[1:], left.dtype),
        compiler_params=PARAMS,
    )(left, right)


def add_scores(queries_ref, chips, place, grads, sums_ref):
    examples, half_rank, lanes = grads.shape
    held = queries_ref.shape[1]
    step = 4 if len(chips) % 4 == 0 else 2
    here = lax.div(lax.axis_index("ex"), 2)
    for first in range(0, len(chips), step):
        sums = [jnp.zeros((step * held, lanes), jnp.float32) for _ in range(examples)]
        for k in range(half_rank):
            query = queries_ref[first : first + step, :, k * lanes : (k + 1) * lanes].astype(jnp.float32)
            query = query.reshape(step * held, lanes)
            for n in range(examples):
                sums[n] = sums[n] + query * grads[n, k : k + 1, :]
        for part in range(step):
            source = lax.bitwise_xor(here, chips[first + part])
            for n in range(examples):
                sums_ref[n, source, place] = sums[n][part * held : (part + 1) * held, :]


def first_score_kernel(parts_count, held, *refs):
    part_refs, query_refs = refs[:parts_count], refs[parts_count : parts_count + len(held)]
    grads_ref, sums_ref, out_t_ref = refs[parts_count + len(held) :]
    rank, tokens = out_t_ref.shape
    core = lax.rem(lax.axis_index("ex"), 2)
    total = part_refs[0][...]
    for part_ref in part_refs[1:]:
        total = total + part_ref[...].astype(jnp.float32)
    out_t_ref[...] = total[rank:, :]
    even = out_t_ref[pl.ds(0, rank // 2, stride=2), :]
    odd = out_t_ref[pl.ds(1, rank // 2, stride=2), :]
    token = lax.broadcasted_iota(jnp.int32, (rank, tokens), 1)
    for n in range(tokens // SEQ):
        mine = jnp.where((token >= n * SEQ) & (token < (n + 1) * SEQ), total[:rank, :], 0.0)
        for side, rows in enumerate((even, odd)):
            grads_ref[n, :, side * rank : (side + 1) * rank] = lax.dot_general(
                rows, mine, LANES_BY_LANES, precision=lax.Precision.HIGHEST, preferred_element_type=jnp.float32
            )
    sums_ref[...] = jnp.zeros_like(sums_ref)
    for queries_ref, (other, chips) in zip(query_refs, held):
        add_scores(queries_ref, chips, lax.rem(core + other, 2), grads_ref, sums_ref)


def last_score_kernel(chips, grads_ref, before_ref, queries_ref, out_ref, sums_ref):
    core = lax.rem(lax.axis_index("ex"), 2)
    sums_ref[...] = before_ref[...]
    add_scores(queries_ref, chips, lax.rem(core + 1, 2), grads_ref, sums_ref)
    examples, *rows, lanes = sums_ref.shape
    ones = jnp.ones((8, lanes), jnp.float32)
    for n in range(examples):
        row = lax.dot_general(
            ones,
            sums_ref[n].reshape(out_ref.shape[1], lanes),
            LANES_BY_LANES,
            precision=lax.Precision.HIGHEST,
            preferred_element_type=jnp.float32,
        )
        out_ref[n : n + 1, :] = row[0:1, :]


def first_scores(parts, queries, held, rank):
    tokens = parts[0].shape[1]
    examples = tokens // SEQ
    chips = 2 * queries[0].shape[0]
    return pl.pallas_call(
        functools.partial(first_score_kernel, len(parts), held),
        out_shape=[
            jax.ShapeDtypeStruct((examples, rank // 2, 2 * rank), jnp.float32),
            jax.ShapeDtypeStruct((examples, chips, 2, queries[0].shape[1], 2 * rank), jnp.float32),
        ],
        scratch_shapes=[pltpu.VMEM((rank, tokens), jnp.float32)],
        compiler_params=PARAMS,
    )(*parts, *queries)


def last_scores(grads, sums, queries, chips):
    examples, all_chips, cores, held, _ = sums.shape
    return pl.pallas_call(
        functools.partial(last_score_kernel, chips),
        out_shape=jax.ShapeDtypeStruct((examples, all_chips * cores * held), jnp.float32),
        scratch_shapes=[pltpu.VMEM(sums.shape, jnp.float32)],
        compiler_params=PARAMS,
    )(grads, sums, queries)


def shards(inputs, out_grads, proj_in, proj_out, queries):
    devices = lax.axis_size("ex")
    chips = devices // 2
    depth = chips // 2
    rank = proj_in.shape[1]
    together = lax.optimization_barrier

    def swap(array, chip=0, core=0):
        distance = 2 * chip + core
        return lax.ppermute(array, "ex", [(i, i ^ distance) for i in range(devices)])

    steps = [1 << bit for bit in reversed(range(chips.bit_length() - 1))]
    held, reach = queries[None], [0]
    came_held = swap(held, chip=steps[0])
    lows = project(inputs, out_grads, proj_in.T, proj_out.T, devices)
    came_held, lows = together((came_held, lows))
    given_y, given, kept_y, kept = lows
    came_y = swap(given_y, core=1)
    came = swap(given, core=1)
    for last, step in zip(steps, steps[1:-1]):
        held, reach = stack(held, came_held), reach + [chip ^ last for chip in reach]
        came_held = swap(held, chip=step)
    across = swap(add_given(kept_y, came_y), chip=1)
    held, reach = stack(held, came_held), reach + [chip ^ steps[-2] for chip in reach]
    came_held = swap(held, chip=1)
    other_held = swap(held, core=1)
    across, came = together((across, came))

    sums = add_kept(kept, came, across)
    parts = list(sums)
    for z in list(range(depth // 2, depth)) + list(range(1, depth // 2)):
        parts[z] = swap(parts[z], chip=2 * z)
    came_held, other_held, parts = together((came_held, other_held, parts))
    other_came = swap(came_held, core=1)
    reach_y = [chip ^ 1 for chip in reach]
    grads, scores = first_scores(parts, [held, other_held, came_held], [(0, reach), (1, reach), (0, reach_y)], rank)
    return last_scores(grads, scores, other_came, reach_y)


def solution(mesh):
    return jax.shard_map(
        shards,
        mesh=mesh,
        in_specs=(
            P("ex", "groups"),
            P("ex", "groups"),
            P("ex", None),
            P("ex", None),
            P("ex", None),
        ),
        out_specs=P(("groups", "ex"), None),
        check_vma=False,
    )
```

```python
import functools

import jax
import jax.numpy as jnp
from jax import lax
from jax.experimental import pallas as pl
from jax.experimental.pallas import tpu as pltpu
from jax.sharding import PartitionSpec as P

SEQ = 64
VMEM_BYTES = 32 * 1024 * 1024
AHEAD = 3
CODE_SCALE = 2.0**-8
LANES_BY_LANES = (((1,), (1,)), ((), ()))
HBM_SPEC = pl.BlockSpec(memory_space=pltpu.HBM)
VMEM_SPEC = pl.BlockSpec(memory_space=pltpu.VMEM)
PARAMS = pltpu.CompilerParams(vmem_limit_bytes=VMEM_BYTES)


def project_kernel(x_hbm, w_hbm, p_in_hbm, p_out_hbm, *refs):
    given_y, given_here, kept_y, kept_here, x_buf, w_buf, p_in, p_out, low, p_sems, x_sems, w_sems = refs
    here = lax.axis_index("ex")
    core, chip = lax.rem(here, 2), lax.div(here, 2)
    depth = kept_y.shape[0]
    rank, width = kept_y.shape[1] // 2, kept_y.shape[2]
    matrices = [
        pltpu.make_async_copy(p_in_hbm, p_in, p_sems.at[0]),
        pltpu.make_async_copy(p_out_hbm, p_out, p_sems.at[1]),
    ]
    chunks = []
    for top, hbm, buf, sems, matrix in ((0, x_hbm, x_buf, x_sems, p_in), (rank, w_hbm, w_buf, w_sems, p_out)):
        rows = buf.shape[0] // sems.shape[0]
        pieces = sems.shape[1]
        for chunk in range(sems.shape[0]):
            copies = []
            for piece in range(pieces):
                part = pl.ds(chunk * rows + piece * (rows // pieces), rows // pieces)
                copies.append(pltpu.make_async_copy(hbm.at[part, :], buf.at[part, :], sems.at[chunk, piece]))
            part = pl.ds(chunk * rows, rows)
            chunks.append((slice(top, top + rank), part, buf, matrix, copies, chunk == 0))
    for copy in matrices + [copy for chunk in chunks[:AHEAD] for copy in chunk[4]]:
        copy.start()
    for copy in matrices:
        copy.wait()
    step = min(1024, low.shape[1])
    for index, (lines, part, buf, matrix, copies, first) in enumerate(chunks):
        for copy in copies:
            copy.wait()
        if index + AHEAD < len(chunks):
            for copy in chunks[index + AHEAD][4]:
                copy.start()
        for column in range(0, low.shape[1], step):
            columns = slice(column, column + step)
            product = jnp.dot(matrix[:, part], buf[part, columns], preferred_element_type=jnp.float32)
            low[lines, columns] = product if first else low[lines, columns] + product
    for flip, given_ref, kept_ref in ((1, given_y, kept_y), (0, given_here, kept_here)):
        for z in range(depth):
            place = lax.bitwise_xor(chip, 2 * z + flip)
            both = low[:, pl.ds(pl.multiple_of(place * 2 * width, 2 * width), 2 * width)]
            left, right = both[:, :width], both[:, width:]
            given_ref[z] = jnp.where(core == 0, right, left)
            kept_ref[z] = jnp.where(core == 0, left, right)


def project(inputs, out_grads, proj_in_t, proj_out_t, devices):
    arrays = [pltpu.with_memory_space_constraint(a, pltpu.HBM) for a in (inputs, out_grads, proj_in_t, proj_out_t)]
    width = inputs.shape[1] // devices
    rank = proj_in_t.shape[0]
    low = jax.ShapeDtypeStruct((devices // 4, 2 * rank, width), jnp.float32)
    chunks = [(a.shape[0] // 256, 4) if a.shape[0] % 256 == 0 else (1, 1) for a in (inputs, out_grads)]
    return pl.pallas_call(
        project_kernel,
        out_shape=[low] * 4,
        in_specs=[HBM_SPEC] * 4,
        out_specs=[VMEM_SPEC] * 4,
        scratch_shapes=[pltpu.VMEM(a.shape, jnp.bfloat16) for a in arrays]
        + [pltpu.VMEM((2 * rank, inputs.shape[1]), jnp.float32), pltpu.SemaphoreType.DMA((2,))]
        + [pltpu.SemaphoreType.DMA(count) for count in chunks],
        compiler_params=PARAMS,
        cost_estimate=pl.CostEstimate(
            flops=2 * rank * (inputs.size + out_grads.size),
            bytes_accessed=2 * (inputs.size + out_grads.size),
            transcendentals=0,
        ),
    )(*arrays)


def put_coded(out_ref, low):
    rows = low.shape[0]
    rounded = low.astype(jnp.bfloat16)
    out_ref[:rows, :] = rounded
    rounded = rounded.astype(jnp.float32)
    left = (low - rounded) / jnp.maximum(jnp.abs(rounded) * CODE_SCALE, 1e-30)
    level = jnp.clip(jnp.floor(2.0 * left) + 2.0, 0.0, 3.0)
    part = rows // 4
    word = level[:part, :]
    for index in range(1, 4):
        word = word + 4.0**index * level[index * part : (index + 1) * part, :]
    out_ref[rows:, :] = word.astype(jnp.bfloat16)


def get_coded(ref):
    part = ref.shape[0] // 5
    word = ref[4 * part :, :].astype(jnp.float32).astype(jnp.int32)
    level = jnp.concatenate([jnp.bitwise_and(jnp.right_shift(word, 2 * index), 3) for index in range(4)], axis=0)
    rounded = ref[: 4 * part, :].astype(jnp.float32)
    return rounded + jnp.abs(rounded) * (CODE_SCALE * 0.5) * (level.astype(jnp.float32) - 1.5)


def add_given_kernel(kept_ref, came_ref, out_ref):
    for block in range(out_ref.shape[0]):
        put_coded(out_ref.at[block], kept_ref[block] + came_ref[block])


def add_given(kept, came):
    blocks, rows, width = kept.shape
    return pl.pallas_call(
        add_given_kernel,
        out_shape=jax.ShapeDtypeStruct((blocks, rows // 4 * 5, width), jnp.bfloat16),
        compiler_params=PARAMS,
    )(kept, came)


def add_kept_kernel(kept_ref, came_ref, across_ref, own_ref, out_ref):
    here = lax.div(lax.axis_index("ex"), 4)
    for z in range(out_ref.shape[0]):
        total = kept_ref[z] + came_ref[z] + get_coded(across_ref.at[z])
        if z == 0:
            own_ref[...] = total
        out_ref[lax.bitwise_xor(here, z)] = total.astype(out_ref.dtype)


def add_kept(kept, came, across):
    return pl.pallas_call(
        add_kept_kernel,
        out_shape=[
            jax.ShapeDtypeStruct(kept.shape[1:], jnp.float32),
            jax.ShapeDtypeStruct(kept.shape, jnp.bfloat16),
        ],
        compiler_params=PARAMS,
    )(kept, came, across)


def stack_kernel(left_ref, right_ref, out_ref):
    out_ref[: left_ref.shape[0]] = left_ref[...]
    out_ref[left_ref.shape[0] :] = right_ref[...]


def stack(left, right):
    return pl.pallas_call(
        stack_kernel,
        out_shape=jax.ShapeDtypeStruct((2 * left.shape[0],) + left.shape[1:], left.dtype),
        compiler_params=PARAMS,
    )(left, right)


def add_scores(queries_ref, chips, place, grads, sums_ref):
    examples, half_rank, lanes = grads.shape
    held = queries_ref.shape[1]
    step = 4 if len(chips) % 4 == 0 else 2
    here = lax.div(lax.axis_index("ex"), 2)
    for first in range(0, len(chips), step):
        sums = [jnp.zeros((step * held, lanes), jnp.float32) for _ in range(examples)]
        for k in range(half_rank):
            query = queries_ref[first : first + step, :, k * lanes : (k + 1) * lanes].astype(jnp.float32)
            query = query.reshape(step * held, lanes)
            for n in range(examples):
                sums[n] = sums[n] + query * grads[n, k : k + 1, :]
        for part in range(step):
            source = lax.bitwise_xor(here, chips[first + part])
            for n in range(examples):
                sums_ref[n, source, place] = sums[n][part * held : (part + 1) * held, :]


def first_score_kernel(held, own_ref, parts_ref, *refs):
    query_refs, (grads_ref, sums_ref, out_t_ref) = refs[: len(held)], refs[len(held) :]
    rank, tokens = out_t_ref.shape
    core = lax.rem(lax.axis_index("ex"), 2)
    total = own_ref[...] - own_ref[...].astype(jnp.bfloat16).astype(jnp.float32)
    for z in range(parts_ref.shape[0]):
        total = total + parts_ref[z].astype(jnp.float32)
    out_t_ref[...] = total[rank:, :]
    even = out_t_ref[pl.ds(0, rank // 2, stride=2), :]
    odd = out_t_ref[pl.ds(1, rank // 2, stride=2), :]
    token = lax.broadcasted_iota(jnp.int32, (rank, tokens), 1)
    for n in range(tokens // SEQ):
        mine = jnp.where((token >= n * SEQ) & (token < (n + 1) * SEQ), total[:rank, :], 0.0)
        for side, rows in enumerate((even, odd)):
            grads_ref[n, :, side * rank : (side + 1) * rank] = lax.dot_general(
                rows, mine, LANES_BY_LANES, precision=lax.Precision.HIGHEST, preferred_element_type=jnp.float32
            )
    sums_ref[...] = jnp.zeros_like(sums_ref)
    for queries_ref, (other, chips) in zip(query_refs, held):
        add_scores(queries_ref, chips, lax.rem(core + other, 2), grads_ref, sums_ref)


def last_score_kernel(chips, grads_ref, before_ref, queries_ref, others_ref, out_ref, sums_ref):
    core = lax.rem(lax.axis_index("ex"), 2)
    sums_ref[...] = before_ref[...]
    add_scores(queries_ref, chips, core, grads_ref, sums_ref)
    add_scores(others_ref, chips, lax.rem(core + 1, 2), grads_ref, sums_ref)
    examples, *rows, lanes = sums_ref.shape
    ones = jnp.ones((8, lanes), jnp.float32)
    for n in range(examples):
        row = lax.dot_general(
            ones,
            sums_ref[n].reshape(out_ref.shape[1], lanes),
            LANES_BY_LANES,
            precision=lax.Precision.HIGHEST,
            preferred_element_type=jnp.float32,
        )
        out_ref[n : n + 1, :] = row[0:1, :]


def first_scores(own, parts, queries, held, rank):
    tokens = own.shape[1]
    examples = tokens // SEQ
    chips = 2 * queries[0].shape[0]
    return pl.pallas_call(
        functools.partial(first_score_kernel, held),
        out_shape=[
            jax.ShapeDtypeStruct((examples, rank // 2, 2 * rank), jnp.float32),
            jax.ShapeDtypeStruct((examples, chips, 2, queries[0].shape[1], 2 * rank), jnp.float32),
        ],
        scratch_shapes=[pltpu.VMEM((rank, tokens), jnp.float32)],
        compiler_params=PARAMS,
    )(own, parts, *queries)


def last_scores(grads, sums, queries, others, chips):
    examples, all_chips, cores, held, _ = sums.shape
    return pl.pallas_call(
        functools.partial(last_score_kernel, chips),
        out_shape=jax.ShapeDtypeStruct((examples, all_chips * cores * held), jnp.float32),
        scratch_shapes=[pltpu.VMEM(sums.shape, jnp.float32)],
        compiler_params=PARAMS,
    )(grads, sums, queries, others)


def shards(inputs, out_grads, proj_in, proj_out, queries):
    devices = lax.axis_size("ex")
    chips = devices // 2
    depth = chips // 2
    rank = proj_in.shape[1]
    together = lax.optimization_barrier

    def swap(array, chip=0, core=0):
        distance = 2 * chip + core
        return lax.ppermute(array, "ex", [(i, i ^ distance) for i in range(devices)])

    steps = [1 << bit for bit in reversed(range(chips.bit_length() - 1))]
    held, reach = queries[None], [0]
    came_held = swap(held, chip=steps[0])
    lows = project(inputs, out_grads, proj_in.T, proj_out.T, devices)
    came_held, lows = together((came_held, lows))
    given_y, given, kept_y, kept = lows
    came_y = swap(given_y, core=1)
    came = swap(given, core=1)
    for last, step in zip(steps, steps[1:-1]):
        held, reach = stack(held, came_held), reach + [chip ^ last for chip in reach]
        came_held = swap(held, chip=step)
    across = swap(add_given(kept_y, came_y), chip=1)
    held, reach = stack(held, came_held), reach + [chip ^ steps[-2] for chip in reach]
    came_held = swap(held, chip=1)
    other_held = swap(held, core=1)
    across, came = together((across, came))

    own, sums = add_kept(kept, came, across)
    z_lines = [list(range(first, devices, 4)) for first in range(4)]
    parts = lax.all_to_all(sums, "ex", split_axis=0, concat_axis=0, tiled=True, axis_index_groups=z_lines)
    came_held, other_held, parts = together((came_held, other_held, parts))
    other_came = swap(came_held, core=1)
    grads, scores = first_scores(own, parts, [held, other_held], [(0, reach), (1, reach)], rank)
    return last_scores(grads, scores, came_held, other_came, [chip ^ 1 for chip in reach])


def solution(mesh):
    return jax.shard_map(
        shards,
        mesh=mesh,
        in_specs=(
            P("ex", "groups"),
            P("ex", "groups"),
            P("ex", None),
            P("ex", None),
            P("ex", None),
        ),
        out_specs=P(("groups", "ex"), None),
        check_vma=False,
    )
```

```python
import functools

import jax
import jax.numpy as jnp
from jax import lax
from jax.experimental import pallas as pl
from jax.experimental.pallas import tpu as pltpu
from jax.sharding import PartitionSpec as P

SEQ = 64
VMEM_BYTES = 32 * 1024 * 1024
AHEAD = 7
CODE_SCALE = 2.0**-8
LANES_BY_LANES = (((1,), (1,)), ((), ()))
HBM_SPEC = pl.BlockSpec(memory_space=pltpu.HBM)
VMEM_SPEC = pl.BlockSpec(memory_space=pltpu.VMEM)
PARAMS = pltpu.CompilerParams(vmem_limit_bytes=VMEM_BYTES)


def project_kernel(x_hbm, w_hbm, p_in_hbm, p_out_hbm, *refs):
    given_y, given_here, kept_y, kept_here, x_buf, w_buf, p_in, p_out, low, p_sems, x_sems, w_sems = refs
    here = lax.axis_index("ex")
    core, chip = lax.rem(here, 2), lax.div(here, 2)
    depth = kept_y.shape[0]
    rank, width = kept_y.shape[1] // 2, kept_y.shape[2]
    matrices = [
        pltpu.make_async_copy(p_in_hbm, p_in, p_sems.at[0]),
        pltpu.make_async_copy(p_out_hbm, p_out, p_sems.at[1]),
    ]
    chunks = []
    for top, hbm, buf, sems, matrix in ((0, x_hbm, x_buf, x_sems, p_in), (rank, w_hbm, w_buf, w_sems, p_out)):
        rows = buf.shape[0] // sems.shape[0]
        for chunk in range(sems.shape[0]):
            part = pl.ds(chunk * rows, rows)
            copy = pltpu.make_async_copy(hbm.at[part, :], buf.at[part, :], sems.at[chunk])
            chunks.append((slice(top, top + rank), part, buf, matrix, copy, chunk == 0))
    for copy in matrices + [chunk[4] for chunk in chunks[:AHEAD]]:
        copy.start()
    for copy in matrices:
        copy.wait()
    step = min(1024, low.shape[1])
    for index, (lines, part, buf, matrix, copy, first) in enumerate(chunks):
        copy.wait()
        if index + AHEAD < len(chunks):
            chunks[index + AHEAD][4].start()
        for column in range(0, low.shape[1], step):
            columns = slice(column, column + step)
            product = jnp.dot(matrix[:, part], buf[part, columns], preferred_element_type=jnp.float32)
            low[lines, columns] = product if first else low[lines, columns] + product
    for flip, given_ref, kept_ref in ((1, given_y, kept_y), (0, given_here, kept_here)):
        for z in range(depth):
            place = lax.bitwise_xor(chip, 2 * z + flip)
            both = low[:, pl.ds(pl.multiple_of(place * 2 * width, 2 * width), 2 * width)]
            left, right = both[:, :width], both[:, width:]
            given_ref[z] = jnp.where(core == 0, right, left)
            kept_ref[z] = jnp.where(core == 0, left, right)


def project(inputs, out_grads, proj_in_t, proj_out_t, devices):
    arrays = [pltpu.with_memory_space_constraint(a, pltpu.HBM) for a in (inputs, out_grads, proj_in_t, proj_out_t)]
    width = inputs.shape[1] // devices
    rank = proj_in_t.shape[0]
    low = jax.ShapeDtypeStruct((devices // 4, 2 * rank, width), jnp.float32)
    chunks = [a.shape[0] // rows if a.shape[0] % rows == 0 else 1 for a, rows in ((inputs, 128), (out_grads, 256))]
    return pl.pallas_call(
        project_kernel,
        out_shape=[low] * 4,
        in_specs=[HBM_SPEC] * 4,
        out_specs=[VMEM_SPEC] * 4,
        scratch_shapes=[pltpu.VMEM(a.shape, jnp.bfloat16) for a in arrays]
        + [pltpu.VMEM((2 * rank, inputs.shape[1]), jnp.float32), pltpu.SemaphoreType.DMA((2,))]
        + [pltpu.SemaphoreType.DMA((count,)) for count in chunks],
        compiler_params=PARAMS,
        cost_estimate=pl.CostEstimate(
            flops=2 * rank * (inputs.size + out_grads.size),
            bytes_accessed=2 * (inputs.size + out_grads.size),
            transcendentals=0,
        ),
    )(*arrays)


def put_coded(out_ref, low):
    rows = low.shape[0]
    rounded = low.astype(jnp.bfloat16)
    out_ref[:rows, :] = rounded
    rounded = rounded.astype(jnp.float32)
    left = (low - rounded) / jnp.maximum(jnp.abs(rounded) * CODE_SCALE, 1e-30)
    level = jnp.clip(jnp.floor(2.0 * left) + 2.0, 0.0, 3.0)
    part = rows // 4
    word = level[:part, :]
    for index in range(1, 4):
        word = word + 4.0**index * level[index * part : (index + 1) * part, :]
    out_ref[rows:, :] = word.astype(jnp.bfloat16)


def add_coded(total, ref):
    part = ref.shape[0] // 5
    word = ref[4 * part :, :].astype(jnp.float32)
    parts = []
    for index in reversed(range(4)):
        level = jnp.floor(word * 0.25**index)
        word = word - level * 4.0**index
        rounded = ref[index * part : (index + 1) * part, :].astype(jnp.float32)
        left = jnp.abs(rounded) * ((CODE_SCALE * 0.5) * level - CODE_SCALE * 0.75)
        parts.append((slice(index * part, (index + 1) * part), total(index * part, part) + rounded + left))
    return parts


def add_given_kernel(kept_ref, came_ref, out_ref):
    for block in range(out_ref.shape[0]):
        put_coded(out_ref.at[block], kept_ref[block] + came_ref[block])


def add_given(kept, came):
    blocks, rows, width = kept.shape
    return pl.pallas_call(
        add_given_kernel,
        out_shape=jax.ShapeDtypeStruct((blocks, rows // 4 * 5, width), jnp.bfloat16),
        compiler_params=PARAMS,
    )(kept, came)


def add_kept_kernel(kept_ref, came_ref, across_ref, *out_refs):
    for z, out_ref in enumerate(out_refs):
        def here(first, rows):
            return kept_ref[z, first : first + rows, :] + came_ref[z, first : first + rows, :]

        for rows, total in add_coded(here, across_ref.at[z]):
            out_ref[rows, :] = total.astype(out_ref.dtype)


def add_kept(kept, came, across, types):
    return pl.pallas_call(
        add_kept_kernel,
        out_shape=[jax.ShapeDtypeStruct(kept.shape[1:], dtype) for dtype in types],
        compiler_params=PARAMS,
    )(kept, came, across)


def stack_kernel(left_ref, right_ref, out_ref):
    out_ref[: left_ref.shape[0]] = left_ref[...]
    out_ref[left_ref.shape[0] :] = right_ref[...]


def stack(left, right):
    return pl.pallas_call(
        stack_kernel,
        out_shape=jax.ShapeDtypeStruct((2 * left.shape[0],) + left.shape[1:], left.dtype),
        compiler_params=PARAMS,
    )(left, right)


def add_scores(queries_ref, chips, place, grads, sums_ref):
    examples, half_rank, lanes = grads.shape
    held = queries_ref.shape[1]
    step = 4 if len(chips) % 4 == 0 else 2
    here = lax.div(lax.axis_index("ex"), 2)
    for first in range(0, len(chips), step):
        sums = [jnp.zeros((step * held, lanes), jnp.float32) for _ in range(examples)]
        for k in range(half_rank):
            query = queries_ref[first : first + step, :, k * lanes : (k + 1) * lanes].astype(jnp.float32)
            query = query.reshape(step * held, lanes)
            for n in range(examples):
                sums[n] = sums[n] + query * grads[n, k : k + 1, :]
        for part in range(step):
            source = lax.bitwise_xor(here, chips[first + part])
            for n in range(examples):
                sums_ref[n, source, place] = sums[n][part * held : (part + 1) * held, :]


def first_score_kernel(parts_count, held, *refs):
    part_refs, query_refs = refs[:parts_count], refs[parts_count : parts_count + len(held)]
    grads_ref, sums_ref, out_t_ref = refs[parts_count + len(held) :]
    rank, tokens = out_t_ref.shape
    core = lax.rem(lax.axis_index("ex"), 2)
    total = part_refs[0][...]
    for part_ref in part_refs[1:]:
        total = total + part_ref[...].astype(jnp.float32)
    out_t_ref[...] = total[rank:, :]
    even = out_t_ref[pl.ds(0, rank // 2, stride=2), :]
    odd = out_t_ref[pl.ds(1, rank // 2, stride=2), :]
    token = lax.broadcasted_iota(jnp.int32, (rank, tokens), 1)
    for n in range(tokens // SEQ):
        mine = jnp.where((token >= n * SEQ) & (token < (n + 1) * SEQ), total[:rank, :], 0.0)
        for side, rows in enumerate((even, odd)):
            grads_ref[n, :, side * rank : (side + 1) * rank] = lax.dot_general(
                rows, mine, LANES_BY_LANES, precision=lax.Precision.HIGHEST, preferred_element_type=jnp.float32
            )
    sums_ref[...] = jnp.zeros_like(sums_ref)
    for queries_ref, (other, chips) in zip(query_refs, held):
        add_scores(queries_ref, chips, lax.rem(core + other, 2), grads_ref, sums_ref)


def last_score_kernel(chips, grads_ref, before_ref, queries_ref, out_ref, sums_ref):
    core = lax.rem(lax.axis_index("ex"), 2)
    sums_ref[...] = before_ref[...]
    add_scores(queries_ref, chips, lax.rem(core + 1, 2), grads_ref, sums_ref)
    examples, *rows, lanes = sums_ref.shape
    ones = jnp.ones((8, lanes), jnp.float32)
    for n in range(examples):
        row = lax.dot_general(
            ones,
            sums_ref[n].reshape(out_ref.shape[1], lanes),
            LANES_BY_LANES,
            precision=lax.Precision.HIGHEST,
            preferred_element_type=jnp.float32,
        )
        out_ref[n : n + 1, :] = row[0:1, :]


def first_scores(parts, queries, held, rank):
    tokens = parts[0].shape[1]
    examples = tokens // SEQ
    chips = 2 * queries[0].shape[0]
    return pl.pallas_call(
        functools.partial(first_score_kernel, len(parts), held),
        out_shape=[
            jax.ShapeDtypeStruct((examples, rank // 2, 2 * rank), jnp.float32),
            jax.ShapeDtypeStruct((examples, chips, 2, queries[0].shape[1], 2 * rank), jnp.float32),
        ],
        scratch_shapes=[pltpu.VMEM((rank, tokens), jnp.float32)],
        compiler_params=PARAMS,
    )(*parts, *queries)


def last_scores(grads, sums, queries, chips):
    examples, all_chips, cores, held, _ = sums.shape
    return pl.pallas_call(
        functools.partial(last_score_kernel, chips),
        out_shape=jax.ShapeDtypeStruct((examples, all_chips * cores * held), jnp.float32),
        scratch_shapes=[pltpu.VMEM(sums.shape, jnp.float32)],
        compiler_params=PARAMS,
    )(grads, sums, queries)


def shards(inputs, out_grads, proj_in, proj_out, queries):
    devices = lax.axis_size("ex")
    chips = devices // 2
    depth = chips // 2
    rank = proj_in.shape[1]
    together = lax.optimization_barrier

    def swap(array, chip=0, core=0):
        distance = 2 * chip + core
        return lax.ppermute(array, "ex", [(i, i ^ distance) for i in range(devices)])

    steps = [1 << bit for bit in reversed(range(chips.bit_length() - 1))]
    held, reach = queries[None], [0]
    came_held = swap(held, chip=steps[0])
    lows = project(inputs, out_grads, proj_in.T, proj_out.T, devices)
    came_held, lows = together((came_held, lows))
    given_y, given, kept_y, kept = lows
    came_y = swap(given_y, core=1)
    came = swap(given, core=1)
    for last, step in zip(steps, steps[1:-1]):
        held, reach = stack(held, came_held), reach + [chip ^ last for chip in reach]
        came_held = swap(held, chip=step)
    across = swap(add_given(kept_y, came_y), chip=1)
    held, reach = stack(held, came_held), reach + [chip ^ steps[-2] for chip in reach]
    came_held = swap(held, chip=1)
    other_held = swap(held, core=1)
    across, came = together((across, came))

    types = [jnp.float32 if z < depth // 2 else jnp.bfloat16 for z in range(depth)]
    parts = list(add_kept(kept, came, across, types))
    for z in list(range(depth // 2, depth)) + list(range(1, depth // 2)):
        parts[z] = swap(parts[z], chip=2 * z)
    came_held, other_held, parts = together((came_held, other_held, parts))
    other_came = swap(came_held, core=1)
    reach_y = [chip ^ 1 for chip in reach]
    held = [held, other_held, came_held]
    grads, scores = first_scores(parts, held, [(0, reach), (1, reach), (0, reach_y)], rank)
    return last_scores(grads, scores, other_came, reach_y)


def solution(mesh):
    return jax.shard_map(
        shards,
        mesh=mesh,
        in_specs=(
            P("ex", "groups"),
            P("ex", "groups"),
            P("ex", None),
            P("ex", None),
            P("ex", None),
        ),
        out_specs=P(("groups", "ex"), None),
        check_vma=False,
    )
```

```python
import functools

import jax
import jax.numpy as jnp
from jax import lax
from jax.experimental import pallas as pl
from jax.experimental.pallas import tpu as pltpu
from jax.sharding import PartitionSpec as P

SEQ = 64
VMEM_BYTES = 32 * 1024 * 1024
AHEAD = 7
NEAR_PAD = 64
CODE_SCALE = 2.0**-8
LANES_BY_LANES = (((1,), (1,)), ((), ()))
HBM_SPEC = pl.BlockSpec(memory_space=pltpu.HBM)
VMEM_SPEC = pl.BlockSpec(memory_space=pltpu.VMEM)
PARAMS = pltpu.CompilerParams(vmem_limit_bytes=VMEM_BYTES)


def project_kernel(x_hbm, w_hbm, p_in_hbm, p_out_hbm, *refs):
    given_y, given_here, kept_y, kept_here, x_buf, w_buf, p_in, p_out, low, p_sems, x_sems, w_sems = refs
    here = lax.axis_index("ex")
    core, chip = lax.rem(here, 2), lax.div(here, 2)
    depth = kept_y.shape[0]
    rank, width = kept_y.shape[1] // 2, kept_y.shape[2]
    matrices = [
        pltpu.make_async_copy(p_in_hbm, p_in, p_sems.at[0]),
        pltpu.make_async_copy(p_out_hbm, p_out, p_sems.at[1]),
    ]
    chunks = []
    for top, hbm, buf, sems, matrix in ((0, x_hbm, x_buf, x_sems, p_in), (rank, w_hbm, w_buf, w_sems, p_out)):
        rows = buf.shape[0] // sems.shape[0]
        for chunk in range(sems.shape[0]):
            part = pl.ds(chunk * rows, rows)
            copy = pltpu.make_async_copy(hbm.at[part, :], buf.at[part, :], sems.at[chunk])
            chunks.append((slice(top, top + rank), part, buf, matrix, copy, chunk == 0))
    for copy in matrices + [chunk[4] for chunk in chunks[:AHEAD]]:
        copy.start()
    for copy in matrices:
        copy.wait()
    step = min(1024, low.shape[1])
    for index, (lines, part, buf, matrix, copy, first) in enumerate(chunks):
        copy.wait()
        if index + AHEAD < len(chunks):
            chunks[index + AHEAD][4].start()
        for column in range(0, low.shape[1], step):
            columns = slice(column, column + step)
            product = jnp.dot(matrix[:, part], buf[part, columns], preferred_element_type=jnp.float32)
            low[lines, columns] = product if first else low[lines, columns] + product
    for flip, given_ref, kept_ref in ((1, given_y, kept_y), (0, given_here, kept_here)):
        for z in range(depth):
            place = lax.bitwise_xor(chip, 2 * z + flip)
            both = low[:, pl.ds(pl.multiple_of(place * 2 * width, 2 * width), 2 * width)]
            left, right = both[:, :width], both[:, width:]
            given_ref[z] = jnp.where(core == 0, right, left)
            kept_ref[z] = jnp.where(core == 0, left, right)


def project(inputs, out_grads, proj_in_t, proj_out_t, devices):
    arrays = [pltpu.with_memory_space_constraint(a, pltpu.HBM) for a in (inputs, out_grads, proj_in_t, proj_out_t)]
    width = inputs.shape[1] // devices
    rank = proj_in_t.shape[0]
    low = jax.ShapeDtypeStruct((devices // 4, 2 * rank, width), jnp.float32)
    chunks = [a.shape[0] // rows if a.shape[0] % rows == 0 else 1 for a, rows in ((inputs, 128), (out_grads, 256))]
    return pl.pallas_call(
        project_kernel,
        out_shape=[low] * 4,
        in_specs=[HBM_SPEC] * 4,
        out_specs=[VMEM_SPEC] * 4,
        scratch_shapes=[pltpu.VMEM(a.shape, jnp.bfloat16) for a in arrays]
        + [pltpu.VMEM((2 * rank, inputs.shape[1]), jnp.float32), pltpu.SemaphoreType.DMA((2,))]
        + [pltpu.SemaphoreType.DMA((count,)) for count in chunks],
        compiler_params=PARAMS,
        cost_estimate=pl.CostEstimate(
            flops=2 * rank * (inputs.size + out_grads.size),
            bytes_accessed=2 * (inputs.size + out_grads.size),
            transcendentals=0,
        ),
    )(*arrays)


def put_coded(out_ref, low):
    rows = low.shape[0]
    rounded = low.astype(jnp.bfloat16)
    out_ref[:rows, :] = rounded
    rounded = rounded.astype(jnp.float32)
    left = (low - rounded) / jnp.maximum(jnp.abs(rounded) * CODE_SCALE, 1e-30)
    level = jnp.clip(jnp.floor(2.0 * left) + 2.0, 0.0, 3.0)
    part = rows // 4
    word = level[:part, :]
    for index in range(1, 4):
        word = word + 4.0**index * level[index * part : (index + 1) * part, :]
    out_ref[rows:, :] = word.astype(jnp.bfloat16)


def add_coded(total, ref):
    part = ref.shape[0] // 5
    word = ref[4 * part :, :].astype(jnp.float32)
    parts = []
    for index in reversed(range(4)):
        level = jnp.floor(word * 0.25**index)
        word = word - level * 4.0**index
        rounded = ref[index * part : (index + 1) * part, :].astype(jnp.float32)
        left = jnp.abs(rounded) * ((CODE_SCALE * 0.5) * level - CODE_SCALE * 0.75)
        parts.append((slice(index * part, (index + 1) * part), total(index * part, part) + rounded + left))
    return parts


def add_given_kernel(kept_ref, came_ref, out_ref):
    for block in range(out_ref.shape[0]):
        put_coded(out_ref.at[block], kept_ref[block] + came_ref[block])


def add_given(kept, came):
    blocks, rows, width = kept.shape
    return pl.pallas_call(
        add_given_kernel,
        out_shape=jax.ShapeDtypeStruct((blocks, rows // 4 * 5, width), jnp.bfloat16),
        compiler_params=PARAMS,
    )(kept, came)


def add_kept_kernel(kept_ref, came_ref, across_ref, *out_refs):
    for z, out_ref in enumerate(out_refs):
        def here(first, rows):
            return kept_ref[z, first : first + rows, :] + came_ref[z, first : first + rows, :]

        for rows, total in add_coded(here, across_ref.at[z]):
            out_ref[rows, :] = total.astype(out_ref.dtype)


def add_kept(kept, came, across, types):
    _, rows, width = kept.shape
    heights = [rows if z == 0 or dtype == jnp.bfloat16 else rows + NEAR_PAD for z, dtype in enumerate(types)]
    return pl.pallas_call(
        add_kept_kernel,
        out_shape=[jax.ShapeDtypeStruct((height, width), dtype) for height, dtype in zip(heights, types)],
        compiler_params=PARAMS,
    )(kept, came, across)


def stack_kernel(left_ref, right_ref, out_ref):
    out_ref[: left_ref.shape[0]] = left_ref[...]
    out_ref[left_ref.shape[0] :] = right_ref[...]


def stack(left, right):
    return pl.pallas_call(
        stack_kernel,
        out_shape=jax.ShapeDtypeStruct((2 * left.shape[0],) + left.shape[1:], left.dtype),
        compiler_params=PARAMS,
    )(left, right)


def add_scores(queries_ref, chips, place, grads, sums_ref):
    examples, half_rank, lanes = grads.shape
    held = queries_ref.shape[1]
    step = 4 if len(chips) % 4 == 0 else 2
    here = lax.div(lax.axis_index("ex"), 2)
    for first in range(0, len(chips), step):
        sums = [jnp.zeros((step * held, lanes), jnp.float32) for _ in range(examples)]
        for k in range(half_rank):
            query = queries_ref[first : first + step, :, k * lanes : (k + 1) * lanes].astype(jnp.float32)
            query = query.reshape(step * held, lanes)
            for n in range(examples):
                sums[n] = sums[n] + query * grads[n, k : k + 1, :]
        for part in range(step):
            source = lax.bitwise_xor(here, chips[first + part])
            for n in range(examples):
                sums_ref[n, source, place] = sums[n][part * held : (part + 1) * held, :]


def first_score_kernel(parts_count, held, *refs):
    part_refs, query_refs = refs[:parts_count], refs[parts_count : parts_count + len(held)]
    grads_ref, sums_ref, out_t_ref = refs[parts_count + len(held) :]
    rank, tokens = out_t_ref.shape
    core = lax.rem(lax.axis_index("ex"), 2)
    total = part_refs[0][...]
    for part_ref in part_refs[1:]:
        total = total + part_ref[: 2 * rank, :].astype(jnp.float32)
    out_t_ref[...] = total[rank:, :]
    even = out_t_ref[pl.ds(0, rank // 2, stride=2), :]
    odd = out_t_ref[pl.ds(1, rank // 2, stride=2), :]
    token = lax.broadcasted_iota(jnp.int32, (rank, tokens), 1)
    for n in range(tokens // SEQ):
        mine = jnp.where((token >= n * SEQ) & (token < (n + 1) * SEQ), total[:rank, :], 0.0)
        for side, rows in enumerate((even, odd)):
            grads_ref[n, :, side * rank : (side + 1) * rank] = lax.dot_general(
                rows, mine, LANES_BY_LANES, precision=lax.Precision.HIGHEST, preferred_element_type=jnp.float32
            )
    sums_ref[...] = jnp.zeros_like(sums_ref)
    for queries_ref, (other, chips) in zip(query_refs, held):
        add_scores(queries_ref, chips, lax.rem(core + other, 2), grads_ref, sums_ref)


def last_score_kernel(chips, grads_ref, before_ref, queries_ref, out_ref, sums_ref):
    core = lax.rem(lax.axis_index("ex"), 2)
    sums_ref[...] = before_ref[...]
    add_scores(queries_ref, chips, lax.rem(core + 1, 2), grads_ref, sums_ref)
    examples, *rows, lanes = sums_ref.shape
    ones = jnp.ones((8, lanes), jnp.float32)
    for n in range(examples):
        row = lax.dot_general(
            ones,
            sums_ref[n].reshape(out_ref.shape[1], lanes),
            LANES_BY_LANES,
            precision=lax.Precision.HIGHEST,
            preferred_element_type=jnp.float32,
        )
        out_ref[n : n + 1, :] = row[0:1, :]


def first_scores(parts, queries, held, rank):
    tokens = parts[0].shape[1]
    examples = tokens // SEQ
    chips = 2 * queries[0].shape[0]
    return pl.pallas_call(
        functools.partial(first_score_kernel, len(parts), held),
        out_shape=[
            jax.ShapeDtypeStruct((examples, rank // 2, 2 * rank), jnp.float32),
            jax.ShapeDtypeStruct((examples, chips, 2, queries[0].shape[1], 2 * rank), jnp.float32),
        ],
        scratch_shapes=[pltpu.VMEM((rank, tokens), jnp.float32)],
        compiler_params=PARAMS,
    )(*parts, *queries)


def last_scores(grads, sums, queries, chips):
    examples, all_chips, cores, held, _ = sums.shape
    return pl.pallas_call(
        functools.partial(last_score_kernel, chips),
        out_shape=jax.ShapeDtypeStruct((examples, all_chips * cores * held), jnp.float32),
        scratch_shapes=[pltpu.VMEM(sums.shape, jnp.float32)],
        compiler_params=PARAMS,
    )(grads, sums, queries)


def shards(inputs, out_grads, proj_in, proj_out, queries):
    devices = lax.axis_size("ex")
    chips = devices // 2
    depth = chips // 2
    rank = proj_in.shape[1]
    together = lax.optimization_barrier

    def swap(array, chip=0, core=0):
        distance = 2 * chip + core
        return lax.ppermute(array, "ex", [(i, i ^ distance) for i in range(devices)])

    steps = [1 << bit for bit in reversed(range(chips.bit_length() - 1))]
    held, reach = queries[None], [0]
    came_held = swap(held, chip=steps[0])
    lows = project(inputs, out_grads, proj_in.T, proj_out.T, devices)
    came_held, lows = together((came_held, lows))
    given_y, given, kept_y, kept = lows
    came_y = swap(given_y, core=1)
    came = swap(given, core=1)
    for last, step in zip(steps, steps[1:-1]):
        held, reach = stack(held, came_held), reach + [chip ^ last for chip in reach]
        came_held = swap(held, chip=step)
    across = swap(add_given(kept_y, came_y), chip=1)
    held, reach = stack(held, came_held), reach + [chip ^ steps[-2] for chip in reach]
    came_held = swap(held, chip=1)
    other_held = swap(held, core=1)
    across, came = together((across, came))

    types = [jnp.float32 if z < depth // 2 else jnp.bfloat16 for z in range(depth)]
    parts = list(add_kept(kept, came, across, types))
    for z in list(range(depth // 2, depth)) + list(range(1, depth // 2)):
        parts[z] = swap(parts[z], chip=2 * z)
    came_held, other_held, parts = together((came_held, other_held, parts))
    other_came = swap(came_held, core=1)
    reach_y = [chip ^ 1 for chip in reach]
    held = [held, other_held, came_held]
    grads, scores = first_scores(parts, held, [(0, reach), (1, reach), (0, reach_y)], rank)
    return last_scores(grads, scores, other_came, reach_y)


def solution(mesh):
    return jax.shard_map(
        shards,
        mesh=mesh,
        in_specs=(
            P("ex", "groups"),
            P("ex", "groups"),
            P("ex", None),
            P("ex", None),
            P("ex", None),
        ),
        out_specs=P(("groups", "ex"), None),
        check_vma=False,
    )
```

```python
import functools

import jax
import jax.numpy as jnp
from jax import lax
from jax.experimental import pallas as pl
from jax.experimental.pallas import tpu as pltpu
from jax.sharding import PartitionSpec as P

SEQ = 64
VMEM_BYTES = 32 * 1024 * 1024
AHEAD = 7
NEAR_PAD = 64
CODE_SCALE = 2.0**-8
LANES_BY_LANES = (((1,), (1,)), ((), ()))
HBM_SPEC = pl.BlockSpec(memory_space=pltpu.HBM)
VMEM_SPEC = pl.BlockSpec(memory_space=pltpu.VMEM)
PARAMS = pltpu.CompilerParams(vmem_limit_bytes=VMEM_BYTES)


def project_kernel(x_hbm, w_hbm, p_in_hbm, p_out_hbm, *refs):
    *given_y, given_here, kept_y, kept_here, x_buf, w_buf, p_in, p_out, low, p_sems, x_sems, w_sems = refs
    here = lax.axis_index("ex")
    core, chip = lax.rem(here, 2), lax.div(here, 2)
    depth = kept_y.shape[0]
    rank, width = kept_y.shape[1] // 2, kept_y.shape[2]
    matrices = [
        pltpu.make_async_copy(p_in_hbm, p_in, p_sems.at[0]),
        pltpu.make_async_copy(p_out_hbm, p_out, p_sems.at[1]),
    ]
    chunks = []
    for top, hbm, buf, sems, matrix in ((0, x_hbm, x_buf, x_sems, p_in), (rank, w_hbm, w_buf, w_sems, p_out)):
        rows = buf.shape[0] // sems.shape[0]
        for chunk in range(sems.shape[0]):
            part = pl.ds(chunk * rows, rows)
            copy = pltpu.make_async_copy(hbm.at[part, :], buf.at[part, :], sems.at[chunk])
            chunks.append((slice(top, top + rank), part, buf, matrix, copy, chunk == 0))
    for copy in matrices + [chunk[4] for chunk in chunks[:AHEAD]]:
        copy.start()
    for copy in matrices:
        copy.wait()
    step = min(1024, low.shape[1])
    for index, (lines, part, buf, matrix, copy, first) in enumerate(chunks):
        copy.wait()
        if index + AHEAD < len(chunks):
            chunks[index + AHEAD][4].start()
        for column in range(0, low.shape[1], step):
            columns = slice(column, column + step)
            product = jnp.dot(matrix[:, part], buf[part, columns], preferred_element_type=jnp.float32)
            low[lines, columns] = product if first else low[lines, columns] + product
    for flip, given_refs, kept_ref in ((1, given_y, kept_y), (0, [given_here], kept_here)):
        for z in range(depth):
            place = lax.bitwise_xor(chip, 2 * z + flip)
            both = low[:, pl.ds(pl.multiple_of(place * 2 * width, 2 * width), 2 * width)]
            left, right = both[:, :width], both[:, width:]
            given_ref = given_refs[z * len(given_refs) // depth]
            given_ref[z % given_ref.shape[0]] = jnp.where(core == 0, right, left)
            kept_ref[z] = jnp.where(core == 0, left, right)


def project(inputs, out_grads, proj_in_t, proj_out_t, devices):
    arrays = [pltpu.with_memory_space_constraint(a, pltpu.HBM) for a in (inputs, out_grads, proj_in_t, proj_out_t)]
    width = inputs.shape[1] // devices
    rank = proj_in_t.shape[0]
    low = jax.ShapeDtypeStruct((devices // 4, 2 * rank, width), jnp.float32)
    half = jax.ShapeDtypeStruct((devices // 8, 2 * rank, width), jnp.float32)
    chunks = [a.shape[0] // rows if a.shape[0] % rows == 0 else 1 for a, rows in ((inputs, 128), (out_grads, 256))]
    return pl.pallas_call(
        project_kernel,
        out_shape=[half] * 2 + [low] * 3,
        in_specs=[HBM_SPEC] * 4,
        out_specs=[VMEM_SPEC] * 5,
        scratch_shapes=[pltpu.VMEM(a.shape, jnp.bfloat16) for a in arrays]
        + [pltpu.VMEM((2 * rank, inputs.shape[1]), jnp.float32), pltpu.SemaphoreType.DMA((2,))]
        + [pltpu.SemaphoreType.DMA((count,)) for count in chunks],
        compiler_params=PARAMS,
        cost_estimate=pl.CostEstimate(
            flops=2 * rank * (inputs.size + out_grads.size),
            bytes_accessed=2 * (inputs.size + out_grads.size),
            transcendentals=0,
        ),
    )(*arrays)


def put_coded(out_ref, low):
    rows = low.shape[0]
    rounded = low.astype(jnp.bfloat16)
    out_ref[:rows, :] = rounded
    rounded = rounded.astype(jnp.float32)
    left = (low - rounded) / jnp.maximum(jnp.abs(rounded) * CODE_SCALE, 1e-30)
    level = jnp.clip(jnp.floor(2.0 * left) + 2.0, 0.0, 3.0)
    part = rows // 4
    word = level[:part, :]
    for index in range(1, 4):
        word = word + 4.0**index * level[index * part : (index + 1) * part, :]
    out_ref[rows:, :] = word.astype(jnp.bfloat16)


def add_coded(total, ref):
    part = ref.shape[0] // 5
    word = ref[4 * part :, :].astype(jnp.float32)
    parts = []
    for index in reversed(range(4)):
        level = jnp.floor(word * 0.25**index)
        word = word - level * 4.0**index
        rounded = ref[index * part : (index + 1) * part, :].astype(jnp.float32)
        left = jnp.abs(rounded) * ((CODE_SCALE * 0.5) * level - CODE_SCALE * 0.75)
        parts.append((slice(index * part, (index + 1) * part), total(index * part, part) + rounded + left))
    return parts


def add_given_kernel(kept_ref, *refs):
    *came_refs, out_ref = refs
    half = came_refs[0].shape[0]
    for block in range(out_ref.shape[0]):
        put_coded(out_ref.at[block], kept_ref[block] + came_refs[block // half][block % half])


def add_given(kept, came):
    blocks, rows, width = kept.shape
    return pl.pallas_call(
        add_given_kernel,
        out_shape=jax.ShapeDtypeStruct((blocks, rows // 4 * 5, width), jnp.bfloat16),
        compiler_params=PARAMS,
    )(kept, *came)


def add_kept_kernel(kept_ref, came_ref, across_ref, *out_refs):
    for z, out_ref in enumerate(out_refs):
        def here(first, rows):
            return kept_ref[z, first : first + rows, :] + came_ref[z, first : first + rows, :]

        for rows, total in add_coded(here, across_ref.at[z]):
            out_ref[rows, :] = total.astype(out_ref.dtype)


def add_kept(kept, came, across, types):
    _, rows, width = kept.shape
    heights = [rows if z == 0 or dtype == jnp.bfloat16 else rows + NEAR_PAD for z, dtype in enumerate(types)]
    return pl.pallas_call(
        add_kept_kernel,
        out_shape=[jax.ShapeDtypeStruct((height, width), dtype) for height, dtype in zip(heights, types)],
        compiler_params=PARAMS,
    )(kept, came, across)


def stack_kernel(left_ref, right_ref, out_ref):
    out_ref[: left_ref.shape[0]] = left_ref[...]
    out_ref[left_ref.shape[0] :] = right_ref[...]


def stack(left, right):
    return pl.pallas_call(
        stack_kernel,
        out_shape=jax.ShapeDtypeStruct((2 * left.shape[0],) + left.shape[1:], left.dtype),
        compiler_params=PARAMS,
    )(left, right)


def add_scores(queries_ref, chips, place, grads, sums_ref):
    examples, half_rank, lanes = grads.shape
    held = queries_ref.shape[1]
    step = 4 if len(chips) % 4 == 0 else 2
    here = lax.div(lax.axis_index("ex"), 2)
    for first in range(0, len(chips), step):
        sums = [jnp.zeros((step * held, lanes), jnp.float32) for _ in range(examples)]
        for k in range(half_rank):
            query = queries_ref[first : first + step, :, k * lanes : (k + 1) * lanes].astype(jnp.float32)
            query = query.reshape(step * held, lanes)
            for n in range(examples):
                sums[n] = sums[n] + query * grads[n, k : k + 1, :]
        for part in range(step):
            source = lax.bitwise_xor(here, chips[first + part])
            for n in range(examples):
                sums_ref[n, source, place] = sums[n][part * held : (part + 1) * held, :]


def first_score_kernel(parts_count, held, *refs):
    part_refs, query_refs = refs[:parts_count], refs[parts_count : parts_count + len(held)]
    grads_ref, sums_ref, out_t_ref = refs[parts_count + len(held) :]
    rank, tokens = out_t_ref.shape
    core = lax.rem(lax.axis_index("ex"), 2)
    total = part_refs[0][...]
    for part_ref in part_refs[1:]:
        total = total + part_ref[: 2 * rank, :].astype(jnp.float32)
    out_t_ref[...] = total[rank:, :]
    even = out_t_ref[pl.ds(0, rank // 2, stride=2), :]
    odd = out_t_ref[pl.ds(1, rank // 2, stride=2), :]
    token = lax.broadcasted_iota(jnp.int32, (rank, tokens), 1)
    for n in range(tokens // SEQ):
        mine = jnp.where((token >= n * SEQ) & (token < (n + 1) * SEQ), total[:rank, :], 0.0)
        for side, rows in enumerate((even, odd)):
            grads_ref[n, :, side * rank : (side + 1) * rank] = lax.dot_general(
                rows, mine, LANES_BY_LANES, precision=lax.Precision.HIGHEST, preferred_element_type=jnp.float32
            )
    sums_ref[...] = jnp.zeros_like(sums_ref)
    for queries_ref, (other, chips) in zip(query_refs, held):
        add_scores(queries_ref, chips, lax.rem(core + other, 2), grads_ref, sums_ref)


def last_score_kernel(chips, grads_ref, before_ref, queries_ref, out_ref, sums_ref):
    core = lax.rem(lax.axis_index("ex"), 2)
    sums_ref[...] = before_ref[...]
    add_scores(queries_ref, chips, lax.rem(core + 1, 2), grads_ref, sums_ref)
    examples, *rows, lanes = sums_ref.shape
    sums = sums_ref[...].reshape(examples * out_ref.shape[1], lanes)
    high = sums.astype(jnp.bfloat16)
    low = (sums - high.astype(jnp.float32)).astype(jnp.bfloat16)
    ones = jnp.ones((16, lanes), jnp.bfloat16)
    row = sum(lax.dot_general(ones, part, LANES_BY_LANES, preferred_element_type=jnp.float32) for part in (high, low))
    for n in range(examples):
        out_ref[n : n + 1, :] = row[0:1, n * out_ref.shape[1] : (n + 1) * out_ref.shape[1]]


def first_scores(parts, queries, held, rank):
    tokens = parts[0].shape[1]
    examples = tokens // SEQ
    chips = 2 * queries[0].shape[0]
    return pl.pallas_call(
        functools.partial(first_score_kernel, len(parts), held),
        out_shape=[
            jax.ShapeDtypeStruct((examples, rank // 2, 2 * rank), jnp.float32),
            jax.ShapeDtypeStruct((examples, chips, 2, queries[0].shape[1], 2 * rank), jnp.float32),
        ],
        scratch_shapes=[pltpu.VMEM((rank, tokens), jnp.float32)],
        compiler_params=PARAMS,
    )(*parts, *queries)


def last_scores(grads, sums, queries, chips):
    examples, all_chips, cores, held, _ = sums.shape
    return pl.pallas_call(
        functools.partial(last_score_kernel, chips),
        out_shape=jax.ShapeDtypeStruct((examples, all_chips * cores * held), jnp.float32),
        scratch_shapes=[pltpu.VMEM(sums.shape, jnp.float32)],
        compiler_params=PARAMS,
    )(grads, sums, queries)


def shards(inputs, out_grads, proj_in, proj_out, queries):
    devices = lax.axis_size("ex")
    chips = devices // 2
    depth = chips // 2
    rank = proj_in.shape[1]
    together = lax.optimization_barrier

    def swap(array, chip=0, core=0):
        distance = 2 * chip + core
        return lax.ppermute(array, "ex", [(i, i ^ distance) for i in range(devices)])

    steps = [1 << bit for bit in reversed(range(chips.bit_length() - 1))]
    held, reach = queries[None], [0]
    came_held = swap(held, chip=steps[0])
    lows = project(inputs, out_grads, proj_in.T, proj_out.T, devices)
    *given_y, given, kept_y, kept = lows
    came_y = [swap(array, core=1) for array in given_y]
    came = swap(given, core=1)
    for last, step in zip(steps, steps[1:-1]):
        held, reach = stack(held, came_held), reach + [chip ^ last for chip in reach]
        came_held = swap(held, chip=step)
    across = swap(add_given(kept_y, came_y), chip=1)
    held, reach = stack(held, came_held), reach + [chip ^ steps[-2] for chip in reach]
    came_held = swap(held, chip=1)
    other_held = swap(held, core=1)
    across, came = together((across, came))

    types = [jnp.float32 if z < depth // 2 else jnp.bfloat16 for z in range(depth)]
    parts = list(add_kept(kept, came, across, types))
    for z in list(range(depth // 2, depth)) + list(range(1, depth // 2)):
        parts[z] = swap(parts[z], chip=2 * z)
    came_held, other_held, parts = together((came_held, other_held, parts))
    other_came = swap(came_held, core=1)
    reach_y = [chip ^ 1 for chip in reach]
    held = [held, other_held, came_held]
    grads, scores = first_scores(parts, held, [(0, reach), (1, reach), (0, reach_y)], rank)
    return last_scores(grads, scores, other_came, reach_y)


def solution(mesh):
    return jax.shard_map(
        shards,
        mesh=mesh,
        in_specs=(
            P("ex", "groups"),
            P("ex", "groups"),
            P("ex", None),
            P("ex", None),
            P("ex", None),
        ),
        out_specs=P(("groups", "ex"), None),
        check_vma=False,
    )
```

```python
import functools

import jax
import jax.numpy as jnp
from jax import lax
from jax.experimental import pallas as pl
from jax.experimental.pallas import tpu as pltpu
from jax.sharding import PartitionSpec as P

SEQ = 64
VMEM_BYTES = 32 * 1024 * 1024
NEAR_PAD = 64
LOADED_ROWS = 256
CODE_SCALE = 2.0**-8
LANES_BY_LANES = (((1,), (1,)), ((), ()))
HBM_SPEC = pl.BlockSpec(memory_space=pltpu.HBM)
VMEM_SPEC = pl.BlockSpec(memory_space=pltpu.VMEM)
PARAMS = pltpu.CompilerParams(vmem_limit_bytes=VMEM_BYTES)


def project_loaded_kernel(x_hbm, w_hbm, p_in_hbm, p_out_hbm, low_in_ref, low_out_ref, x_buf, w_buf, p_in, p_out, sems, p_sems):
    matrices = [
        pltpu.make_async_copy(p_in_hbm, p_in, p_sems.at[0]),
        pltpu.make_async_copy(p_out_hbm, p_out, p_sems.at[1]),
    ]
    chunks = []
    for hbm, buf, matrix, low_ref in ((x_hbm, x_buf, p_in, low_in_ref), (w_hbm, w_buf, p_out, low_out_ref)):
        count = buf.shape[0] // LOADED_ROWS if buf.shape[0] % LOADED_ROWS == 0 else 1
        for chunk in range(count):
            part = pl.ds(chunk * (buf.shape[0] // count), buf.shape[0] // count)
            copy = pltpu.make_async_copy(hbm.at[part, :], buf.at[part, :], sems.at[len(chunks)])
            chunks.append((part, buf, matrix, low_ref, copy, chunk == 0))
    for copy in matrices + [chunk[4] for chunk in chunks]:
        copy.start()
    for copy in matrices:
        copy.wait()
    step = min(1024, low_in_ref.shape[1])
    for part, buf, matrix, low_ref, copy, first in chunks:
        copy.wait()
        for column in range(0, low_ref.shape[1], step):
            columns = slice(column, column + step)
            product = jnp.dot(matrix[:, part], buf[part, columns], preferred_element_type=jnp.float32)
            low_ref[:, columns] = product if first else low_ref[:, columns] + product


def project_loaded(inputs, out_grads, proj_in_t, proj_out_t, rows):
    arrays = [pltpu.with_memory_space_constraint(a, pltpu.HBM) for a in (inputs, out_grads, proj_in_t, proj_out_t)]
    rank, tokens = proj_in_t.shape[0], inputs.shape[1]
    chunks = sum(a // LOADED_ROWS if a % LOADED_ROWS == 0 else 1 for a in (inputs.shape[0], rows))
    return pl.pallas_call(
        project_loaded_kernel,
        out_shape=[jax.ShapeDtypeStruct((rank, tokens), jnp.float32)] * 2,
        in_specs=[HBM_SPEC] * 4,
        out_specs=[VMEM_SPEC] * 2,
        scratch_shapes=[
            pltpu.VMEM(inputs.shape, jnp.bfloat16),
            pltpu.VMEM((rows, tokens), jnp.bfloat16),
            pltpu.VMEM(proj_in_t.shape, jnp.bfloat16),
            pltpu.VMEM(proj_out_t.shape, jnp.bfloat16),
            pltpu.SemaphoreType.DMA((chunks,)),
            pltpu.SemaphoreType.DMA((2,)),
        ],
        compiler_params=PARAMS,
        cost_estimate=pl.CostEstimate(
            flops=2 * rank * (inputs.shape[0] + rows) * tokens,
            bytes_accessed=2 * (inputs.shape[0] + rows) * tokens,
            transcendentals=0,
        ),
    )(*arrays)


def project_kernel(done, low_in_ref, low_out_ref, p_ref, w_ref, *refs):
    *given_y, given_here, kept_y, kept_here = refs
    here = lax.axis_index("ex")
    core, chip = lax.rem(here, 2), lax.div(here, 2)
    depth = kept_y.shape[0]
    rank, width = kept_y.shape[1] // 2, kept_y.shape[2]
    for flip, given_refs, kept_ref in ((1, given_y, kept_y), (0, [given_here], kept_here)):
        for z in range(depth):
            place = lax.bitwise_xor(chip, 2 * z + flip)
            columns = pl.ds(pl.multiple_of(place * 2 * width, 2 * width), 2 * width)
            low_out = jnp.dot(p_ref[:, done:], w_ref[done:, columns], preferred_element_type=jnp.float32)
            low_out = low_out + low_out_ref[:, columns]
            given_ref = given_refs[z * len(given_refs) // depth]
            for lines, low in ((slice(0, rank), low_in_ref[:, columns]), (slice(rank, 2 * rank), low_out)):
                left, right = low[:, :width], low[:, width:]
                given_ref[z % given_ref.shape[0], lines, :] = jnp.where(core == 0, right, left)
                kept_ref[z, lines, :] = jnp.where(core == 0, left, right)


def project(inputs, out_grads, proj_in_t, proj_out_t, devices):
    rank, width = proj_in_t.shape[0], inputs.shape[1] // devices
    units = out_grads.shape[0]
    rows = 2 * LOADED_ROWS if units % LOADED_ROWS == 0 else 16
    lows = project_loaded(inputs, out_grads, proj_in_t, proj_out_t, rows)
    low = jax.ShapeDtypeStruct((devices // 4, 2 * rank, width), jnp.float32)
    half = jax.ShapeDtypeStruct((devices // 8, 2 * rank, width), jnp.float32)
    return pl.pallas_call(
        functools.partial(project_kernel, rows),
        out_shape=[half] * 2 + [low] * 3,
        in_specs=[VMEM_SPEC] * 4,
        out_specs=[VMEM_SPEC] * 5,
        compiler_params=PARAMS,
        cost_estimate=pl.CostEstimate(
            flops=2 * rank * out_grads.size, bytes_accessed=2 * out_grads.size, transcendentals=0
        ),
    )(*lows, proj_out_t, out_grads)


def put_coded(out_ref, low):
    rows = low.shape[0]
    rounded = low.astype(jnp.bfloat16)
    out_ref[:rows, :] = rounded
    rounded = rounded.astype(jnp.float32)
    left = (low - rounded) / jnp.maximum(jnp.abs(rounded) * CODE_SCALE, 1e-30)
    level = jnp.clip(jnp.floor(2.0 * left) + 2.0, 0.0, 3.0)
    part = rows // 4
    word = level[:part, :]
    for index in range(1, 4):
        word = word + 4.0**index * level[index * part : (index + 1) * part, :]
    out_ref[rows:, :] = word.astype(jnp.bfloat16)


def add_coded(total, ref):
    part = ref.shape[0] // 5
    word = ref[4 * part :, :].astype(jnp.float32)
    parts = []
    for index in reversed(range(4)):
        level = jnp.floor(word * 0.25**index)
        word = word - level * 4.0**index
        rounded = ref[index * part : (index + 1) * part, :].astype(jnp.float32)
        left = jnp.abs(rounded) * ((CODE_SCALE * 0.5) * level - CODE_SCALE * 0.75)
        parts.append((slice(index * part, (index + 1) * part), total(index * part, part) + rounded + left))
    return parts


def add_given_kernel(kept_ref, *refs):
    *came_refs, out_ref = refs
    half = came_refs[0].shape[0]
    for block in range(out_ref.shape[0]):
        put_coded(out_ref.at[block], kept_ref[block] + came_refs[block // half][block % half])


def add_given(kept, came):
    blocks, rows, width = kept.shape
    return pl.pallas_call(
        add_given_kernel,
        out_shape=jax.ShapeDtypeStruct((blocks, rows // 4 * 5, width), jnp.bfloat16),
        compiler_params=PARAMS,
    )(kept, *came)


def add_kept_kernel(kept_ref, came_ref, across_ref, *out_refs):
    for z, out_ref in enumerate(out_refs):
        def here(first, rows):
            return kept_ref[z, first : first + rows, :] + came_ref[z, first : first + rows, :]

        for rows, total in add_coded(here, across_ref.at[z]):
            out_ref[rows, :] = total.astype(out_ref.dtype)


def add_kept(kept, came, across, types):
    _, rows, width = kept.shape
    heights = [rows if z == 0 or dtype == jnp.bfloat16 else rows + NEAR_PAD for z, dtype in enumerate(types)]
    return pl.pallas_call(
        add_kept_kernel,
        out_shape=[jax.ShapeDtypeStruct((height, width), dtype) for height, dtype in zip(heights, types)],
        compiler_params=PARAMS,
    )(kept, came, across)


def stack_kernel(left_ref, right_ref, out_ref):
    out_ref[: left_ref.shape[0]] = left_ref[...]
    out_ref[left_ref.shape[0] :] = right_ref[...]


def stack(left, right):
    return pl.pallas_call(
        stack_kernel,
        out_shape=jax.ShapeDtypeStruct((2 * left.shape[0],) + left.shape[1:], left.dtype),
        compiler_params=PARAMS,
    )(left, right)


def add_scores(queries_ref, chips, place, grads, sums_ref):
    examples, half_rank, lanes = grads.shape
    held = queries_ref.shape[1]
    step = 4 if len(chips) % 4 == 0 else 2
    here = lax.div(lax.axis_index("ex"), 2)
    for first in range(0, len(chips), step):
        sums = [jnp.zeros((step * held, lanes), jnp.float32) for _ in range(examples)]
        for k in range(half_rank):
            query = queries_ref[first : first + step, :, k * lanes : (k + 1) * lanes].astype(jnp.float32)
            query = query.reshape(step * held, lanes)
            for n in range(examples):
                sums[n] = sums[n] + query * grads[n, k : k + 1, :]
        for part in range(step):
            source = lax.bitwise_xor(here, chips[first + part])
            for n in range(examples):
                sums_ref[n, source, place] = sums[n][part * held : (part + 1) * held, :]


def first_score_kernel(parts_count, held, *refs):
    part_refs, query_refs = refs[:parts_count], refs[parts_count : parts_count + len(held)]
    grads_ref, sums_ref, out_t_ref = refs[parts_count + len(held) :]
    rank, tokens = out_t_ref.shape
    core = lax.rem(lax.axis_index("ex"), 2)
    total = part_refs[0][...]
    for part_ref in part_refs[1:]:
        total = total + part_ref[: 2 * rank, :].astype(jnp.float32)
    out_t_ref[...] = total[rank:, :]
    even = out_t_ref[pl.ds(0, rank // 2, stride=2), :]
    odd = out_t_ref[pl.ds(1, rank // 2, stride=2), :]
    token = lax.broadcasted_iota(jnp.int32, (rank, tokens), 1)
    for n in range(tokens // SEQ):
        mine = jnp.where((token >= n * SEQ) & (token < (n + 1) * SEQ), total[:rank, :], 0.0)
        for side, rows in enumerate((even, odd)):
            grads_ref[n, :, side * rank : (side + 1) * rank] = lax.dot_general(
                rows, mine, LANES_BY_LANES, precision=lax.Precision.HIGHEST, preferred_element_type=jnp.float32
            )
    sums_ref[...] = jnp.zeros_like(sums_ref)
    for queries_ref, (other, chips) in zip(query_refs, held):
        add_scores(queries_ref, chips, lax.rem(core + other, 2), grads_ref, sums_ref)


def last_score_kernel(chips, grads_ref, before_ref, queries_ref, out_ref, sums_ref):
    core = lax.rem(lax.axis_index("ex"), 2)
    sums_ref[...] = before_ref[...]
    add_scores(queries_ref, chips, lax.rem(core + 1, 2), grads_ref, sums_ref)
    examples, *rows, lanes = sums_ref.shape
    sums = sums_ref[...].reshape(examples * out_ref.shape[1], lanes)
    high = sums.astype(jnp.bfloat16)
    low = (sums - high.astype(jnp.float32)).astype(jnp.bfloat16)
    ones = jnp.ones((16, lanes), jnp.bfloat16)
    row = sum(lax.dot_general(ones, part, LANES_BY_LANES, preferred_element_type=jnp.float32) for part in (high, low))
    for n in range(examples):
        out_ref[n : n + 1, :] = row[0:1, n * out_ref.shape[1] : (n + 1) * out_ref.shape[1]]


def first_scores(parts, queries, held, rank):
    tokens = parts[0].shape[1]
    examples = tokens // SEQ
    chips = 2 * queries[0].shape[0]
    return pl.pallas_call(
        functools.partial(first_score_kernel, len(parts), held),
        out_shape=[
            jax.ShapeDtypeStruct((examples, rank // 2, 2 * rank), jnp.float32),
            jax.ShapeDtypeStruct((examples, chips, 2, queries[0].shape[1], 2 * rank), jnp.float32),
        ],
        scratch_shapes=[pltpu.VMEM((rank, tokens), jnp.float32)],
        compiler_params=PARAMS,
    )(*parts, *queries)


def last_scores(grads, sums, queries, chips):
    examples, all_chips, cores, held, _ = sums.shape
    return pl.pallas_call(
        functools.partial(last_score_kernel, chips),
        out_shape=jax.ShapeDtypeStruct((examples, all_chips * cores * held), jnp.float32),
        scratch_shapes=[pltpu.VMEM(sums.shape, jnp.float32)],
        compiler_params=PARAMS,
    )(grads, sums, queries)


def shards(inputs, out_grads, proj_in, proj_out, queries):
    devices = lax.axis_size("ex")
    chips = devices // 2
    depth = chips // 2
    rank = proj_in.shape[1]
    together = lax.optimization_barrier

    def swap(array, chip=0, core=0):
        distance = 2 * chip + core
        return lax.ppermute(array, "ex", [(i, i ^ distance) for i in range(devices)])

    steps = [1 << bit for bit in reversed(range(chips.bit_length() - 1))]
    held, reach = queries[None], [0]
    came_held = swap(held, chip=steps[0])
    lows = project(inputs, out_grads, proj_in.T, proj_out.T, devices)
    *given_y, given, kept_y, kept = lows
    came_y = [swap(array, core=1) for array in given_y]
    came = swap(given, core=1)
    for last, step in zip(steps, steps[1:-1]):
        held, reach = stack(held, came_held), reach + [chip ^ last for chip in reach]
        came_held = swap(held, chip=step)
    across = swap(add_given(kept_y, came_y), chip=1)
    held, reach = stack(held, came_held), reach + [chip ^ steps[-2] for chip in reach]
    came_held = swap(held, chip=1)
    other_held = swap(held, core=1)
    across, came = together((across, came))

    types = [jnp.float32 if z < depth // 2 else jnp.bfloat16 for z in range(depth)]
    parts = list(add_kept(kept, came, across, types))
    for z in list(range(depth // 2, depth)) + list(range(1, depth // 2)):
        parts[z] = swap(parts[z], chip=2 * z)
    came_held, other_held, parts = together((came_held, other_held, parts))
    other_came = swap(came_held, core=1)
    reach_y = [chip ^ 1 for chip in reach]
    held = [held, other_held, came_held]
    grads, scores = first_scores(parts, held, [(0, reach), (1, reach), (0, reach_y)], rank)
    return last_scores(grads, scores, other_came, reach_y)


def solution(mesh):
    return jax.shard_map(
        shards,
        mesh=mesh,
        in_specs=(
            P("ex", "groups"),
            P("ex", "groups"),
            P("ex", None),
            P("ex", None),
            P("ex", None),
        ),
        out_specs=P(("groups", "ex"), None),
        check_vma=False,
    )
```

```python
import functools

import jax
import jax.numpy as jnp
from jax import lax
from jax.experimental import pallas as pl
from jax.experimental.pallas import tpu as pltpu
from jax.sharding import PartitionSpec as P

SEQ = 64
VMEM_BYTES = 32 * 1024 * 1024
NEAR_PAD = 64
LOADED_ROWS = 128
CODE_SCALE = 2.0**-8
LANES_BY_LANES = (((1,), (1,)), ((), ()))
HBM_SPEC = pl.BlockSpec(memory_space=pltpu.HBM)
VMEM_SPEC = pl.BlockSpec(memory_space=pltpu.VMEM)
PARAMS = pltpu.CompilerParams(vmem_limit_bytes=VMEM_BYTES)


def project_loaded_kernel(x_hbm, w_hbm, p_in_hbm, p_out_hbm, low_in_ref, low_out_ref, x_buf, w_buf, p_in, p_out, sems, p_sems):
    matrices = [
        pltpu.make_async_copy(p_in_hbm, p_in, p_sems.at[0]),
        pltpu.make_async_copy(p_out_hbm.at[:, pl.ds(0, p_out.shape[1])], p_out, p_sems.at[1]),
    ]
    chunks = []
    for hbm, buf, matrix, low_ref in ((x_hbm, x_buf, p_in, low_in_ref), (w_hbm, w_buf, p_out, low_out_ref)):
        count = buf.shape[0] // LOADED_ROWS if buf.shape[0] % LOADED_ROWS == 0 else 1
        for chunk in range(count):
            part = pl.ds(chunk * (buf.shape[0] // count), buf.shape[0] // count)
            copy = pltpu.make_async_copy(hbm.at[part, :], buf.at[part, :], sems.at[len(chunks)])
            chunks.append((part, buf, matrix, low_ref, copy, chunk == 0))
    for copy in matrices + [chunk[4] for chunk in chunks]:
        copy.start()
    for copy in matrices:
        copy.wait()
    step = min(1024, low_in_ref.shape[1])
    for part, buf, matrix, low_ref, copy, first in chunks:
        copy.wait()
        for column in range(0, low_ref.shape[1], step):
            columns = slice(column, column + step)
            product = jnp.dot(matrix[:, part], buf[part, columns], preferred_element_type=jnp.float32)
            low_ref[:, columns] = product if first else low_ref[:, columns] + product


def project_loaded(inputs, out_grads, proj_in_t, proj_out_t, rows):
    arrays = [pltpu.with_memory_space_constraint(a, pltpu.HBM) for a in (inputs, out_grads, proj_in_t, proj_out_t)]
    rank, tokens = proj_in_t.shape[0], inputs.shape[1]
    chunks = sum(a // LOADED_ROWS if a % LOADED_ROWS == 0 else 1 for a in (inputs.shape[0], rows))
    return pl.pallas_call(
        project_loaded_kernel,
        out_shape=[jax.ShapeDtypeStruct((rank, tokens), jnp.float32)] * 2,
        in_specs=[HBM_SPEC] * 4,
        out_specs=[VMEM_SPEC] * 2,
        scratch_shapes=[
            pltpu.VMEM(inputs.shape, jnp.bfloat16),
            pltpu.VMEM((rows, tokens), jnp.bfloat16),
            pltpu.VMEM(proj_in_t.shape, jnp.bfloat16),
            pltpu.VMEM((rank, max(rows, 128)), jnp.bfloat16),
            pltpu.SemaphoreType.DMA((chunks,)),
            pltpu.SemaphoreType.DMA((2,)),
        ],
        compiler_params=PARAMS,
        cost_estimate=pl.CostEstimate(
            flops=2 * rank * (inputs.shape[0] + rows) * tokens,
            bytes_accessed=2 * (inputs.shape[0] + rows) * tokens,
            transcendentals=0,
        ),
    )(*arrays)


def project_kernel(done, low_in_ref, low_out_ref, p_ref, w_ref, *refs):
    *given_y, given_here, kept_y, kept_here = refs
    here = lax.axis_index("ex")
    core, chip = lax.rem(here, 2), lax.div(here, 2)
    depth = kept_y.shape[0]
    rank, width = kept_y.shape[1] // 2, kept_y.shape[2]
    for flip, given_refs, kept_ref in ((1, given_y, kept_y), (0, [given_here], kept_here)):
        for z in range(depth):
            place = lax.bitwise_xor(chip, 2 * z + flip)
            columns = pl.ds(pl.multiple_of(place * 2 * width, 2 * width), 2 * width)
            low_out = jnp.dot(p_ref[:, done:], w_ref[done:, columns], preferred_element_type=jnp.float32)
            low_out = low_out + low_out_ref[:, columns]
            given_ref = given_refs[z * len(given_refs) // depth]
            for lines, low in ((slice(0, rank), low_in_ref[:, columns]), (slice(rank, 2 * rank), low_out)):
                left, right = low[:, :width], low[:, width:]
                given_ref[z % given_ref.shape[0], lines, :] = jnp.where(core == 0, right, left)
                kept_ref[z, lines, :] = jnp.where(core == 0, left, right)


def project(inputs, out_grads, proj_in_t, proj_out_t, devices):
    rank, width = proj_in_t.shape[0], inputs.shape[1] // devices
    units = out_grads.shape[0]
    rows = LOADED_ROWS if units % LOADED_ROWS == 0 else 16
    lows = project_loaded(inputs, out_grads, proj_in_t, proj_out_t, rows)
    low = jax.ShapeDtypeStruct((devices // 4, 2 * rank, width), jnp.float32)
    half = jax.ShapeDtypeStruct((devices // 8, 2 * rank, width), jnp.float32)
    return pl.pallas_call(
        functools.partial(project_kernel, rows),
        out_shape=[half] * 2 + [low] * 3,
        in_specs=[VMEM_SPEC] * 4,
        out_specs=[VMEM_SPEC] * 5,
        compiler_params=PARAMS,
        cost_estimate=pl.CostEstimate(
            flops=2 * rank * out_grads.size, bytes_accessed=2 * out_grads.size, transcendentals=0
        ),
    )(*lows, proj_out_t, out_grads)


def put_coded(out_ref, low):
    rows = low.shape[0]
    rounded = low.astype(jnp.bfloat16)
    out_ref[:rows, :] = rounded
    rounded = rounded.astype(jnp.float32)
    left = (low - rounded) / jnp.maximum(jnp.abs(rounded) * CODE_SCALE, 1e-30)
    level = jnp.clip(jnp.floor(2.0 * left) + 2.0, 0.0, 3.0)
    part = rows // 4
    word = level[:part, :]
    for index in range(1, 4):
        word = word + 4.0**index * level[index * part : (index + 1) * part, :]
    out_ref[rows:, :] = word.astype(jnp.bfloat16)


def add_coded(total, ref):
    part = ref.shape[0] // 5
    word = ref[4 * part :, :].astype(jnp.float32)
    parts = []
    for index in reversed(range(4)):
        level = jnp.floor(word * 0.25**index)
        word = word - level * 4.0**index
        rounded = ref[index * part : (index + 1) * part, :].astype(jnp.float32)
        left = jnp.abs(rounded) * ((CODE_SCALE * 0.5) * level - CODE_SCALE * 0.75)
        parts.append((slice(index * part, (index + 1) * part), total(index * part, part) + rounded + left))
    return parts


def add_given_kernel(kept_ref, *refs):
    *came_refs, out_ref = refs
    half = came_refs[0].shape[0]
    for block in range(out_ref.shape[0]):
        put_coded(out_ref.at[block], kept_ref[block] + came_refs[block // half][block % half])


def add_given(kept, came):
    blocks, rows, width = kept.shape
    return pl.pallas_call(
        add_given_kernel,
        out_shape=jax.ShapeDtypeStruct((blocks, rows // 4 * 5, width), jnp.bfloat16),
        compiler_params=PARAMS,
    )(kept, *came)


def add_kept_kernel(kept_ref, came_ref, across_ref, *out_refs):
    for z, out_ref in enumerate(out_refs):
        def here(first, rows):
            return kept_ref[z, first : first + rows, :] + came_ref[z, first : first + rows, :]

        for rows, total in add_coded(here, across_ref.at[z]):
            out_ref[rows, :] = total.astype(out_ref.dtype)


def add_kept(kept, came, across, types):
    _, rows, width = kept.shape
    heights = [rows if z == 0 or dtype == jnp.bfloat16 else rows + NEAR_PAD for z, dtype in enumerate(types)]
    return pl.pallas_call(
        add_kept_kernel,
        out_shape=[jax.ShapeDtypeStruct((height, width), dtype) for height, dtype in zip(heights, types)],
        compiler_params=PARAMS,
    )(kept, came, across)


def stack_kernel(left_ref, right_ref, out_ref):
    out_ref[: left_ref.shape[0]] = left_ref[...]
    out_ref[left_ref.shape[0] :] = right_ref[...]


def stack(left, right):
    return pl.pallas_call(
        stack_kernel,
        out_shape=jax.ShapeDtypeStruct((2 * left.shape[0],) + left.shape[1:], left.dtype),
        compiler_params=PARAMS,
    )(left, right)


def add_scores(queries_ref, chips, place, grads, sums_ref):
    examples, half_rank, lanes = grads.shape
    held = queries_ref.shape[1]
    step = 4 if len(chips) % 4 == 0 else 2
    here = lax.div(lax.axis_index("ex"), 2)
    for first in range(0, len(chips), step):
        sums = [jnp.zeros((step * held, lanes), jnp.float32) for _ in range(examples)]
        for k in range(half_rank):
            query = queries_ref[first : first + step, :, k * lanes : (k + 1) * lanes].astype(jnp.float32)
            query = query.reshape(step * held, lanes)
            for n in range(examples):
                sums[n] = sums[n] + query * grads[n, k : k + 1, :]
        for part in range(step):
            source = lax.bitwise_xor(here, chips[first + part])
            for n in range(examples):
                sums_ref[n, source, place] = sums[n][part * held : (part + 1) * held, :]


def first_score_kernel(parts_count, held, *refs):
    part_refs, query_refs = refs[:parts_count], refs[parts_count : parts_count + len(held)]
    grads_ref, sums_ref, out_t_ref = refs[parts_count + len(held) :]
    rank, tokens = out_t_ref.shape
    core = lax.rem(lax.axis_index("ex"), 2)
    total = part_refs[0][...]
    for part_ref in part_refs[1:]:
        total = total + part_ref[: 2 * rank, :].astype(jnp.float32)
    out_t_ref[...] = total[rank:, :]
    even = out_t_ref[pl.ds(0, rank // 2, stride=2), :]
    odd = out_t_ref[pl.ds(1, rank // 2, stride=2), :]
    token = lax.broadcasted_iota(jnp.int32, (rank, tokens), 1)
    for n in range(tokens // SEQ):
        mine = jnp.where((token >= n * SEQ) & (token < (n + 1) * SEQ), total[:rank, :], 0.0)
        for side, rows in enumerate((even, odd)):
            grads_ref[n, :, side * rank : (side + 1) * rank] = lax.dot_general(
                rows, mine, LANES_BY_LANES, precision=lax.Precision.HIGHEST, preferred_element_type=jnp.float32
            )
    sums_ref[...] = jnp.zeros_like(sums_ref)
    for queries_ref, (other, chips) in zip(query_refs, held):
        add_scores(queries_ref, chips, lax.rem(core + other, 2), grads_ref, sums_ref)


def last_score_kernel(chips, grads_ref, before_ref, queries_ref, out_ref, sums_ref):
    core = lax.rem(lax.axis_index("ex"), 2)
    sums_ref[...] = before_ref[...]
    add_scores(queries_ref, chips, lax.rem(core + 1, 2), grads_ref, sums_ref)
    examples, *rows, lanes = sums_ref.shape
    sums = sums_ref[...].reshape(examples * out_ref.shape[1], lanes)
    high = sums.astype(jnp.bfloat16)
    low = (sums - high.astype(jnp.float32)).astype(jnp.bfloat16)
    ones = jnp.ones((16, lanes), jnp.bfloat16)
    row = sum(lax.dot_general(ones, part, LANES_BY_LANES, preferred_element_type=jnp.float32) for part in (high, low))
    for n in range(examples):
        out_ref[n : n + 1, :] = row[0:1, n * out_ref.shape[1] : (n + 1) * out_ref.shape[1]]


def first_scores(parts, queries, held, rank):
    tokens = parts[0].shape[1]
    examples = tokens // SEQ
    chips = 2 * queries[0].shape[0]
    return pl.pallas_call(
        functools.partial(first_score_kernel, len(parts), held),
        out_shape=[
            jax.ShapeDtypeStruct((examples, rank // 2, 2 * rank), jnp.float32),
            jax.ShapeDtypeStruct((examples, chips, 2, queries[0].shape[1], 2 * rank), jnp.float32),
        ],
        scratch_shapes=[pltpu.VMEM((rank, tokens), jnp.float32)],
        compiler_params=PARAMS,
    )(*parts, *queries)


def last_scores(grads, sums, queries, chips):
    examples, all_chips, cores, held, _ = sums.shape
    return pl.pallas_call(
        functools.partial(last_score_kernel, chips),
        out_shape=jax.ShapeDtypeStruct((examples, all_chips * cores * held), jnp.float32),
        scratch_shapes=[pltpu.VMEM(sums.shape, jnp.float32)],
        compiler_params=PARAMS,
    )(grads, sums, queries)


def shards(inputs, out_grads, proj_in, proj_out, queries):
    devices = lax.axis_size("ex")
    chips = devices // 2
    depth = chips // 2
    rank = proj_in.shape[1]
    together = lax.optimization_barrier

    def swap(array, chip=0, core=0):
        distance = 2 * chip + core
        return lax.ppermute(array, "ex", [(i, i ^ distance) for i in range(devices)])

    steps = [1 << bit for bit in reversed(range(chips.bit_length() - 1))]
    held, reach = queries[None], [0]
    came_held = swap(held, chip=steps[0])
    lows = project(inputs, out_grads, proj_in.T, proj_out.T, devices)
    *given_y, given, kept_y, kept = lows
    came_y = [swap(array, core=1) for array in given_y]
    came = swap(given, core=1)
    for last, step in zip(steps, steps[1:-1]):
        held, reach = stack(held, came_held), reach + [chip ^ last for chip in reach]
        came_held = swap(held, chip=step)
    across = swap(add_given(kept_y, came_y), chip=1)
    held, reach = stack(held, came_held), reach + [chip ^ steps[-2] for chip in reach]
    came_held = swap(held, chip=1)
    other_held = swap(held, core=1)
    across, came = together((across, came))

    types = [jnp.float32 if z < depth // 2 else jnp.bfloat16 for z in range(depth)]
    parts = list(add_kept(kept, came, across, types))
    for z in list(range(depth // 2, depth)) + list(range(1, depth // 2)):
        parts[z] = swap(parts[z], chip=2 * z)
    came_held, other_held, parts = together((came_held, other_held, parts))
    other_came = swap(came_held, core=1)
    reach_y = [chip ^ 1 for chip in reach]
    held = [held, other_held, came_held]
    grads, scores = first_scores(parts, held, [(0, reach), (1, reach), (0, reach_y)], rank)
    return last_scores(grads, scores, other_came, reach_y)


def solution(mesh):
    return jax.shard_map(
        shards,
        mesh=mesh,
        in_specs=(
            P("ex", "groups"),
            P("ex", "groups"),
            P("ex", None),
            P("ex", None),
            P("ex", None),
        ),
        out_specs=P(("groups", "ex"), None),
        check_vma=False,
    )
```

```python
import functools

import jax
import jax.numpy as jnp
from jax import lax
from jax.experimental import pallas as pl
from jax.experimental.pallas import tpu as pltpu
from jax.sharding import PartitionSpec as P

SEQ = 64
VMEM_BYTES = 32 * 1024 * 1024
NEAR_PAD = 96
LOADED_ROWS = 128
LEFT_OVER = 0.36 * 2.0**-8
LANES_BY_LANES = (((1,), (1,)), ((), ()))
HBM_SPEC = pl.BlockSpec(memory_space=pltpu.HBM)
VMEM_SPEC = pl.BlockSpec(memory_space=pltpu.VMEM)
PARAMS = pltpu.CompilerParams(vmem_limit_bytes=VMEM_BYTES)


def project_loaded_kernel(x_hbm, w_hbm, p_in_hbm, p_out_hbm, low_in_ref, low_out_ref, x_buf, w_buf, p_in, p_out, sems, p_sems):
    matrices = [
        pltpu.make_async_copy(p_in_hbm, p_in, p_sems.at[0]),
        pltpu.make_async_copy(p_out_hbm.at[:, pl.ds(0, p_out.shape[1])], p_out, p_sems.at[1]),
    ]
    chunks = []
    for hbm, buf, matrix, low_ref in ((x_hbm, x_buf, p_in, low_in_ref), (w_hbm, w_buf, p_out, low_out_ref)):
        count = buf.shape[0] // LOADED_ROWS if buf.shape[0] % LOADED_ROWS == 0 else 1
        for chunk in range(count):
            part = pl.ds(chunk * (buf.shape[0] // count), buf.shape[0] // count)
            copy = pltpu.make_async_copy(hbm.at[part, :], buf.at[part, :], sems.at[len(chunks)])
            chunks.append((part, buf, matrix, low_ref, copy, chunk == 0))
    for copy in matrices + [chunk[4] for chunk in chunks]:
        copy.start()
    for copy in matrices:
        copy.wait()
    step = min(1024, low_in_ref.shape[1])
    for part, buf, matrix, low_ref, copy, first in chunks:
        copy.wait()
        for column in range(0, low_ref.shape[1], step):
            columns = slice(column, column + step)
            product = jnp.dot(matrix[:, part], buf[part, columns], preferred_element_type=jnp.float32)
            low_ref[:, columns] = product if first else low_ref[:, columns] + product


def project_loaded(inputs, out_grads, proj_in_t, proj_out_t, rows):
    arrays = [pltpu.with_memory_space_constraint(a, pltpu.HBM) for a in (inputs, out_grads, proj_in_t, proj_out_t)]
    rank, tokens = proj_in_t.shape[0], inputs.shape[1]
    chunks = sum(a // LOADED_ROWS if a % LOADED_ROWS == 0 else 1 for a in (inputs.shape[0], rows))
    return pl.pallas_call(
        project_loaded_kernel,
        out_shape=[jax.ShapeDtypeStruct((rank, tokens), jnp.float32)] * 2,
        in_specs=[HBM_SPEC] * 4,
        out_specs=[VMEM_SPEC] * 2,
        scratch_shapes=[
            pltpu.VMEM(inputs.shape, jnp.bfloat16),
            pltpu.VMEM((rows, tokens), jnp.bfloat16),
            pltpu.VMEM(proj_in_t.shape, jnp.bfloat16),
            pltpu.VMEM((rank, max(rows, 128)), jnp.bfloat16),
            pltpu.SemaphoreType.DMA((chunks,)),
            pltpu.SemaphoreType.DMA((2,)),
        ],
        compiler_params=PARAMS,
        cost_estimate=pl.CostEstimate(
            flops=2 * rank * (inputs.shape[0] + rows) * tokens,
            bytes_accessed=2 * (inputs.shape[0] + rows) * tokens,
            transcendentals=0,
        ),
    )(*arrays)


def project_kernel(done, low_in_ref, low_out_ref, p_ref, w_ref, *refs):
    *given, kept_y, kept_here = refs
    given_y, given_here = given[:-1], given[-1:]
    here = lax.axis_index("ex")
    core, chip = lax.rem(here, 2), lax.div(here, 2)
    depth = kept_y.shape[0]
    rank, width = kept_y.shape[1] // 2, kept_y.shape[2]
    for flip, given_refs, kept_ref in ((1, given_y, kept_y), (0, given_here, kept_here)):
        for z in range(depth):
            place = lax.bitwise_xor(chip, 2 * z + flip)
            columns = pl.ds(pl.multiple_of(place * 2 * width, 2 * width), 2 * width)
            low_out = jnp.dot(p_ref[:, done:], w_ref[done:, columns], preferred_element_type=jnp.float32)
            low_out = low_out + low_out_ref[:, columns]
            given_ref = given_refs[z * len(given_refs) // depth]
            for lines, low in ((slice(0, rank), low_in_ref[:, columns]), (slice(rank, 2 * rank), low_out)):
                left, right = low[:, :width], low[:, width:]
                given_ref[z % given_ref.shape[0], lines, :] = jnp.where(core == 0, right, left)
                kept_ref[z, lines, :] = jnp.where(core == 0, left, right)


def project(inputs, out_grads, proj_in_t, proj_out_t, devices):
    rank, width = proj_in_t.shape[0], inputs.shape[1] // devices
    units = out_grads.shape[0]
    rows = LOADED_ROWS if units % LOADED_ROWS == 0 else 16
    lows = project_loaded(inputs, out_grads, proj_in_t, proj_out_t, rows)
    low = jax.ShapeDtypeStruct((devices // 4, 2 * rank, width), jnp.float32)
    half = jax.ShapeDtypeStruct((devices // 8, 2 * rank, width), jnp.float32)
    return pl.pallas_call(
        functools.partial(project_kernel, rows),
        out_shape=[half] * 2 + [low] * 3,
        in_specs=[VMEM_SPEC] * 4,
        out_specs=[VMEM_SPEC] * 5,
        compiler_params=PARAMS,
        cost_estimate=pl.CostEstimate(
            flops=2 * rank * out_grads.size, bytes_accessed=2 * out_grads.size, transcendentals=0
        ),
    )(*lows, proj_out_t, out_grads)


def put_coded(out_ref, low):
    rows = low.shape[0]
    rounded = low.astype(jnp.bfloat16)
    out_ref[:rows, :] = rounded
    above = jnp.where(low > rounded.astype(jnp.float32), 1.0, 0.0)
    part = rows // 8
    word = above[:part, :]
    for index in range(1, 8):
        word = word + 2.0**index * above[index * part : (index + 1) * part, :]
    out_ref[rows:, :] = word.astype(jnp.bfloat16)


def add_coded(total, ref):
    part = ref.shape[0] // 9
    word = ref[8 * part :, :].astype(jnp.float32)
    parts = []
    for index in reversed(range(8)):
        above = jnp.floor(word * 0.5**index)
        word = word - above * 2.0**index
        rounded = ref[index * part : (index + 1) * part, :].astype(jnp.float32)
        left = jnp.abs(rounded) * ((2.0 * LEFT_OVER) * above - LEFT_OVER)
        parts.append((slice(index * part, (index + 1) * part), total(index * part, part) + rounded + left))
    return parts


def add_given_kernel(kept_ref, *refs):
    *came_refs, out_ref = refs
    half = came_refs[0].shape[0]
    for block in range(out_ref.shape[0]):
        put_coded(out_ref.at[block], kept_ref[block] + came_refs[block // half][block % half])


def add_given(kept, came):
    blocks, rows, width = kept.shape
    return pl.pallas_call(
        add_given_kernel,
        out_shape=jax.ShapeDtypeStruct((blocks, rows // 8 * 9, width), jnp.bfloat16),
        compiler_params=PARAMS,
    )(kept, *came)


def add_kept_kernel(kept_ref, came_ref, across_ref, *out_refs):
    for z, out_ref in enumerate(out_refs):
        def here(first, rows):
            return kept_ref[z, first : first + rows, :] + came_ref[z, first : first + rows, :]

        for rows, total in add_coded(here, across_ref.at[z]):
            out_ref[rows, :] = total.astype(out_ref.dtype)


def add_kept(kept, came, across, types):
    _, rows, width = kept.shape
    heights = [rows if z == 0 or dtype == jnp.bfloat16 else rows + NEAR_PAD for z, dtype in enumerate(types)]
    return pl.pallas_call(
        add_kept_kernel,
        out_shape=[jax.ShapeDtypeStruct((height, width), dtype) for height, dtype in zip(heights, types)],
        compiler_params=PARAMS,
    )(kept, came, across)


def stack_kernel(left_ref, right_ref, out_ref):
    out_ref[: left_ref.shape[0]] = left_ref[...]
    out_ref[left_ref.shape[0] :] = right_ref[...]


def stack(left, right):
    return pl.pallas_call(
        stack_kernel,
        out_shape=jax.ShapeDtypeStruct((2 * left.shape[0],) + left.shape[1:], left.dtype),
        compiler_params=PARAMS,
    )(left, right)


def add_scores(queries_ref, chips, place, grads, sums_ref):
    examples, half_rank, lanes = grads.shape
    held = queries_ref.shape[1]
    step = 4 if len(chips) % 4 == 0 else 2
    here = lax.div(lax.axis_index("ex"), 2)
    for first in range(0, len(chips), step):
        sums = [jnp.zeros((step * held, lanes), jnp.float32) for _ in range(examples)]
        for k in range(half_rank):
            query = queries_ref[first : first + step, :, k * lanes : (k + 1) * lanes].astype(jnp.float32)
            query = query.reshape(step * held, lanes)
            for n in range(examples):
                sums[n] = sums[n] + query * grads[n, k : k + 1, :]
        for part in range(step):
            source = lax.bitwise_xor(here, chips[first + part])
            for n in range(examples):
                sums_ref[n, source, place] = sums[n][part * held : (part + 1) * held, :]


def first_score_kernel(parts_count, held, *refs):
    part_refs, query_refs = refs[:parts_count], refs[parts_count : parts_count + len(held)]
    grads_ref, sums_ref, out_t_ref = refs[parts_count + len(held) :]
    rank, tokens = out_t_ref.shape
    core = lax.rem(lax.axis_index("ex"), 2)
    total = part_refs[0][...]
    for part_ref in part_refs[1:]:
        total = total + part_ref[: 2 * rank, :].astype(jnp.float32)
    out_t_ref[...] = total[rank:, :]
    even = out_t_ref[pl.ds(0, rank // 2, stride=2), :]
    odd = out_t_ref[pl.ds(1, rank // 2, stride=2), :]
    token = lax.broadcasted_iota(jnp.int32, (rank, tokens), 1)
    for n in range(tokens // SEQ):
        mine = jnp.where((token >= n * SEQ) & (token < (n + 1) * SEQ), total[:rank, :], 0.0)
        for side, rows in enumerate((even, odd)):
            grads_ref[n, :, side * rank : (side + 1) * rank] = lax.dot_general(
                rows, mine, LANES_BY_LANES, precision=lax.Precision.HIGHEST, preferred_element_type=jnp.float32
            )
    sums_ref[...] = jnp.zeros_like(sums_ref)
    for queries_ref, (other, chips) in zip(query_refs, held):
        add_scores(queries_ref, chips, lax.rem(core + other, 2), grads_ref, sums_ref)


def last_score_kernel(chips, grads_ref, before_ref, queries_ref, out_ref, sums_ref):
    core = lax.rem(lax.axis_index("ex"), 2)
    sums_ref[...] = before_ref[...]
    add_scores(queries_ref, chips, lax.rem(core + 1, 2), grads_ref, sums_ref)
    examples, *rows, lanes = sums_ref.shape
    sums = sums_ref[...].reshape(examples * out_ref.shape[1], lanes)
    high = sums.astype(jnp.bfloat16)
    low = (sums - high.astype(jnp.float32)).astype(jnp.bfloat16)
    ones = jnp.ones((16, lanes), jnp.bfloat16)
    row = sum(lax.dot_general(ones, part, LANES_BY_LANES, preferred_element_type=jnp.float32) for part in (high, low))
    for n in range(examples):
        out_ref[n : n + 1, :] = row[0:1, n * out_ref.shape[1] : (n + 1) * out_ref.shape[1]]


def first_scores(parts, queries, held, rank):
    tokens = parts[0].shape[1]
    examples = tokens // SEQ
    chips = 2 * queries[0].shape[0]
    return pl.pallas_call(
        functools.partial(first_score_kernel, len(parts), held),
        out_shape=[
            jax.ShapeDtypeStruct((examples, rank // 2, 2 * rank), jnp.float32),
            jax.ShapeDtypeStruct((examples, chips, 2, queries[0].shape[1], 2 * rank), jnp.float32),
        ],
        scratch_shapes=[pltpu.VMEM((rank, tokens), jnp.float32)],
        compiler_params=PARAMS,
    )(*parts, *queries)


def last_scores(grads, sums, queries, chips):
    examples, all_chips, cores, held, _ = sums.shape
    return pl.pallas_call(
        functools.partial(last_score_kernel, chips),
        out_shape=jax.ShapeDtypeStruct((examples, all_chips * cores * held), jnp.float32),
        scratch_shapes=[pltpu.VMEM(sums.shape, jnp.float32)],
        compiler_params=PARAMS,
    )(grads, sums, queries)


def shards(inputs, out_grads, proj_in, proj_out, queries):
    devices = lax.axis_size("ex")
    chips = devices // 2
    depth = chips // 2
    rank = proj_in.shape[1]
    together = lax.optimization_barrier

    def swap(array, chip=0, core=0):
        distance = 2 * chip + core
        return lax.ppermute(array, "ex", [(i, i ^ distance) for i in range(devices)])

    steps = [1 << bit for bit in reversed(range(chips.bit_length() - 1))]
    held, reach = queries[None], [0]
    came_held = swap(held, chip=steps[0])
    lows = project(inputs, out_grads, proj_in.T, proj_out.T, devices)
    *given_y, given, kept_y, kept = lows
    came_y = [swap(array, core=1) for array in given_y]
    came = swap(given, core=1)
    for last, step in zip(steps, steps[1:-1]):
        held, reach = stack(held, came_held), reach + [chip ^ last for chip in reach]
        came_held = swap(held, chip=step)
    across = swap(add_given(kept_y, came_y), chip=1)
    held, reach = stack(held, came_held), reach + [chip ^ steps[-2] for chip in reach]
    came_held = swap(held, chip=1)
    other_held = swap(held, core=1)
    across, came = together((across, came))

    types = [jnp.float32 if z < depth // 2 else jnp.bfloat16 for z in range(depth)]
    parts = list(add_kept(kept, came, across, types))
    for z in list(range(depth // 2, depth)) + list(range(1, depth // 2)):
        parts[z] = swap(parts[z], chip=2 * z)
    came_held, other_held, parts = together((came_held, other_held, parts))
    other_came = swap(came_held, core=1)
    reach_y = [chip ^ 1 for chip in reach]
    held = [held, other_held, came_held]
    grads, scores = first_scores(parts, held, [(0, reach), (1, reach), (0, reach_y)], rank)
    return last_scores(grads, scores, other_came, reach_y)


def solution(mesh):
    return jax.shard_map(
        shards,
        mesh=mesh,
        in_specs=(
            P("ex", "groups"),
            P("ex", "groups"),
            P("ex", None),
            P("ex", None),
            P("ex", None),
        ),
        out_specs=P(("groups", "ex"), None),
        check_vma=False,
    )
```

```python
import functools

import jax
import jax.numpy as jnp
from jax import lax
from jax.experimental import pallas as pl
from jax.experimental.pallas import tpu as pltpu
from jax.sharding import PartitionSpec as P

SEQ = 64
VMEM_BYTES = 32 * 1024 * 1024
LOADED_ROWS = 128
LEFT_OVER = 0.36 * 2.0**-8
LANES_BY_LANES = (((1,), (1,)), ((), ()))
HBM_SPEC = pl.BlockSpec(memory_space=pltpu.HBM)
VMEM_SPEC = pl.BlockSpec(memory_space=pltpu.VMEM)
PARAMS = pltpu.CompilerParams(vmem_limit_bytes=VMEM_BYTES)


def project_loaded_kernel(x_hbm, w_hbm, p_in_hbm, p_out_hbm, low_in_ref, low_out_ref, x_buf, w_buf, p_in, p_out, sems, p_sems):
    matrices = [
        pltpu.make_async_copy(p_in_hbm, p_in, p_sems.at[0]),
        pltpu.make_async_copy(p_out_hbm.at[:, pl.ds(0, p_out.shape[1])], p_out, p_sems.at[1]),
    ]
    chunks = []
    for hbm, buf, matrix, low_ref in ((x_hbm, x_buf, p_in, low_in_ref), (w_hbm, w_buf, p_out, low_out_ref)):
        count = buf.shape[0] // LOADED_ROWS if buf.shape[0] % LOADED_ROWS == 0 else 1
        for chunk in range(count):
            part = pl.ds(chunk * (buf.shape[0] // count), buf.shape[0] // count)
            copy = pltpu.make_async_copy(hbm.at[part, :], buf.at[part, :], sems.at[len(chunks)])
            chunks.append((part, buf, matrix, low_ref, copy, chunk == 0))
    for copy in matrices + [chunk[4] for chunk in chunks]:
        copy.start()
    for copy in matrices:
        copy.wait()
    step = min(1024, low_in_ref.shape[1])
    for part, buf, matrix, low_ref, copy, first in chunks:
        copy.wait()
        for column in range(0, low_ref.shape[1], step):
            columns = slice(column, column + step)
            product = jnp.dot(matrix[:, part], buf[part, columns], preferred_element_type=jnp.float32)
            low_ref[:, columns] = product if first else low_ref[:, columns] + product


def project_loaded(inputs, out_grads, proj_in_t, proj_out_t, rows):
    arrays = [pltpu.with_memory_space_constraint(a, pltpu.HBM) for a in (inputs, out_grads, proj_in_t, proj_out_t)]
    rank, tokens = proj_in_t.shape[0], inputs.shape[1]
    chunks = sum(a // LOADED_ROWS if a % LOADED_ROWS == 0 else 1 for a in (inputs.shape[0], rows))
    return pl.pallas_call(
        project_loaded_kernel,
        out_shape=[jax.ShapeDtypeStruct((rank, tokens), jnp.float32)] * 2,
        in_specs=[HBM_SPEC] * 4,
        out_specs=[VMEM_SPEC] * 2,
        scratch_shapes=[
            pltpu.VMEM(inputs.shape, jnp.bfloat16),
            pltpu.VMEM((rows, tokens), jnp.bfloat16),
            pltpu.VMEM(proj_in_t.shape, jnp.bfloat16),
            pltpu.VMEM((rank, max(rows, 128)), jnp.bfloat16),
            pltpu.SemaphoreType.DMA((chunks,)),
            pltpu.SemaphoreType.DMA((2,)),
        ],
        compiler_params=PARAMS,
        cost_estimate=pl.CostEstimate(
            flops=2 * rank * (inputs.shape[0] + rows) * tokens,
            bytes_accessed=2 * (inputs.shape[0] + rows) * tokens,
            transcendentals=0,
        ),
    )(*arrays)


def project_kernel(done, low_in_ref, low_out_ref, p_ref, w_ref, *refs):
    *given, kept_y, kept_here = refs
    given_y, given_here = given[:-1], given[-1:]
    here = lax.axis_index("ex")
    core, chip = lax.rem(here, 2), lax.div(here, 2)
    depth = kept_y.shape[0]
    rank, width = kept_y.shape[1] // 2, kept_y.shape[2]
    for flip, given_refs, kept_ref in ((1, given_y, kept_y), (0, given_here, kept_here)):
        for z in range(depth):
            place = lax.bitwise_xor(chip, 2 * z + flip)
            columns = pl.ds(pl.multiple_of(place * 2 * width, 2 * width), 2 * width)
            low_out = jnp.dot(p_ref[:, done:], w_ref[done:, columns], preferred_element_type=jnp.float32)
            low_out = low_out + low_out_ref[:, columns]
            given_ref = given_refs[z * len(given_refs) // depth]
            for lines, low in ((slice(0, rank), low_in_ref[:, columns]), (slice(rank, 2 * rank), low_out)):
                left, right = low[:, :width], low[:, width:]
                given_ref[z % given_ref.shape[0], lines, :] = jnp.where(core == 0, right, left)
                kept_ref[z, lines, :] = jnp.where(core == 0, left, right)


def project(inputs, out_grads, proj_in_t, proj_out_t, devices):
    rank, width = proj_in_t.shape[0], inputs.shape[1] // devices
    units = out_grads.shape[0]
    rows = LOADED_ROWS if units % LOADED_ROWS == 0 else 16
    lows = project_loaded(inputs, out_grads, proj_in_t, proj_out_t, rows)
    low = jax.ShapeDtypeStruct((devices // 4, 2 * rank, width), jnp.float32)
    half = jax.ShapeDtypeStruct((devices // 8, 2 * rank, width), jnp.float32)
    return pl.pallas_call(
        functools.partial(project_kernel, rows),
        out_shape=[half] * 2 + [low] * 3,
        in_specs=[VMEM_SPEC] * 4,
        out_specs=[VMEM_SPEC] * 5,
        compiler_params=PARAMS,
        cost_estimate=pl.CostEstimate(
            flops=2 * rank * out_grads.size, bytes_accessed=2 * out_grads.size, transcendentals=0
        ),
    )(*lows, proj_out_t, out_grads)


def put_coded(out_ref, low):
    rows = low.shape[0]
    rounded = low.astype(jnp.bfloat16)
    out_ref[:rows, :] = rounded
    above = jnp.where(low > rounded.astype(jnp.float32), 1.0, 0.0)
    part = rows // 8
    word = above[:part, :]
    for index in range(1, 8):
        word = word + 2.0**index * above[index * part : (index + 1) * part, :]
    out_ref[rows:, :] = word.astype(jnp.bfloat16)


def add_coded(total, ref):
    part = ref.shape[0] // 9
    word = ref[8 * part :, :].astype(jnp.float32)
    parts = []
    for index in reversed(range(8)):
        above = jnp.floor(word * 0.5**index)
        word = word - above * 2.0**index
        rounded = ref[index * part : (index + 1) * part, :].astype(jnp.float32)
        left = jnp.abs(rounded) * ((2.0 * LEFT_OVER) * above - LEFT_OVER)
        parts.append((slice(index * part, (index + 1) * part), total(index * part, part) + rounded + left))
    return parts


def add_given_kernel(kept_ref, *refs):
    *came_refs, out_ref = refs
    half = came_refs[0].shape[0]
    for block in range(out_ref.shape[0]):
        put_coded(out_ref.at[block], kept_ref[block] + came_refs[block // half][block % half])


def add_given(kept, came):
    blocks, rows, width = kept.shape
    return pl.pallas_call(
        add_given_kernel,
        out_shape=jax.ShapeDtypeStruct((blocks, rows // 8 * 9, width), jnp.bfloat16),
        compiler_params=PARAMS,
    )(kept, *came)


def add_kept_kernel(kept_ref, came_ref, across_ref, *out_refs):
    for z, out_ref in enumerate(out_refs):
        def here(first, rows):
            return kept_ref[z, first : first + rows, :] + came_ref[z, first : first + rows, :]

        for rows, total in add_coded(here, across_ref.at[z]):
            out_ref[rows, :] = total.astype(out_ref.dtype)


def add_kept(kept, came, across, types):
    return pl.pallas_call(
        add_kept_kernel,
        out_shape=[jax.ShapeDtypeStruct(kept.shape[1:], dtype) for dtype in types],
        compiler_params=PARAMS,
    )(kept, came, across)


def stack_kernel(left_ref, right_ref, out_ref):
    out_ref[: left_ref.shape[0]] = left_ref[...]
    out_ref[left_ref.shape[0] :] = right_ref[...]


def stack(left, right):
    return pl.pallas_call(
        stack_kernel,
        out_shape=jax.ShapeDtypeStruct((2 * left.shape[0],) + left.shape[1:], left.dtype),
        compiler_params=PARAMS,
    )(left, right)


def add_scores(queries_ref, chips, place, grads, sums_ref):
    examples, half_rank, lanes = grads.shape
    held = queries_ref.shape[1]
    step = 4 if len(chips) % 4 == 0 else 2
    here = lax.div(lax.axis_index("ex"), 2)
    for first in range(0, len(chips), step):
        sums = [jnp.zeros((step * held, lanes), jnp.float32) for _ in range(examples)]
        for k in range(half_rank):
            query = queries_ref[first : first + step, :, k * lanes : (k + 1) * lanes].astype(jnp.float32)
            query = query.reshape(step * held, lanes)
            for n in range(examples):
                sums[n] = sums[n] + query * grads[n, k : k + 1, :]
        for part in range(step):
            source = lax.bitwise_xor(here, chips[first + part])
            for n in range(examples):
                sums_ref[n, source, place] = sums[n][part * held : (part + 1) * held, :]


def first_score_kernel(parts_count, held, *refs):
    part_refs, query_refs = refs[:parts_count], refs[parts_count : parts_count + len(held)]
    grads_ref, sums_ref, out_t_ref = refs[parts_count + len(held) :]
    rank, tokens = out_t_ref.shape
    core = lax.rem(lax.axis_index("ex"), 2)
    total = part_refs[0][...]
    for part_ref in part_refs[1:]:
        total = total + part_ref[...].astype(jnp.float32)
    out_t_ref[...] = total[rank:, :]
    even = out_t_ref[pl.ds(0, rank // 2, stride=2), :]
    odd = out_t_ref[pl.ds(1, rank // 2, stride=2), :]
    token = lax.broadcasted_iota(jnp.int32, (rank, tokens), 1)
    for n in range(tokens // SEQ):
        mine = jnp.where((token >= n * SEQ) & (token < (n + 1) * SEQ), total[:rank, :], 0.0)
        for side, rows in enumerate((even, odd)):
            grads_ref[n, :, side * rank : (side + 1) * rank] = lax.dot_general(
                rows, mine, LANES_BY_LANES, precision=lax.Precision.HIGHEST, preferred_element_type=jnp.float32
            )
    sums_ref[...] = jnp.zeros_like(sums_ref)
    for queries_ref, (other, chips) in zip(query_refs, held):
        add_scores(queries_ref, chips, lax.rem(core + other, 2), grads_ref, sums_ref)


def last_score_kernel(chips, grads_ref, before_ref, queries_ref, out_ref, sums_ref):
    core = lax.rem(lax.axis_index("ex"), 2)
    sums_ref[...] = before_ref[...]
    add_scores(queries_ref, chips, lax.rem(core + 1, 2), grads_ref, sums_ref)
    examples, *rows, lanes = sums_ref.shape
    sums = sums_ref[...].reshape(examples * out_ref.shape[1], lanes)
    high = sums.astype(jnp.bfloat16)
    low = (sums - high.astype(jnp.float32)).astype(jnp.bfloat16)
    ones = jnp.ones((16, lanes), jnp.bfloat16)
    row = sum(lax.dot_general(ones, part, LANES_BY_LANES, preferred_element_type=jnp.float32) for part in (high, low))
    for n in range(examples):
        out_ref[n : n + 1, :] = row[0:1, n * out_ref.shape[1] : (n + 1) * out_ref.shape[1]]


def first_scores(parts, queries, held, rank):
    tokens = parts[0].shape[1]
    examples = tokens // SEQ
    chips = 2 * queries[0].shape[0]
    return pl.pallas_call(
        functools.partial(first_score_kernel, len(parts), held),
        out_shape=[
            jax.ShapeDtypeStruct((examples, rank // 2, 2 * rank), jnp.float32),
            jax.ShapeDtypeStruct((examples, chips, 2, queries[0].shape[1], 2 * rank), jnp.float32),
        ],
        scratch_shapes=[pltpu.VMEM((rank, tokens), jnp.float32)],
        compiler_params=PARAMS,
    )(*parts, *queries)


def last_scores(grads, sums, queries, chips):
    examples, all_chips, cores, held, _ = sums.shape
    return pl.pallas_call(
        functools.partial(last_score_kernel, chips),
        out_shape=jax.ShapeDtypeStruct((examples, all_chips * cores * held), jnp.float32),
        scratch_shapes=[pltpu.VMEM(sums.shape, jnp.float32)],
        compiler_params=PARAMS,
    )(grads, sums, queries)


def shards(inputs, out_grads, proj_in, proj_out, queries):
    devices = lax.axis_size("ex")
    chips = devices // 2
    depth = chips // 2
    rank = proj_in.shape[1]
    together = lax.optimization_barrier

    def swap(array, chip=0, core=0):
        distance = 2 * chip + core
        return lax.ppermute(array, "ex", [(i, i ^ distance) for i in range(devices)])

    steps = [1 << bit for bit in reversed(range(chips.bit_length() - 1))]
    held, reach = queries[None], [0]
    came_held = swap(held, chip=steps[0])
    lows = project(inputs, out_grads, proj_in.T, proj_out.T, devices)
    *given_y, given, kept_y, kept = lows
    came_y = [swap(array, core=1) for array in given_y]
    came = swap(given, core=1)
    for last, step in zip(steps, steps[1:-1]):
        held, reach = stack(held, came_held), reach + [chip ^ last for chip in reach]
        came_held = swap(held, chip=step)
    across = swap(add_given(kept_y, came_y), chip=1)
    early, early_reach = held, reach
    late, late_reach = came_held, [chip ^ steps[-2] for chip in reach]
    held, reach = stack(early, late), early_reach + late_reach
    came_held = swap(held, chip=1)
    other_early = swap(early, core=1)
    across, came, other_early = together((across, came, other_early))

    types = [jnp.float32 if z < depth // 2 else jnp.bfloat16 for z in range(depth)]
    parts = list(add_kept(kept, came, across, types))
    late, parts = together((late, parts))
    other_late = swap(late, core=1)
    for z in list(range(depth // 2, depth)) + list(range(1, depth // 2)):
        parts[z] = swap(parts[z], chip=2 * z)
    came_held, other_late, parts = together((came_held, other_late, parts))
    other_came = swap(came_held, core=1)
    reach_y = [chip ^ 1 for chip in reach]
    queries = [held, other_early, other_late, came_held]
    reaches = [(0, reach), (1, early_reach), (1, late_reach), (0, reach_y)]
    grads, scores = first_scores(parts, queries, reaches, rank)
    return last_scores(grads, scores, other_came, reach_y)


def solution(mesh):
    return jax.shard_map(
        shards,
        mesh=mesh,
        in_specs=(
            P("ex", "groups"),
            P("ex", "groups"),
            P("ex", None),
            P("ex", None),
            P("ex", None),
        ),
        out_specs=P(("groups", "ex"), None),
        check_vma=False,
    )
```

```python
import functools

import jax
import jax.numpy as jnp
from jax import lax
from jax.experimental import pallas as pl
from jax.experimental.pallas import tpu as pltpu
from jax.sharding import PartitionSpec as P

SEQ = 64
VMEM_BYTES = 32 * 1024 * 1024
LOADED_ROWS = 128
LEFT_OVER = 0.36 * 2.0**-8
LANES_BY_LANES = (((1,), (1,)), ((), ()))
HBM_SPEC = pl.BlockSpec(memory_space=pltpu.HBM)
VMEM_SPEC = pl.BlockSpec(memory_space=pltpu.VMEM)
PARAMS = pltpu.CompilerParams(vmem_limit_bytes=VMEM_BYTES)


def project_loaded_kernel(x_hbm, w_hbm, p_in_hbm, p_out_hbm, low_in_ref, low_out_ref, x_buf, w_buf, p_in, p_out, sems, p_sems):
    matrices = [
        pltpu.make_async_copy(p_in_hbm, p_in, p_sems.at[0]),
        pltpu.make_async_copy(p_out_hbm.at[:, pl.ds(0, p_out.shape[1])], p_out, p_sems.at[1]),
    ]
    chunks = []
    for hbm, buf, matrix, low_ref in ((x_hbm, x_buf, p_in, low_in_ref), (w_hbm, w_buf, p_out, low_out_ref)):
        count = buf.shape[0] // LOADED_ROWS if buf.shape[0] % LOADED_ROWS == 0 else 1
        for chunk in range(count):
            part = pl.ds(chunk * (buf.shape[0] // count), buf.shape[0] // count)
            copy = pltpu.make_async_copy(hbm.at[part, :], buf.at[part, :], sems.at[len(chunks)])
            chunks.append((part, buf, matrix, low_ref, copy, chunk == 0))
    for copy in matrices + [chunk[4] for chunk in chunks]:
        copy.start()
    for copy in matrices:
        copy.wait()
    step = min(1024, low_in_ref.shape[1])
    for part, buf, matrix, low_ref, copy, first in chunks:
        copy.wait()
        for column in range(0, low_ref.shape[1], step):
            columns = slice(column, column + step)
            product = jnp.dot(matrix[:, part], buf[part, columns], preferred_element_type=jnp.float32)
            low_ref[:, columns] = product if first else low_ref[:, columns] + product


def project_loaded(inputs, out_grads, proj_in_t, proj_out_t, rows):
    arrays = [pltpu.with_memory_space_constraint(a, pltpu.HBM) for a in (inputs, out_grads, proj_in_t, proj_out_t)]
    rank, tokens = proj_in_t.shape[0], inputs.shape[1]
    chunks = sum(a // LOADED_ROWS if a % LOADED_ROWS == 0 else 1 for a in (inputs.shape[0], rows))
    return pl.pallas_call(
        project_loaded_kernel,
        out_shape=[jax.ShapeDtypeStruct((rank, tokens), jnp.float32)] * 2,
        in_specs=[HBM_SPEC] * 4,
        out_specs=[VMEM_SPEC] * 2,
        scratch_shapes=[
            pltpu.VMEM(inputs.shape, jnp.bfloat16),
            pltpu.VMEM((rows, tokens), jnp.bfloat16),
            pltpu.VMEM(proj_in_t.shape, jnp.bfloat16),
            pltpu.VMEM((rank, max(rows, 128)), jnp.bfloat16),
            pltpu.SemaphoreType.DMA((chunks,)),
            pltpu.SemaphoreType.DMA((2,)),
        ],
        compiler_params=PARAMS,
        cost_estimate=pl.CostEstimate(
            flops=2 * rank * (inputs.shape[0] + rows) * tokens,
            bytes_accessed=2 * (inputs.shape[0] + rows) * tokens,
            transcendentals=0,
        ),
    )(*arrays)


def project_kernel(done, low_in_ref, low_out_ref, p_ref, w_ref, *refs):
    *given, kept_y, kept_here = refs
    given_y, given_here = given[:-1], given[-1:]
    here = lax.axis_index("ex")
    core, chip = lax.rem(here, 2), lax.div(here, 2)
    depth = kept_y.shape[0]
    rank, width = kept_y.shape[1] // 2, kept_y.shape[2]
    for flip, given_refs, kept_ref in ((1, given_y, kept_y), (0, given_here, kept_here)):
        for z in range(depth):
            place = lax.bitwise_xor(chip, 2 * z + flip)
            columns = pl.ds(pl.multiple_of(place * 2 * width, 2 * width), 2 * width)
            low_out = jnp.dot(p_ref[:, done:], w_ref[done:, columns], preferred_element_type=jnp.float32)
            low_out = low_out + low_out_ref[:, columns]
            given_ref = given_refs[z * len(given_refs) // depth]
            for lines, low in ((slice(0, rank), low_in_ref[:, columns]), (slice(rank, 2 * rank), low_out)):
                left, right = low[:, :width], low[:, width:]
                given_ref[z % given_ref.shape[0], lines, :] = jnp.where(core == 0, right, left)
                kept_ref[z, lines, :] = jnp.where(core == 0, left, right)


def project(inputs, out_grads, proj_in_t, proj_out_t, devices):
    rank, width = proj_in_t.shape[0], inputs.shape[1] // devices
    units = out_grads.shape[0]
    rows = LOADED_ROWS if units % LOADED_ROWS == 0 else 16
    lows = project_loaded(inputs, out_grads, proj_in_t, proj_out_t, rows)
    low = jax.ShapeDtypeStruct((devices // 4, 2 * rank, width), jnp.float32)
    half = jax.ShapeDtypeStruct((devices // 8, 2 * rank, width), jnp.float32)
    return pl.pallas_call(
        functools.partial(project_kernel, rows),
        out_shape=[half] * 2 + [low] * 3,
        in_specs=[VMEM_SPEC] * 4,
        out_specs=[VMEM_SPEC] * 5,
        compiler_params=PARAMS,
        cost_estimate=pl.CostEstimate(
            flops=2 * rank * out_grads.size, bytes_accessed=2 * out_grads.size, transcendentals=0
        ),
    )(*lows, proj_out_t, out_grads)


def put_coded(out_ref, low):
    rows = low.shape[0]
    rounded = low.astype(jnp.bfloat16)
    out_ref[:rows, :] = rounded
    above = jnp.where(low > rounded.astype(jnp.float32), 1.0, 0.0)
    part = rows // 8
    word = above[:part, :]
    for index in range(1, 8):
        word = word + 2.0**index * above[index * part : (index + 1) * part, :]
    out_ref[rows:, :] = word.astype(jnp.bfloat16)


def add_coded(total, ref):
    part = ref.shape[0] // 9
    word = ref[8 * part :, :].astype(jnp.float32)
    parts = []
    for index in reversed(range(8)):
        above = jnp.floor(word * 0.5**index)
        word = word - above * 2.0**index
        rounded = ref[index * part : (index + 1) * part, :].astype(jnp.float32)
        left = jnp.abs(rounded) * ((2.0 * LEFT_OVER) * above - LEFT_OVER)
        parts.append((slice(index * part, (index + 1) * part), total(index * part, part) + rounded + left))
    return parts


def add_given_kernel(kept_ref, *refs):
    *came_refs, out_ref = refs
    half = came_refs[0].shape[0]
    for block in range(out_ref.shape[0]):
        put_coded(out_ref.at[block], kept_ref[block] + came_refs[block // half][block % half])


def add_given(kept, came):
    blocks, rows, width = kept.shape
    return pl.pallas_call(
        add_given_kernel,
        out_shape=jax.ShapeDtypeStruct((blocks, rows // 8 * 9, width), jnp.bfloat16),
        compiler_params=PARAMS,
    )(kept, *came)


def add_kept_kernel(kept_ref, came_ref, across_ref, *out_refs):
    for z, out_ref in enumerate(out_refs):
        def here(first, rows):
            return kept_ref[z, first : first + rows, :] + came_ref[z, first : first + rows, :]

        sums = add_coded(here, across_ref.at[z])
        if out_ref.shape[0] != kept_ref.shape[1]:
            put_coded(out_ref, jnp.concatenate([total for _, total in reversed(sums)], axis=0))
            continue
        for rows, total in sums:
            out_ref[rows, :] = total.astype(out_ref.dtype)


def add_kept(kept, came, across):
    depth, rows, width = kept.shape
    own = jax.ShapeDtypeStruct((rows, width), jnp.float32)
    near = jax.ShapeDtypeStruct((rows // 8 * 9, width), jnp.bfloat16)
    far = jax.ShapeDtypeStruct((rows, width), jnp.bfloat16)
    return pl.pallas_call(
        add_kept_kernel,
        out_shape=[own] + [near] * (depth // 2 - 1) + [far] * (depth // 2),
        compiler_params=PARAMS,
    )(kept, came, across)


def stack_kernel(left_ref, right_ref, out_ref):
    out_ref[: left_ref.shape[0]] = left_ref[...]
    out_ref[left_ref.shape[0] :] = right_ref[...]


def stack(left, right):
    return pl.pallas_call(
        stack_kernel,
        out_shape=jax.ShapeDtypeStruct((2 * left.shape[0],) + left.shape[1:], left.dtype),
        compiler_params=PARAMS,
    )(left, right)


def add_scores(queries_ref, chips, place, grads, sums_ref):
    examples, half_rank, lanes = grads.shape
    held = queries_ref.shape[1]
    step = 4 if len(chips) % 4 == 0 else 2
    here = lax.div(lax.axis_index("ex"), 2)
    for first in range(0, len(chips), step):
        sums = [jnp.zeros((step * held, lanes), jnp.float32) for _ in range(examples)]
        for k in range(half_rank):
            query = queries_ref[first : first + step, :, k * lanes : (k + 1) * lanes].astype(jnp.float32)
            query = query.reshape(step * held, lanes)
            for n in range(examples):
                sums[n] = sums[n] + query * grads[n, k : k + 1, :]
        for part in range(step):
            source = lax.bitwise_xor(here, chips[first + part])
            for n in range(examples):
                sums_ref[n, source, place] = sums[n][part * held : (part + 1) * held, :]


def first_score_kernel(parts_count, held, *refs):
    part_refs, query_refs = refs[:parts_count], refs[parts_count : parts_count + len(held)]
    grads_ref, sums_ref, total_ref = refs[parts_count + len(held) :]
    rank, tokens = total_ref.shape[0] // 2, total_ref.shape[1]
    core = lax.rem(lax.axis_index("ex"), 2)
    total_ref[...] = part_refs[0][...]
    for part_ref in part_refs[1:]:
        if part_ref.shape[0] == 2 * rank:
            total_ref[...] += part_ref[...].astype(jnp.float32)
        else:
            for rows, total in add_coded(lambda first, count: total_ref[first : first + count, :], part_ref):
                total_ref[rows, :] = total
    even = total_ref[pl.ds(rank, rank // 2, stride=2), :]
    odd = total_ref[pl.ds(rank + 1, rank // 2, stride=2), :]
    token = lax.broadcasted_iota(jnp.int32, (rank, tokens), 1)
    for n in range(tokens // SEQ):
        mine = jnp.where((token >= n * SEQ) & (token < (n + 1) * SEQ), total_ref[:rank, :], 0.0)
        for side, rows in enumerate((even, odd)):
            grads_ref[n, :, side * rank : (side + 1) * rank] = lax.dot_general(
                rows, mine, LANES_BY_LANES, precision=lax.Precision.HIGHEST, preferred_element_type=jnp.float32
            )
    sums_ref[...] = jnp.zeros_like(sums_ref)
    for queries_ref, (other, chips) in zip(query_refs, held):
        add_scores(queries_ref, chips, lax.rem(core + other, 2), grads_ref, sums_ref)


def last_score_kernel(chips, grads_ref, before_ref, queries_ref, out_ref, sums_ref):
    core = lax.rem(lax.axis_index("ex"), 2)
    sums_ref[...] = before_ref[...]
    add_scores(queries_ref, chips, lax.rem(core + 1, 2), grads_ref, sums_ref)
    examples, *rows, lanes = sums_ref.shape
    sums = sums_ref[...].reshape(examples * out_ref.shape[1], lanes)
    high = sums.astype(jnp.bfloat16)
    low = (sums - high.astype(jnp.float32)).astype(jnp.bfloat16)
    ones = jnp.ones((16, lanes), jnp.bfloat16)
    row = sum(lax.dot_general(ones, part, LANES_BY_LANES, preferred_element_type=jnp.float32) for part in (high, low))
    for n in range(examples):
        out_ref[n : n + 1, :] = row[0:1, n * out_ref.shape[1] : (n + 1) * out_ref.shape[1]]


def first_scores(parts, queries, held, rank):
    tokens = parts[0].shape[1]
    examples = tokens // SEQ
    chips = 2 * queries[0].shape[0]
    return pl.pallas_call(
        functools.partial(first_score_kernel, len(parts), held),
        out_shape=[
            jax.ShapeDtypeStruct((examples, rank // 2, 2 * rank), jnp.float32),
            jax.ShapeDtypeStruct((examples, chips, 2, queries[0].shape[1], 2 * rank), jnp.float32),
        ],
        scratch_shapes=[pltpu.VMEM((2 * rank, tokens), jnp.float32)],
        compiler_params=PARAMS,
    )(*parts, *queries)


def last_scores(grads, sums, queries, chips):
    examples, all_chips, cores, held, _ = sums.shape
    return pl.pallas_call(
        functools.partial(last_score_kernel, chips),
        out_shape=jax.ShapeDtypeStruct((examples, all_chips * cores * held), jnp.float32),
        scratch_shapes=[pltpu.VMEM(sums.shape, jnp.float32)],
        compiler_params=PARAMS,
    )(grads, sums, queries)


def shards(inputs, out_grads, proj_in, proj_out, queries):
    devices = lax.axis_size("ex")
    chips = devices // 2
    depth = chips // 2
    rank = proj_in.shape[1]
    together = lax.optimization_barrier

    def swap(array, chip=0, core=0):
        distance = 2 * chip + core
        return lax.ppermute(array, "ex", [(i, i ^ distance) for i in range(devices)])

    steps = [1 << bit for bit in reversed(range(chips.bit_length() - 1))]
    held, reach = queries[None], [0]
    came_held = swap(held, chip=steps[0])
    lows = project(inputs, out_grads, proj_in.T, proj_out.T, devices)
    *given_y, given, kept_y, kept = lows
    came_y = [swap(array, core=1) for array in given_y]
    came = swap(given, core=1)
    for last, step in zip(steps, steps[1:-1]):
        held, reach = stack(held, came_held), reach + [chip ^ last for chip in reach]
        came_held = swap(held, chip=step)
    across = swap(add_given(kept_y, came_y), chip=1)
    early, early_reach = held, reach
    late, late_reach = came_held, [chip ^ steps[-2] for chip in reach]
    held, reach = stack(early, late), early_reach + late_reach
    came_held = swap(held, chip=1)
    other_early = swap(early, core=1)
    across, came, other_early = together((across, came, other_early))

    parts = list(add_kept(kept, came, across))
    late, parts = together((late, parts))
    other_late = swap(late, core=1)
    for z in list(range(depth // 2, depth)) + list(range(1, depth // 2)):
        parts[z] = swap(parts[z], chip=2 * z)
    came_held, other_late, parts = together((came_held, other_late, parts))
    other_came = swap(came_held, core=1)
    reach_y = [chip ^ 1 for chip in reach]
    queries = [held, other_early, other_late, came_held]
    reaches = [(0, reach), (1, early_reach), (1, late_reach), (0, reach_y)]
    grads, scores = first_scores(parts, queries, reaches, rank)
    return last_scores(grads, scores, other_came, reach_y)


def solution(mesh):
    return jax.shard_map(
        shards,
        mesh=mesh,
        in_specs=(
            P("ex", "groups"),
            P("ex", "groups"),
            P("ex", None),
            P("ex", None),
            P("ex", None),
        ),
        out_specs=P(("groups", "ex"), None),
        check_vma=False,
    )
```

```python
import functools

import jax
import jax.numpy as jnp
from jax import lax
from jax.experimental import pallas as pl
from jax.experimental.pallas import tpu as pltpu
from jax.sharding import PartitionSpec as P

SEQ = 64
VMEM_BYTES = 32 * 1024 * 1024
LOADED_ROWS = 128
LEFT_OVER = 0.36 * 2.0**-8
LANES_BY_LANES = (((1,), (1,)), ((), ()))
HBM_SPEC = pl.BlockSpec(memory_space=pltpu.HBM)
VMEM_SPEC = pl.BlockSpec(memory_space=pltpu.VMEM)
PARAMS = pltpu.CompilerParams(vmem_limit_bytes=VMEM_BYTES)


def project_loaded_kernel(x_hbm, w_hbm, p_in_hbm, p_out_hbm, low_in_ref, low_out_ref, x_buf, w_buf, p_in, p_out, sems, p_sems):
    matrices = [
        pltpu.make_async_copy(p_in_hbm, p_in, p_sems.at[0]),
        pltpu.make_async_copy(p_out_hbm.at[:, pl.ds(0, p_out.shape[1])], p_out, p_sems.at[1]),
    ]
    chunks = []
    for hbm, buf, matrix, low_ref in ((x_hbm, x_buf, p_in, low_in_ref), (w_hbm, w_buf, p_out, low_out_ref)):
        count = buf.shape[0] // LOADED_ROWS if buf.shape[0] % LOADED_ROWS == 0 else 1
        for chunk in range(count):
            part = pl.ds(chunk * (buf.shape[0] // count), buf.shape[0] // count)
            copy = pltpu.make_async_copy(hbm.at[part, :], buf.at[part, :], sems.at[len(chunks)])
            chunks.append((part, buf, matrix, low_ref, copy, chunk == 0))
    for copy in matrices + [chunk[4] for chunk in chunks]:
        copy.start()
    for copy in matrices:
        copy.wait()
    step = min(1024, low_in_ref.shape[1])
    for part, buf, matrix, low_ref, copy, first in chunks:
        copy.wait()
        for column in range(0, low_ref.shape[1], step):
            columns = slice(column, column + step)
            product = jnp.dot(matrix[:, part], buf[part, columns], preferred_element_type=jnp.float32)
            low_ref[:, columns] = product if first else low_ref[:, columns] + product


def project_loaded(inputs, out_grads, proj_in_t, proj_out_t, rows):
    arrays = [pltpu.with_memory_space_constraint(a, pltpu.HBM) for a in (inputs, out_grads, proj_in_t, proj_out_t)]
    rank, tokens = proj_in_t.shape[0], inputs.shape[1]
    chunks = sum(a // LOADED_ROWS if a % LOADED_ROWS == 0 else 1 for a in (inputs.shape[0], rows))
    return pl.pallas_call(
        project_loaded_kernel,
        out_shape=[jax.ShapeDtypeStruct((rank, tokens), jnp.float32)] * 2,
        in_specs=[HBM_SPEC] * 4,
        out_specs=[VMEM_SPEC] * 2,
        scratch_shapes=[
            pltpu.VMEM(inputs.shape, jnp.bfloat16),
            pltpu.VMEM((rows, tokens), jnp.bfloat16),
            pltpu.VMEM(proj_in_t.shape, jnp.bfloat16),
            pltpu.VMEM((rank, max(rows, 128)), jnp.bfloat16),
            pltpu.SemaphoreType.DMA((chunks,)),
            pltpu.SemaphoreType.DMA((2,)),
        ],
        compiler_params=PARAMS,
        cost_estimate=pl.CostEstimate(
            flops=2 * rank * (inputs.shape[0] + rows) * tokens,
            bytes_accessed=2 * (inputs.shape[0] + rows) * tokens,
            transcendentals=0,
        ),
    )(*arrays)


def project_kernel(done, low_in_ref, low_out_ref, p_ref, w_ref, *refs):
    *given, kept_y, kept_here = refs
    given_y, given_here = given[:-1], given[-1:]
    here = lax.axis_index("ex")
    core, chip = lax.rem(here, 2), lax.div(here, 2)
    depth = kept_y.shape[0]
    rank, width = kept_y.shape[1] // 2, kept_y.shape[2]
    for flip, given_refs, kept_ref in ((1, given_y, kept_y), (0, given_here, kept_here)):
        for z in range(depth):
            place = lax.bitwise_xor(chip, 2 * z + flip)
            columns = pl.ds(pl.multiple_of(place * 2 * width, 2 * width), 2 * width)
            low_out = jnp.dot(p_ref[:, done:], w_ref[done:, columns], preferred_element_type=jnp.float32)
            low_out = low_out + low_out_ref[:, columns]
            given_ref = given_refs[z * len(given_refs) // depth]
            for lines, low in ((slice(0, rank), low_in_ref[:, columns]), (slice(rank, 2 * rank), low_out)):
                left, right = low[:, :width], low[:, width:]
                given_ref[z % given_ref.shape[0], lines, :] = jnp.where(core == 0, right, left)
                kept_ref[z, lines, :] = jnp.where(core == 0, left, right)


def project(inputs, out_grads, proj_in_t, proj_out_t, devices):
    rank, width = proj_in_t.shape[0], inputs.shape[1] // devices
    units = out_grads.shape[0]
    rows = LOADED_ROWS if units % LOADED_ROWS == 0 else 16
    lows = project_loaded(inputs, out_grads, proj_in_t, proj_out_t, rows)
    low = jax.ShapeDtypeStruct((devices // 4, 2 * rank, width), jnp.float32)
    half = jax.ShapeDtypeStruct((devices // 8, 2 * rank, width), jnp.float32)
    return pl.pallas_call(
        functools.partial(project_kernel, rows),
        out_shape=[half] * 2 + [low] * 3,
        in_specs=[VMEM_SPEC] * 4,
        out_specs=[VMEM_SPEC] * 5,
        compiler_params=PARAMS,
        cost_estimate=pl.CostEstimate(
            flops=2 * rank * out_grads.size, bytes_accessed=2 * out_grads.size, transcendentals=0
        ),
    )(*lows, proj_out_t, out_grads)


def put_coded(out_ref, low):
    rows = low.shape[0]
    rounded = low.astype(jnp.bfloat16)
    out_ref[:rows, :] = rounded
    above = jnp.where(low > rounded.astype(jnp.float32), 1.0, 0.0)
    part = rows // 8
    word = above[:part, :]
    for index in range(1, 8):
        word = word + 2.0**index * above[index * part : (index + 1) * part, :]
    out_ref[rows:, :] = word.astype(jnp.bfloat16)


def add_coded(total, ref):
    part = ref.shape[0] // 9
    word = ref[8 * part :, :].astype(jnp.float32)
    parts = []
    for index in reversed(range(8)):
        above = jnp.floor(word * 0.5**index)
        word = word - above * 2.0**index
        rounded = ref[index * part : (index + 1) * part, :].astype(jnp.float32)
        left = jnp.abs(rounded) * ((2.0 * LEFT_OVER) * above - LEFT_OVER)
        parts.append((slice(index * part, (index + 1) * part), total(index * part, part) + rounded + left))
    return parts


def add_given_kernel(kept_ref, *refs):
    *came_refs, out_ref = refs
    half = came_refs[0].shape[0]
    for block in range(out_ref.shape[0]):
        put_coded(out_ref.at[block], kept_ref[block] + came_refs[block // half][block % half])


def add_given(kept, came):
    blocks, rows, width = kept.shape
    return pl.pallas_call(
        add_given_kernel,
        out_shape=jax.ShapeDtypeStruct((blocks, rows // 8 * 9, width), jnp.bfloat16),
        compiler_params=PARAMS,
    )(kept, *came)


def add_kept_kernel(kept_ref, came_ref, across_ref, own_ref, *out_refs):
    for z in range(len(out_refs) + 1):
        def here(first, rows):
            return kept_ref[z, first : first + rows, :] + came_ref[z, first : first + rows, :]

        sums = add_coded(here, across_ref.at[z])
        if z == 0:
            for rows, total in sums:
                own_ref[rows, :] = total
        else:
            put_coded(out_refs[len(out_refs) - z], jnp.concatenate([total for _, total in reversed(sums)], axis=0))


def add_kept(kept, came, across):
    depth, rows, width = kept.shape
    own = jax.ShapeDtypeStruct((rows, width), jnp.float32)
    coded = jax.ShapeDtypeStruct((rows // 8 * 9, width), jnp.bfloat16)
    return pl.pallas_call(
        add_kept_kernel,
        out_shape=[own] + [coded] * (depth - 1),
        compiler_params=PARAMS,
    )(kept, came, across)


def stack_kernel(left_ref, right_ref, out_ref):
    out_ref[: left_ref.shape[0]] = left_ref[...]
    out_ref[left_ref.shape[0] :] = right_ref[...]


def stack(left, right):
    return pl.pallas_call(
        stack_kernel,
        out_shape=jax.ShapeDtypeStruct((2 * left.shape[0],) + left.shape[1:], left.dtype),
        compiler_params=PARAMS,
    )(left, right)


def add_scores(queries_ref, chips, place, grads, sums_ref):
    examples, half_rank, lanes = grads.shape
    held = queries_ref.shape[1]
    step = 4 if len(chips) % 4 == 0 else 2
    here = lax.div(lax.axis_index("ex"), 2)
    for first in range(0, len(chips), step):
        sums = [jnp.zeros((step * held, lanes), jnp.float32) for _ in range(examples)]
        for k in range(half_rank):
            query = queries_ref[first : first + step, :, k * lanes : (k + 1) * lanes].astype(jnp.float32)
            query = query.reshape(step * held, lanes)
            for n in range(examples):
                sums[n] = sums[n] + query * grads[n, k : k + 1, :]
        for part in range(step):
            source = lax.bitwise_xor(here, chips[first + part])
            for n in range(examples):
                sums_ref[n, source, place] = sums[n][part * held : (part + 1) * held, :]


def first_score_kernel(parts_count, held, *refs):
    part_refs, query_refs = refs[:parts_count], refs[parts_count : parts_count + len(held)]
    grads_ref, sums_ref, total_ref = refs[parts_count + len(held) :]
    rank, tokens = total_ref.shape[0] // 2, total_ref.shape[1]
    core = lax.rem(lax.axis_index("ex"), 2)
    total_ref[...] = part_refs[0][...]
    for part_ref in part_refs[1:]:
        for rows, total in add_coded(lambda first, count: total_ref[first : first + count, :], part_ref):
            total_ref[rows, :] = total
    even = total_ref[pl.ds(rank, rank // 2, stride=2), :]
    odd = total_ref[pl.ds(rank + 1, rank // 2, stride=2), :]
    token = lax.broadcasted_iota(jnp.int32, (rank, tokens), 1)
    for n in range(tokens // SEQ):
        mine = jnp.where((token >= n * SEQ) & (token < (n + 1) * SEQ), total_ref[:rank, :], 0.0)
        for side, rows in enumerate((even, odd)):
            grads_ref[n, :, side * rank : (side + 1) * rank] = lax.dot_general(
                rows, mine, LANES_BY_LANES, precision=lax.Precision.HIGHEST, preferred_element_type=jnp.float32
            )
    sums_ref[...] = jnp.zeros_like(sums_ref)
    for queries_ref, (other, chips) in zip(query_refs, held):
        add_scores(queries_ref, chips, lax.rem(core + other, 2), grads_ref, sums_ref)


def last_score_kernel(chips, grads_ref, before_ref, queries_ref, out_ref, sums_ref):
    core = lax.rem(lax.axis_index("ex"), 2)
    sums_ref[...] = before_ref[...]
    add_scores(queries_ref, chips, lax.rem(core + 1, 2), grads_ref, sums_ref)
    examples, *rows, lanes = sums_ref.shape
    sums = sums_ref[...].reshape(examples * out_ref.shape[1], lanes)
    high = sums.astype(jnp.bfloat16)
    low = (sums - high.astype(jnp.float32)).astype(jnp.bfloat16)
    ones = jnp.ones((16, lanes), jnp.bfloat16)
    row = sum(lax.dot_general(ones, part, LANES_BY_LANES, preferred_element_type=jnp.float32) for part in (high, low))
    for n in range(examples):
        out_ref[n : n + 1, :] = row[0:1, n * out_ref.shape[1] : (n + 1) * out_ref.shape[1]]


def first_scores(parts, queries, held, rank):
    tokens = parts[0].shape[1]
    examples = tokens // SEQ
    chips = 2 * queries[0].shape[0]
    return pl.pallas_call(
        functools.partial(first_score_kernel, len(parts), held),
        out_shape=[
            jax.ShapeDtypeStruct((examples, rank // 2, 2 * rank), jnp.float32),
            jax.ShapeDtypeStruct((examples, chips, 2, queries[0].shape[1], 2 * rank), jnp.float32),
        ],
        scratch_shapes=[pltpu.VMEM((2 * rank, tokens), jnp.float32)],
        compiler_params=PARAMS,
    )(*parts, *queries)


def last_scores(grads, sums, queries, chips):
    examples, all_chips, cores, held, _ = sums.shape
    return pl.pallas_call(
        functools.partial(last_score_kernel, chips),
        out_shape=jax.ShapeDtypeStruct((examples, all_chips * cores * held), jnp.float32),
        scratch_shapes=[pltpu.VMEM(sums.shape, jnp.float32)],
        compiler_params=PARAMS,
    )(grads, sums, queries)


def shards(inputs, out_grads, proj_in, proj_out, queries):
    devices = lax.axis_size("ex")
    chips = devices // 2
    depth = chips // 2
    rank = proj_in.shape[1]
    together = lax.optimization_barrier

    def swap(array, chip=0, core=0):
        distance = 2 * chip + core
        return lax.ppermute(array, "ex", [(i, i ^ distance) for i in range(devices)])

    steps = [1 << bit for bit in reversed(range(chips.bit_length() - 1))]
    held, reach = queries[None], [0]
    came_held = swap(held, chip=steps[0])
    lows = project(inputs, out_grads, proj_in.T, proj_out.T, devices)
    *given_y, given, kept_y, kept = lows
    came_y = [swap(array, core=1) for array in given_y]
    came = swap(given, core=1)
    for last, step in zip(steps, steps[1:-1]):
        held, reach = stack(held, came_held), reach + [chip ^ last for chip in reach]
        came_held = swap(held, chip=step)
    across = swap(add_given(kept_y, came_y), chip=1)
    early, early_reach = held, reach
    late, late_reach = came_held, [chip ^ steps[-2] for chip in reach]
    held, reach = stack(early, late), early_reach + late_reach
    came_held = swap(held, chip=1)
    other_early = swap(early, core=1)
    across, came, other_early = together((across, came, other_early))

    parts = list(add_kept(kept, came, across))
    late, parts = together((late, parts))
    other_late = swap(late, core=1)
    parts[1:] = [swap(part, chip=2 * z) for z, part in zip(reversed(range(1, depth)), parts[1:])]
    came_held, other_late, parts = together((came_held, other_late, parts))
    other_came = swap(came_held, core=1)
    reach_y = [chip ^ 1 for chip in reach]
    queries = [held, other_early, other_late, came_held]
    reaches = [(0, reach), (1, early_reach), (1, late_reach), (0, reach_y)]
    grads, scores = first_scores(parts, queries, reaches, rank)
    return last_scores(grads, scores, other_came, reach_y)


def solution(mesh):
    return jax.shard_map(
        shards,
        mesh=mesh,
        in_specs=(
            P("ex", "groups"),
            P("ex", "groups"),
            P("ex", None),
            P("ex", None),
            P("ex", None),
        ),
        out_specs=P(("groups", "ex"), None),
        check_vma=False,
    )
```

```python
import functools

import jax
import jax.numpy as jnp
from jax import lax
from jax.experimental import pallas as pl
from jax.experimental.pallas import tpu as pltpu
from jax.sharding import PartitionSpec as P

SEQ = 64
VMEM_BYTES = 32 * 1024 * 1024
LOADED_ROWS = 128
PLAIN = 2
LEFT_OVER = 0.36 * 2.0**-8
LANES_BY_LANES = (((1,), (1,)), ((), ()))
HBM_SPEC = pl.BlockSpec(memory_space=pltpu.HBM)
VMEM_SPEC = pl.BlockSpec(memory_space=pltpu.VMEM)
PARAMS = pltpu.CompilerParams(vmem_limit_bytes=VMEM_BYTES)


def project_loaded_kernel(x_hbm, w_hbm, p_in_hbm, p_out_hbm, low_in_ref, low_out_ref, x_buf, w_buf, p_in, p_out, sems, p_sems):
    matrices = [
        pltpu.make_async_copy(p_in_hbm, p_in, p_sems.at[0]),
        pltpu.make_async_copy(p_out_hbm.at[:, pl.ds(0, p_out.shape[1])], p_out, p_sems.at[1]),
    ]
    chunks = []
    for hbm, buf, matrix, low_ref in ((x_hbm, x_buf, p_in, low_in_ref), (w_hbm, w_buf, p_out, low_out_ref)):
        count = buf.shape[0] // LOADED_ROWS if buf.shape[0] % LOADED_ROWS == 0 else 1
        for chunk in range(count):
            part = pl.ds(chunk * (buf.shape[0] // count), buf.shape[0] // count)
            copy = pltpu.make_async_copy(hbm.at[part, :], buf.at[part, :], sems.at[len(chunks)])
            chunks.append((part, buf, matrix, low_ref, copy, chunk == 0))
    for copy in matrices + [chunk[4] for chunk in chunks]:
        copy.start()
    for copy in matrices:
        copy.wait()
    step = min(1024, low_in_ref.shape[1])
    for part, buf, matrix, low_ref, copy, first in chunks:
        copy.wait()
        for column in range(0, low_ref.shape[1], step):
            columns = slice(column, column + step)
            product = jnp.dot(matrix[:, part], buf[part, columns], preferred_element_type=jnp.float32)
            low_ref[:, columns] = product if first else low_ref[:, columns] + product


def project_loaded(inputs, out_grads, proj_in_t, proj_out_t, rows):
    arrays = [pltpu.with_memory_space_constraint(a, pltpu.HBM) for a in (inputs, out_grads, proj_in_t, proj_out_t)]
    rank, tokens = proj_in_t.shape[0], inputs.shape[1]
    chunks = sum(a // LOADED_ROWS if a % LOADED_ROWS == 0 else 1 for a in (inputs.shape[0], rows))
    return pl.pallas_call(
        project_loaded_kernel,
        out_shape=[jax.ShapeDtypeStruct((rank, tokens), jnp.float32)] * 2,
        in_specs=[HBM_SPEC] * 4,
        out_specs=[VMEM_SPEC] * 2,
        scratch_shapes=[
            pltpu.VMEM(inputs.shape, jnp.bfloat16),
            pltpu.VMEM((rows, tokens), jnp.bfloat16),
            pltpu.VMEM(proj_in_t.shape, jnp.bfloat16),
            pltpu.VMEM((rank, max(rows, 128)), jnp.bfloat16),
            pltpu.SemaphoreType.DMA((chunks,)),
            pltpu.SemaphoreType.DMA((2,)),
        ],
        compiler_params=PARAMS,
        cost_estimate=pl.CostEstimate(
            flops=2 * rank * (inputs.shape[0] + rows) * tokens,
            bytes_accessed=2 * (inputs.shape[0] + rows) * tokens,
            transcendentals=0,
        ),
    )(*arrays)


def project_kernel(done, low_in_ref, low_out_ref, p_ref, w_ref, *refs):
    *given, kept_y, kept_here = refs
    given_y, given_here = given[:-1], given[-1:]
    here = lax.axis_index("ex")
    core, chip = lax.rem(here, 2), lax.div(here, 2)
    depth = kept_y.shape[0]
    rank, width = kept_y.shape[1] // 2, kept_y.shape[2]
    for flip, given_refs, kept_ref in ((1, given_y, kept_y), (0, given_here, kept_here)):
        for z in range(depth):
            place = lax.bitwise_xor(chip, 2 * z + flip)
            columns = pl.ds(pl.multiple_of(place * 2 * width, 2 * width), 2 * width)
            low_out = jnp.dot(p_ref[:, done:], w_ref[done:, columns], preferred_element_type=jnp.float32)
            low_out = low_out + low_out_ref[:, columns]
            given_ref = given_refs[z * len(given_refs) // depth]
            for lines, low in ((slice(0, rank), low_in_ref[:, columns]), (slice(rank, 2 * rank), low_out)):
                left, right = low[:, :width], low[:, width:]
                given_ref[z % given_ref.shape[0], lines, :] = jnp.where(core == 0, right, left)
                kept_ref[z, lines, :] = jnp.where(core == 0, left, right)


def project(inputs, out_grads, proj_in_t, proj_out_t, devices):
    rank, width = proj_in_t.shape[0], inputs.shape[1] // devices
    units = out_grads.shape[0]
    rows = LOADED_ROWS if units % LOADED_ROWS == 0 else 16
    lows = project_loaded(inputs, out_grads, proj_in_t, proj_out_t, rows)
    low = jax.ShapeDtypeStruct((devices // 4, 2 * rank, width), jnp.float32)
    half = jax.ShapeDtypeStruct((devices // 8, 2 * rank, width), jnp.float32)
    return pl.pallas_call(
        functools.partial(project_kernel, rows),
        out_shape=[half] * 2 + [low] * 3,
        in_specs=[VMEM_SPEC] * 4,
        out_specs=[VMEM_SPEC] * 5,
        compiler_params=PARAMS,
        cost_estimate=pl.CostEstimate(
            flops=2 * rank * out_grads.size, bytes_accessed=2 * out_grads.size, transcendentals=0
        ),
    )(*lows, proj_out_t, out_grads)


def put_coded(out_ref, low):
    rows = low.shape[0]
    rounded = low.astype(jnp.bfloat16)
    out_ref[:rows, :] = rounded
    above = jnp.where(low > rounded.astype(jnp.float32), 1.0, 0.0)
    part = rows // 8
    word = above[:part, :]
    for index in range(1, 8):
        word = word + 2.0**index * above[index * part : (index + 1) * part, :]
    out_ref[rows:, :] = word.astype(jnp.bfloat16)


def add_coded(total, ref):
    part = ref.shape[0] // 9
    word = ref[8 * part :, :].astype(jnp.float32)
    parts = []
    for index in reversed(range(8)):
        above = jnp.floor(word * 0.5**index)
        word = word - above * 2.0**index
        rounded = ref[index * part : (index + 1) * part, :].astype(jnp.float32)
        left = jnp.abs(rounded) * ((2.0 * LEFT_OVER) * above - LEFT_OVER)
        parts.append((slice(index * part, (index + 1) * part), total(index * part, part) + rounded + left))
    return parts


def add_given_kernel(kept_ref, *refs):
    *came_refs, out_ref = refs
    half = came_refs[0].shape[0]
    for block in range(out_ref.shape[0]):
        put_coded(out_ref.at[block], kept_ref[block] + came_refs[block // half][block % half])


def add_given(kept, came):
    blocks, rows, width = kept.shape
    return pl.pallas_call(
        add_given_kernel,
        out_shape=jax.ShapeDtypeStruct((blocks, rows // 8 * 9, width), jnp.bfloat16),
        compiler_params=PARAMS,
    )(kept, *came)


def add_kept_kernel(kept_ref, came_ref, across_ref, own_ref, *out_refs):
    for z in range(len(out_refs) + 1):
        def here(first, rows):
            return kept_ref[z, first : first + rows, :] + came_ref[z, first : first + rows, :]

        sums = add_coded(here, across_ref.at[z])
        if z == 0:
            for rows, total in sums:
                own_ref[rows, :] = total
        elif z <= PLAIN:
            for rows, total in sums:
                out_refs[len(out_refs) - z][rows, :] = total.astype(jnp.bfloat16)
        else:
            put_coded(out_refs[len(out_refs) - z], jnp.concatenate([total for _, total in reversed(sums)], axis=0))


def add_kept(kept, came, across):
    depth, rows, width = kept.shape
    own = jax.ShapeDtypeStruct((rows, width), jnp.float32)
    heights = [rows if z <= PLAIN else rows // 8 * 9 for z in reversed(range(1, depth))]
    return pl.pallas_call(
        add_kept_kernel,
        out_shape=[own] + [jax.ShapeDtypeStruct((height, width), jnp.bfloat16) for height in heights],
        compiler_params=PARAMS,
    )(kept, came, across)


def stack_kernel(left_ref, right_ref, out_ref):
    out_ref[: left_ref.shape[0]] = left_ref[...]
    out_ref[left_ref.shape[0] :] = right_ref[...]


def stack(left, right):
    return pl.pallas_call(
        stack_kernel,
        out_shape=jax.ShapeDtypeStruct((2 * left.shape[0],) + left.shape[1:], left.dtype),
        compiler_params=PARAMS,
    )(left, right)


def add_scores(queries_ref, chips, place, grads, sums_ref):
    examples, half_rank, lanes = grads.shape
    held = queries_ref.shape[1]
    step = 4 if len(chips) % 4 == 0 else 2
    here = lax.div(lax.axis_index("ex"), 2)
    for first in range(0, len(chips), step):
        sums = [jnp.zeros((step * held, lanes), jnp.float32) for _ in range(examples)]
        for k in range(half_rank):
            query = queries_ref[first : first + step, :, k * lanes : (k + 1) * lanes].astype(jnp.float32)
            query = query.reshape(step * held, lanes)
            for n in range(examples):
                sums[n] = sums[n] + query * grads[n, k : k + 1, :]
        for part in range(step):
            source = lax.bitwise_xor(here, chips[first + part])
            for n in range(examples):
                sums_ref[n, source, place] = sums[n][part * held : (part + 1) * held, :]


def first_score_kernel(parts_count, held, *refs):
    part_refs, query_refs = refs[:parts_count], refs[parts_count : parts_count + len(held)]
    grads_ref, sums_ref, total_ref = refs[parts_count + len(held) :]
    rank, tokens = total_ref.shape[0] // 2, total_ref.shape[1]
    core = lax.rem(lax.axis_index("ex"), 2)
    total_ref[...] = part_refs[0][...]
    for part_ref in part_refs[1:]:
        if part_ref.shape[0] == 2 * rank:
            total_ref[...] += part_ref[...].astype(jnp.float32)
            continue
        for rows, total in add_coded(lambda first, count: total_ref[first : first + count, :], part_ref):
            total_ref[rows, :] = total
    even = total_ref[pl.ds(rank, rank // 2, stride=2), :]
    odd = total_ref[pl.ds(rank + 1, rank // 2, stride=2), :]
    token = lax.broadcasted_iota(jnp.int32, (rank, tokens), 1)
    for n in range(tokens // SEQ):
        mine = jnp.where((token >= n * SEQ) & (token < (n + 1) * SEQ), total_ref[:rank, :], 0.0)
        for side, rows in enumerate((even, odd)):
            grads_ref[n, :, side * rank : (side + 1) * rank] = lax.dot_general(
                rows, mine, LANES_BY_LANES, precision=lax.Precision.HIGHEST, preferred_element_type=jnp.float32
            )
    sums_ref[...] = jnp.zeros_like(sums_ref)
    for queries_ref, (other, chips) in zip(query_refs, held):
        add_scores(queries_ref, chips, lax.rem(core + other, 2), grads_ref, sums_ref)


def last_score_kernel(chips, grads_ref, before_ref, queries_ref, out_ref, sums_ref):
    core = lax.rem(lax.axis_index("ex"), 2)
    sums_ref[...] = before_ref[...]
    add_scores(queries_ref, chips, lax.rem(core + 1, 2), grads_ref, sums_ref)
    examples, *rows, lanes = sums_ref.shape
    sums = sums_ref[...].reshape(examples * out_ref.shape[1], lanes)
    high = sums.astype(jnp.bfloat16)
    low = (sums - high.astype(jnp.float32)).astype(jnp.bfloat16)
    ones = jnp.ones((16, lanes), jnp.bfloat16)
    row = sum(lax.dot_general(ones, part, LANES_BY_LANES, preferred_element_type=jnp.float32) for part in (high, low))
    for n in range(examples):
        out_ref[n : n + 1, :] = row[0:1, n * out_ref.shape[1] : (n + 1) * out_ref.shape[1]]


def first_scores(parts, queries, held, rank):
    tokens = parts[0].shape[1]
    examples = tokens // SEQ
    chips = 2 * queries[0].shape[0]
    return pl.pallas_call(
        functools.partial(first_score_kernel, len(parts), held),
        out_shape=[
            jax.ShapeDtypeStruct((examples, rank // 2, 2 * rank), jnp.float32),
            jax.ShapeDtypeStruct((examples, chips, 2, queries[0].shape[1], 2 * rank), jnp.float32),
        ],
        scratch_shapes=[pltpu.VMEM((2 * rank, tokens), jnp.float32)],
        compiler_params=PARAMS,
    )(*parts, *queries)


def last_scores(grads, sums, queries, chips):
    examples, all_chips, cores, held, _ = sums.shape
    return pl.pallas_call(
        functools.partial(last_score_kernel, chips),
        out_shape=jax.ShapeDtypeStruct((examples, all_chips * cores * held), jnp.float32),
        scratch_shapes=[pltpu.VMEM(sums.shape, jnp.float32)],
        compiler_params=PARAMS,
    )(grads, sums, queries)


def shards(inputs, out_grads, proj_in, proj_out, queries):
    devices = lax.axis_size("ex")
    chips = devices // 2
    depth = chips // 2
    rank = proj_in.shape[1]
    together = lax.optimization_barrier

    def swap(array, chip=0, core=0):
        distance = 2 * chip + core
        return lax.ppermute(array, "ex", [(i, i ^ distance) for i in range(devices)])

    steps = [1 << bit for bit in reversed(range(chips.bit_length() - 1))]
    held, reach = queries[None], [0]
    came_held = swap(held, chip=steps[0])
    lows = project(inputs, out_grads, proj_in.T, proj_out.T, devices)
    *given_y, given, kept_y, kept = lows
    came_y = [swap(array, core=1) for array in given_y]
    came = swap(given, core=1)
    for last, step in zip(steps, steps[1:-1]):
        held, reach = stack(held, came_held), reach + [chip ^ last for chip in reach]
        came_held = swap(held, chip=step)
    across = swap(add_given(kept_y, came_y), chip=1)
    early, early_reach = held, reach
    late, late_reach = came_held, [chip ^ steps[-2] for chip in reach]
    held, reach = stack(early, late), early_reach + late_reach
    came_held = swap(held, chip=1)
    other_early = swap(early, core=1)
    across, came, other_early = together((across, came, other_early))

    parts = list(add_kept(kept, came, across))
    late, parts = together((late, parts))
    other_late = swap(late, core=1)
    parts[1:] = [swap(part, chip=2 * z) for z, part in zip(reversed(range(1, depth)), parts[1:])]
    came_held, other_late, parts = together((came_held, other_late, parts))
    other_came = swap(came_held, core=1)
    reach_y = [chip ^ 1 for chip in reach]
    queries = [held, other_early, other_late, came_held]
    reaches = [(0, reach), (1, early_reach), (1, late_reach), (0, reach_y)]
    grads, scores = first_scores(parts, queries, reaches, rank)
    return last_scores(grads, scores, other_came, reach_y)


def solution(mesh):
    return jax.shard_map(
        shards,
        mesh=mesh,
        in_specs=(
            P("ex", "groups"),
            P("ex", "groups"),
            P("ex", None),
            P("ex", None),
            P("ex", None),
        ),
        out_specs=P(("groups", "ex"), None),
        check_vma=False,
    )
```

```python
import functools

import jax
import jax.numpy as jnp
from jax import lax
from jax.experimental import pallas as pl
from jax.experimental.pallas import tpu as pltpu
from jax.sharding import PartitionSpec as P

SEQ = 64
VMEM_BYTES = 32 * 1024 * 1024
LOADED_ROWS = 128
PLAIN = 2
LEFT_OVER = 0.36 * 2.0**-8
LANES_BY_LANES = (((1,), (1,)), ((), ()))
HBM_SPEC = pl.BlockSpec(memory_space=pltpu.HBM)
VMEM_SPEC = pl.BlockSpec(memory_space=pltpu.VMEM)
PARAMS = pltpu.CompilerParams(vmem_limit_bytes=VMEM_BYTES)


def project_loaded_kernel(x_hbm, w_hbm, p_in_hbm, p_out_hbm, low_in_ref, low_out_ref, x_buf, w_buf, p_in, p_out, sems, p_sems):
    matrices = [
        pltpu.make_async_copy(p_in_hbm, p_in, p_sems.at[0]),
        pltpu.make_async_copy(p_out_hbm.at[:, pl.ds(0, p_out.shape[1])], p_out, p_sems.at[1]),
    ]
    chunks = []
    for hbm, buf, matrix, low_ref in ((x_hbm, x_buf, p_in, low_in_ref), (w_hbm, w_buf, p_out, low_out_ref)):
        count = buf.shape[0] // LOADED_ROWS if buf.shape[0] % LOADED_ROWS == 0 else 1
        for chunk in range(count):
            part = pl.ds(chunk * (buf.shape[0] // count), buf.shape[0] // count)
            copy = pltpu.make_async_copy(hbm.at[part, :], buf.at[part, :], sems.at[len(chunks)])
            chunks.append((part, buf, matrix, low_ref, copy, chunk == 0))
    for copy in matrices + [chunk[4] for chunk in chunks]:
        copy.start()
    for copy in matrices:
        copy.wait()
    step = min(1024, low_in_ref.shape[1])
    for part, buf, matrix, low_ref, copy, first in chunks:
        copy.wait()
        for column in range(0, low_ref.shape[1], step):
            columns = slice(column, column + step)
            product = jnp.dot(matrix[:, part], buf[part, columns], preferred_element_type=jnp.float32)
            low_ref[:, columns] = product if first else low_ref[:, columns] + product


def project_loaded(inputs, out_grads, proj_in_t, proj_out_t, rows):
    arrays = [pltpu.with_memory_space_constraint(a, pltpu.HBM) for a in (inputs, out_grads, proj_in_t, proj_out_t)]
    rank, tokens = proj_in_t.shape[0], inputs.shape[1]
    chunks = sum(a // LOADED_ROWS if a % LOADED_ROWS == 0 else 1 for a in (inputs.shape[0], rows))
    return pl.pallas_call(
        project_loaded_kernel,
        out_shape=[jax.ShapeDtypeStruct((rank, tokens), jnp.float32)] * 2,
        in_specs=[HBM_SPEC] * 4,
        out_specs=[VMEM_SPEC] * 2,
        scratch_shapes=[
            pltpu.VMEM(inputs.shape, jnp.bfloat16),
            pltpu.VMEM((rows, tokens), jnp.bfloat16),
            pltpu.VMEM(proj_in_t.shape, jnp.bfloat16),
            pltpu.VMEM((rank, max(rows, 128)), jnp.bfloat16),
            pltpu.SemaphoreType.DMA((chunks,)),
            pltpu.SemaphoreType.DMA((2,)),
        ],
        compiler_params=PARAMS,
        cost_estimate=pl.CostEstimate(
            flops=2 * rank * (inputs.shape[0] + rows) * tokens,
            bytes_accessed=2 * (inputs.shape[0] + rows) * tokens,
            transcendentals=0,
        ),
    )(*arrays)


def project_kernel(done, flip, low_in_ref, low_out_ref, p_ref, w_ref, *refs):
    *given_refs, kept_ref = refs
    here = lax.axis_index("ex")
    core, chip = lax.rem(here, 2), lax.div(here, 2)
    depth = kept_ref.shape[0]
    rank, width = kept_ref.shape[1] // 2, kept_ref.shape[2]
    for z in range(depth):
        place = lax.bitwise_xor(chip, 2 * z + flip)
        columns = pl.ds(pl.multiple_of(place * 2 * width, 2 * width), 2 * width)
        low_out = jnp.dot(p_ref[:, done:], w_ref[done:, columns], preferred_element_type=jnp.float32)
        low_out = low_out + low_out_ref[:, columns]
        given_ref = given_refs[z * len(given_refs) // depth]
        for lines, low in ((slice(0, rank), low_in_ref[:, columns]), (slice(rank, 2 * rank), low_out)):
            left, right = low[:, :width], low[:, width:]
            given_ref[z % given_ref.shape[0], lines, :] = jnp.where(core == 0, right, left)
            kept_ref[z, lines, :] = jnp.where(core == 0, left, right)


def project(inputs, out_grads, proj_in_t, proj_out_t, devices):
    rank, width = proj_in_t.shape[0], inputs.shape[1] // devices
    units = out_grads.shape[0]
    rows = LOADED_ROWS if units % LOADED_ROWS == 0 else 16
    lows = project_loaded(inputs, out_grads, proj_in_t, proj_out_t, rows)

    def part(flip, given_count):
        low = jax.ShapeDtypeStruct((devices // 4, 2 * rank, width), jnp.float32)
        given = jax.ShapeDtypeStruct((devices // 4 // given_count, 2 * rank, width), jnp.float32)
        *given, kept = pl.pallas_call(
            functools.partial(project_kernel, rows, flip),
            out_shape=[given] * given_count + [low],
            in_specs=[VMEM_SPEC] * 4,
            out_specs=[VMEM_SPEC] * (given_count + 1),
            compiler_params=PARAMS,
            cost_estimate=pl.CostEstimate(
                flops=rank * out_grads.size, bytes_accessed=out_grads.size, transcendentals=0
            ),
        )(*lows, proj_out_t, out_grads)
        return given, kept

    return part(1, 2), part(0, 1)


def put_coded(out_ref, low):
    rows = low.shape[0]
    rounded = low.astype(jnp.bfloat16)
    out_ref[:rows, :] = rounded
    above = jnp.where(low > rounded.astype(jnp.float32), 1.0, 0.0)
    part = rows // 8
    word = above[:part, :]
    for index in range(1, 8):
        word = word + 2.0**index * above[index * part : (index + 1) * part, :]
    out_ref[rows:, :] = word.astype(jnp.bfloat16)


def add_coded(total, ref):
    part = ref.shape[0] // 9
    word = ref[8 * part :, :].astype(jnp.float32)
    parts = []
    for index in reversed(range(8)):
        above = jnp.floor(word * 0.5**index)
        word = word - above * 2.0**index
        rounded = ref[index * part : (index + 1) * part, :].astype(jnp.float32)
        left = jnp.abs(rounded) * ((2.0 * LEFT_OVER) * above - LEFT_OVER)
        parts.append((slice(index * part, (index + 1) * part), total(index * part, part) + rounded + left))
    return parts


def add_given_kernel(kept_ref, *refs):
    *came_refs, out_ref = refs
    half = came_refs[0].shape[0]
    for block in range(out_ref.shape[0]):
        put_coded(out_ref.at[block], kept_ref[block] + came_refs[block // half][block % half])


def add_given(kept, came):
    blocks, rows, width = kept.shape
    return pl.pallas_call(
        add_given_kernel,
        out_shape=jax.ShapeDtypeStruct((blocks, rows // 8 * 9, width), jnp.bfloat16),
        compiler_params=PARAMS,
    )(kept, *came)


def add_kept_kernel(kept_ref, came_ref, across_ref, own_ref, *out_refs):
    for z in range(len(out_refs) + 1):
        def here(first, rows):
            return kept_ref[z, first : first + rows, :] + came_ref[z, first : first + rows, :]

        sums = add_coded(here, across_ref.at[z])
        if z == 0:
            for rows, total in sums:
                own_ref[rows, :] = total
        elif z <= PLAIN:
            for rows, total in sums:
                out_refs[len(out_refs) - z][rows, :] = total.astype(jnp.bfloat16)
        else:
            put_coded(out_refs[len(out_refs) - z], jnp.concatenate([total for _, total in reversed(sums)], axis=0))


def add_kept(kept, came, across):
    depth, rows, width = kept.shape
    own = jax.ShapeDtypeStruct((rows, width), jnp.float32)
    heights = [rows if z <= PLAIN else rows // 8 * 9 for z in reversed(range(1, depth))]
    return pl.pallas_call(
        add_kept_kernel,
        out_shape=[own] + [jax.ShapeDtypeStruct((height, width), jnp.bfloat16) for height in heights],
        compiler_params=PARAMS,
    )(kept, came, across)


def stack_kernel(left_ref, right_ref, out_ref):
    out_ref[: left_ref.shape[0]] = left_ref[...]
    out_ref[left_ref.shape[0] :] = right_ref[...]


def stack(left, right):
    return pl.pallas_call(
        stack_kernel,
        out_shape=jax.ShapeDtypeStruct((2 * left.shape[0],) + left.shape[1:], left.dtype),
        compiler_params=PARAMS,
    )(left, right)


def add_scores(queries_ref, chips, place, grads, sums_ref):
    examples, half_rank, lanes = grads.shape
    held = queries_ref.shape[1]
    step = 4 if len(chips) % 4 == 0 else 2
    here = lax.div(lax.axis_index("ex"), 2)
    for first in range(0, len(chips), step):
        sums = [jnp.zeros((step * held, lanes), jnp.float32) for _ in range(examples)]
        for k in range(half_rank):
            query = queries_ref[first : first + step, :, k * lanes : (k + 1) * lanes].astype(jnp.float32)
            query = query.reshape(step * held, lanes)
            for n in range(examples):
                sums[n] = sums[n] + query * grads[n, k : k + 1, :]
        for part in range(step):
            source = lax.bitwise_xor(here, chips[first + part])
            for n in range(examples):
                sums_ref[n, source, place] = sums[n][part * held : (part + 1) * held, :]


def first_score_kernel(parts_count, held, *refs):
    part_refs, query_refs = refs[:parts_count], refs[parts_count : parts_count + len(held)]
    grads_ref, sums_ref, total_ref = refs[parts_count + len(held) :]
    rank, tokens = total_ref.shape[0] // 2, total_ref.shape[1]
    core = lax.rem(lax.axis_index("ex"), 2)
    total_ref[...] = part_refs[0][...]
    for part_ref in part_refs[1:]:
        if part_ref.shape[0] == 2 * rank:
            total_ref[...] += part_ref[...].astype(jnp.float32)
            continue
        for rows, total in add_coded(lambda first, count: total_ref[first : first + count, :], part_ref):
            total_ref[rows, :] = total
    even = total_ref[pl.ds(rank, rank // 2, stride=2), :]
    odd = total_ref[pl.ds(rank + 1, rank // 2, stride=2), :]
    token = lax.broadcasted_iota(jnp.int32, (rank, tokens), 1)
    for n in range(tokens // SEQ):
        mine = jnp.where((token >= n * SEQ) & (token < (n + 1) * SEQ), total_ref[:rank, :], 0.0)
        for side, rows in enumerate((even, odd)):
            grads_ref[n, :, side * rank : (side + 1) * rank] = lax.dot_general(
                rows, mine, LANES_BY_LANES, precision=lax.Precision.HIGHEST, preferred_element_type=jnp.float32
            )
    sums_ref[...] = jnp.zeros_like(sums_ref)
    for queries_ref, (other, chips) in zip(query_refs, held):
        add_scores(queries_ref, chips, lax.rem(core + other, 2), grads_ref, sums_ref)


def last_score_kernel(chips, grads_ref, before_ref, queries_ref, out_ref, sums_ref):
    core = lax.rem(lax.axis_index("ex"), 2)
    sums_ref[...] = before_ref[...]
    add_scores(queries_ref, chips, lax.rem(core + 1, 2), grads_ref, sums_ref)
    examples, *rows, lanes = sums_ref.shape
    sums = sums_ref[...].reshape(examples * out_ref.shape[1], lanes)
    high = sums.astype(jnp.bfloat16)
    low = (sums - high.astype(jnp.float32)).astype(jnp.bfloat16)
    ones = jnp.ones((16, lanes), jnp.bfloat16)
    row = sum(lax.dot_general(ones, part, LANES_BY_LANES, preferred_element_type=jnp.float32) for part in (high, low))
    for n in range(examples):
        out_ref[n : n + 1, :] = row[0:1, n * out_ref.shape[1] : (n + 1) * out_ref.shape[1]]


def first_scores(parts, queries, held, rank):
    tokens = parts[0].shape[1]
    examples = tokens // SEQ
    chips = 2 * queries[0].shape[0]
    return pl.pallas_call(
        functools.partial(first_score_kernel, len(parts), held),
        out_shape=[
            jax.ShapeDtypeStruct((examples, rank // 2, 2 * rank), jnp.float32),
            jax.ShapeDtypeStruct((examples, chips, 2, queries[0].shape[1], 2 * rank), jnp.float32),
        ],
        scratch_shapes=[pltpu.VMEM((2 * rank, tokens), jnp.float32)],
        compiler_params=PARAMS,
    )(*parts, *queries)


def last_scores(grads, sums, queries, chips):
    examples, all_chips, cores, held, _ = sums.shape
    return pl.pallas_call(
        functools.partial(last_score_kernel, chips),
        out_shape=jax.ShapeDtypeStruct((examples, all_chips * cores * held), jnp.float32),
        scratch_shapes=[pltpu.VMEM(sums.shape, jnp.float32)],
        compiler_params=PARAMS,
    )(grads, sums, queries)


def shards(inputs, out_grads, proj_in, proj_out, queries):
    devices = lax.axis_size("ex")
    chips = devices // 2
    depth = chips // 2
    rank = proj_in.shape[1]
    together = lax.optimization_barrier

    def swap(array, chip=0, core=0):
        distance = 2 * chip + core
        return lax.ppermute(array, "ex", [(i, i ^ distance) for i in range(devices)])

    steps = [1 << bit for bit in reversed(range(chips.bit_length() - 1))]
    held, reach = queries[None], [0]
    came_held = swap(held, chip=steps[0])
    (given_y, kept_y), (given, kept) = project(inputs, out_grads, proj_in.T, proj_out.T, devices)
    came_y = [swap(array, core=1) for array in given_y]
    came = swap(given[0], core=1)
    for last, step in zip(steps, steps[1:-1]):
        held, reach = stack(held, came_held), reach + [chip ^ last for chip in reach]
        came_held = swap(held, chip=step)
    across = swap(add_given(kept_y, came_y), chip=1)
    early, early_reach = held, reach
    late, late_reach = came_held, [chip ^ steps[-2] for chip in reach]
    held, reach = stack(early, late), early_reach + late_reach
    came_held = swap(held, chip=1)
    other_early = swap(early, core=1)
    across, came, other_early = together((across, came, other_early))

    parts = list(add_kept(kept, came, across))
    late, parts = together((late, parts))
    other_late = swap(late, core=1)
    parts[1:] = [swap(part, chip=2 * z) for z, part in zip(reversed(range(1, depth)), parts[1:])]
    came_held, other_late, parts = together((came_held, other_late, parts))
    other_came = swap(came_held, core=1)
    reach_y = [chip ^ 1 for chip in reach]
    queries = [held, other_early, other_late, came_held]
    reaches = [(0, reach), (1, early_reach), (1, late_reach), (0, reach_y)]
    grads, scores = first_scores(parts, queries, reaches, rank)
    return last_scores(grads, scores, other_came, reach_y)


def solution(mesh):
    return jax.shard_map(
        shards,
        mesh=mesh,
        in_specs=(
            P("ex", "groups"),
            P("ex", "groups"),
            P("ex", None),
            P("ex", None),
            P("ex", None),
        ),
        out_specs=P(("groups", "ex"), None),
        check_vma=False,
    )
```

```python
import functools

import jax
import jax.numpy as jnp
from jax import lax
from jax.experimental import pallas as pl
from jax.experimental.pallas import tpu as pltpu
from jax.sharding import PartitionSpec as P

SEQ = 64
VMEM_BYTES = 32 * 1024 * 1024
LOADED_ROWS = 128
PLAIN = 2
LEFT_OVER = 0.36 * 2.0**-8
LANES_BY_LANES = (((1,), (1,)), ((), ()))
HBM_SPEC = pl.BlockSpec(memory_space=pltpu.HBM)
VMEM_SPEC = pl.BlockSpec(memory_space=pltpu.VMEM)
PARAMS = pltpu.CompilerParams(vmem_limit_bytes=VMEM_BYTES)


def project_loaded_kernel(x_hbm, w_hbm, p_in_hbm, p_out_hbm, low_in_ref, low_out_ref, x_buf, w_buf, p_in, p_out, sems, p_sems):
    matrices = [
        pltpu.make_async_copy(p_in_hbm, p_in, p_sems.at[0]),
        pltpu.make_async_copy(p_out_hbm.at[:, pl.ds(0, p_out.shape[1])], p_out, p_sems.at[1]),
    ]
    chunks = []
    for hbm, buf, matrix, low_ref in ((x_hbm, x_buf, p_in, low_in_ref), (w_hbm, w_buf, p_out, low_out_ref)):
        count = buf.shape[0] // LOADED_ROWS if buf.shape[0] % LOADED_ROWS == 0 else 1
        for chunk in range(count):
            part = pl.ds(chunk * (buf.shape[0] // count), buf.shape[0] // count)
            copy = pltpu.make_async_copy(hbm.at[part, :], buf.at[part, :], sems.at[len(chunks)])
            chunks.append((part, buf, matrix, low_ref, copy, chunk == 0))
    for copy in matrices + [chunk[4] for chunk in chunks]:
        copy.start()
    for copy in matrices:
        copy.wait()
    step = min(1024, low_in_ref.shape[1])
    for part, buf, matrix, low_ref, copy, first in chunks:
        copy.wait()
        for column in range(0, low_ref.shape[1], step):
            columns = slice(column, column + step)
            product = jnp.dot(matrix[:, part], buf[part, columns], preferred_element_type=jnp.float32)
            low_ref[:, columns] = product if first else low_ref[:, columns] + product


def project_loaded(inputs, out_grads, proj_in_t, proj_out_t, rows):
    arrays = [pltpu.with_memory_space_constraint(a, pltpu.HBM) for a in (inputs, out_grads, proj_in_t, proj_out_t)]
    rank, tokens = proj_in_t.shape[0], inputs.shape[1]
    chunks = sum(a // LOADED_ROWS if a % LOADED_ROWS == 0 else 1 for a in (inputs.shape[0], rows))
    return pl.pallas_call(
        project_loaded_kernel,
        out_shape=[jax.ShapeDtypeStruct((rank, tokens), jnp.float32)] * 2,
        in_specs=[HBM_SPEC] * 4,
        out_specs=[VMEM_SPEC] * 2,
        scratch_shapes=[
            pltpu.VMEM(inputs.shape, jnp.bfloat16),
            pltpu.VMEM((rows, tokens), jnp.bfloat16),
            pltpu.VMEM(proj_in_t.shape, jnp.bfloat16),
            pltpu.VMEM((rank, max(rows, 128)), jnp.bfloat16),
            pltpu.SemaphoreType.DMA((chunks,)),
            pltpu.SemaphoreType.DMA((2,)),
        ],
        compiler_params=PARAMS,
        cost_estimate=pl.CostEstimate(
            flops=2 * rank * (inputs.shape[0] + rows) * tokens,
            bytes_accessed=2 * (inputs.shape[0] + rows) * tokens,
            transcendentals=0,
        ),
    )(*arrays)


def project_kernel(done, flip, low_in_ref, low_out_ref, p_ref, w_ref, *refs):
    *given_refs, kept_ref = refs
    here = lax.axis_index("ex")
    core, chip = lax.rem(here, 2), lax.div(here, 2)
    depth = kept_ref.shape[0]
    rank, width = kept_ref.shape[1] // 2, kept_ref.shape[2]
    for z in range(depth):
        place = lax.bitwise_xor(chip, 2 * z + flip)
        columns = pl.ds(pl.multiple_of(place * 2 * width, 2 * width), 2 * width)
        low_out = jnp.dot(p_ref[:, done:], w_ref[done:, columns], preferred_element_type=jnp.float32)
        low_out = low_out + low_out_ref[:, columns]
        given_ref = given_refs[z * len(given_refs) // depth]
        for lines, low in ((slice(0, rank), low_in_ref[:, columns]), (slice(rank, 2 * rank), low_out)):
            left, right = low[:, :width], low[:, width:]
            given_ref[z % given_ref.shape[0], lines, :] = jnp.where(core == 0, right, left)
            kept_ref[z, lines, :] = jnp.where(core == 0, left, right)


def project(inputs, out_grads, proj_in_t, proj_out_t, devices):
    rank, width = proj_in_t.shape[0], inputs.shape[1] // devices
    units = out_grads.shape[0]
    rows = LOADED_ROWS if units % LOADED_ROWS == 0 else 16
    lows = project_loaded(inputs, out_grads, proj_in_t, proj_out_t, rows)

    def part(flip, given_count):
        low = jax.ShapeDtypeStruct((devices // 4, 2 * rank, width), jnp.float32)
        given = jax.ShapeDtypeStruct((devices // 4 // given_count, 2 * rank, width), jnp.float32)
        *given, kept = pl.pallas_call(
            functools.partial(project_kernel, rows, flip),
            out_shape=[given] * given_count + [low],
            in_specs=[VMEM_SPEC] * 4,
            out_specs=[VMEM_SPEC] * (given_count + 1),
            compiler_params=PARAMS,
            cost_estimate=pl.CostEstimate(
                flops=rank * out_grads.size, bytes_accessed=out_grads.size, transcendentals=0
            ),
        )(*lows, proj_out_t, out_grads)
        return given, kept

    return part(1, 2), part(0, 1)


def put_coded(out_ref, low):
    rows = low.shape[0]
    rounded = low.astype(jnp.bfloat16)
    out_ref[:rows, :] = rounded
    above = jnp.where(low > rounded.astype(jnp.float32), 1.0, 0.0)
    part = rows // 8
    word = above[:part, :]
    for index in range(1, 8):
        word = word + 2.0**index * above[index * part : (index + 1) * part, :]
    out_ref[rows:, :] = word.astype(jnp.bfloat16)


def add_coded(total, ref):
    part = ref.shape[0] // 9
    word = ref[8 * part :, :].astype(jnp.float32)
    parts = []
    for index in reversed(range(8)):
        above = jnp.floor(word * 0.5**index)
        word = word - above * 2.0**index
        rounded = ref[index * part : (index + 1) * part, :].astype(jnp.float32)
        left = jnp.abs(rounded) * ((2.0 * LEFT_OVER) * above - LEFT_OVER)
        parts.append((slice(index * part, (index + 1) * part), total(index * part, part) + rounded + left))
    return parts


def add_given_kernel(kept_ref, *refs):
    *came_refs, out_ref = refs
    half = came_refs[0].shape[0]
    for block in range(out_ref.shape[0]):
        put_coded(out_ref.at[block], kept_ref[block] + came_refs[block // half][block % half])


def add_given(kept, came):
    blocks, rows, width = kept.shape
    return pl.pallas_call(
        add_given_kernel,
        out_shape=jax.ShapeDtypeStruct((blocks, rows // 8 * 9, width), jnp.bfloat16),
        compiler_params=PARAMS,
    )(kept, *came)


def add_kept_kernel(kept_ref, came_ref, across_ref, own_ref, *out_refs):
    for z in range(len(out_refs) + 1):
        def here(first, rows):
            return kept_ref[z, first : first + rows, :] + came_ref[z, first : first + rows, :]

        sums = add_coded(here, across_ref.at[z])
        if z == 0:
            for rows, total in sums:
                own_ref[rows, :] = total
        elif z <= PLAIN:
            for rows, total in sums:
                out_refs[len(out_refs) - z][rows, :] = total.astype(jnp.bfloat16)
        else:
            put_coded(out_refs[len(out_refs) - z], jnp.concatenate([total for _, total in reversed(sums)], axis=0))


def add_kept(kept, came, across):
    depth, rows, width = kept.shape
    own = jax.ShapeDtypeStruct((rows, width), jnp.float32)
    heights = [rows if z <= PLAIN else rows // 8 * 9 for z in reversed(range(1, depth))]
    return pl.pallas_call(
        add_kept_kernel,
        out_shape=[own] + [jax.ShapeDtypeStruct((height, width), jnp.bfloat16) for height in heights],
        compiler_params=PARAMS,
    )(kept, came, across)


def halves_kernel(in_ref, *out_refs):
    half = out_refs[0].shape[0]
    for index, out_ref in enumerate(out_refs):
        out_ref[...] = in_ref[index * half : (index + 1) * half]


def halves(array):
    half = jax.ShapeDtypeStruct((array.shape[0] // 2,) + array.shape[1:], array.dtype)
    return pl.pallas_call(halves_kernel, out_shape=[half] * 2, compiler_params=PARAMS)(array)


def stack_kernel(left_ref, right_ref, out_ref):
    out_ref[: left_ref.shape[0]] = left_ref[...]
    out_ref[left_ref.shape[0] :] = right_ref[...]


def stack(left, right):
    return pl.pallas_call(
        stack_kernel,
        out_shape=jax.ShapeDtypeStruct((2 * left.shape[0],) + left.shape[1:], left.dtype),
        compiler_params=PARAMS,
    )(left, right)


def add_scores(queries_ref, chips, place, grads, sums_ref):
    examples, half_rank, lanes = grads.shape
    held = queries_ref.shape[1]
    step = 4 if len(chips) % 4 == 0 else 2
    here = lax.div(lax.axis_index("ex"), 2)
    for first in range(0, len(chips), step):
        sums = [jnp.zeros((step * held, lanes), jnp.float32) for _ in range(examples)]
        for k in range(half_rank):
            query = queries_ref[first : first + step, :, k * lanes : (k + 1) * lanes].astype(jnp.float32)
            query = query.reshape(step * held, lanes)
            for n in range(examples):
                sums[n] = sums[n] + query * grads[n, k : k + 1, :]
        for part in range(step):
            source = lax.bitwise_xor(here, chips[first + part])
            for n in range(examples):
                sums_ref[n, source, place] = sums[n][part * held : (part + 1) * held, :]


def first_score_kernel(parts_count, held, *refs):
    part_refs, query_refs = refs[:parts_count], refs[parts_count : parts_count + len(held)]
    grads_ref, sums_ref, total_ref = refs[parts_count + len(held) :]
    rank, tokens = total_ref.shape[0] // 2, total_ref.shape[1]
    core = lax.rem(lax.axis_index("ex"), 2)
    total_ref[...] = part_refs[0][...]
    for part_ref in part_refs[1:]:
        if part_ref.shape[0] == 2 * rank:
            total_ref[...] += part_ref[...].astype(jnp.float32)
            continue
        for rows, total in add_coded(lambda first, count: total_ref[first : first + count, :], part_ref):
            total_ref[rows, :] = total
    even = total_ref[pl.ds(rank, rank // 2, stride=2), :]
    odd = total_ref[pl.ds(rank + 1, rank // 2, stride=2), :]
    token = lax.broadcasted_iota(jnp.int32, (rank, tokens), 1)
    for n in range(tokens // SEQ):
        mine = jnp.where((token >= n * SEQ) & (token < (n + 1) * SEQ), total_ref[:rank, :], 0.0)
        for side, rows in enumerate((even, odd)):
            grads_ref[n, :, side * rank : (side + 1) * rank] = lax.dot_general(
                rows, mine, LANES_BY_LANES, precision=lax.Precision.HIGHEST, preferred_element_type=jnp.float32
            )
    sums_ref[...] = jnp.zeros_like(sums_ref)
    for queries_ref, (other, chips) in zip(query_refs, held):
        add_scores(queries_ref, chips, lax.rem(core + other, 2), grads_ref, sums_ref)


def last_score_kernel(chips, grads_ref, before_ref, first_ref, second_ref, out_ref, sums_ref):
    core = lax.rem(lax.axis_index("ex"), 2)
    sums_ref[...] = before_ref[...]
    half = len(chips) // 2
    for queries_ref, reach in ((first_ref, chips[:half]), (second_ref, chips[half:])):
        add_scores(queries_ref, reach, lax.rem(core + 1, 2), grads_ref, sums_ref)
    examples, *rows, lanes = sums_ref.shape
    sums = sums_ref[...].reshape(examples * out_ref.shape[1], lanes)
    high = sums.astype(jnp.bfloat16)
    low = (sums - high.astype(jnp.float32)).astype(jnp.bfloat16)
    ones = jnp.ones((16, 2 * lanes), jnp.bfloat16)
    both = jnp.concatenate([high, low], axis=1)
    row = lax.dot_general(ones, both, LANES_BY_LANES, preferred_element_type=jnp.float32)
    for n in range(examples):
        out_ref[n : n + 1, :] = row[0:1, n * out_ref.shape[1] : (n + 1) * out_ref.shape[1]]


def first_scores(parts, queries, held, rank):
    tokens = parts[0].shape[1]
    examples = tokens // SEQ
    chips = 2 * queries[0].shape[0]
    return pl.pallas_call(
        functools.partial(first_score_kernel, len(parts), held),
        out_shape=[
            jax.ShapeDtypeStruct((examples, rank // 2, 2 * rank), jnp.float32),
            jax.ShapeDtypeStruct((examples, chips, 2, queries[0].shape[1], 2 * rank), jnp.float32),
        ],
        scratch_shapes=[pltpu.VMEM((2 * rank, tokens), jnp.float32)],
        compiler_params=PARAMS,
    )(*parts, *queries)


def last_scores(grads, sums, first, second, chips):
    examples, all_chips, cores, held, _ = sums.shape
    return pl.pallas_call(
        functools.partial(last_score_kernel, chips),
        out_shape=jax.ShapeDtypeStruct((examples, all_chips * cores * held), jnp.float32),
        scratch_shapes=[pltpu.VMEM(sums.shape, jnp.float32)],
        compiler_params=PARAMS,
    )(grads, sums, first, second)


def shards(inputs, out_grads, proj_in, proj_out, queries):
    devices = lax.axis_size("ex")
    chips = devices // 2
    depth = chips // 2
    rank = proj_in.shape[1]
    together = lax.optimization_barrier

    def swap(array, chip=0, core=0):
        distance = 2 * chip + core
        return lax.ppermute(array, "ex", [(i, i ^ distance) for i in range(devices)])

    steps = [1 << bit for bit in reversed(range(chips.bit_length() - 1))]
    held, reach = queries[None], [0]
    came_held = swap(held, chip=steps[0])
    (given_y, kept_y), (given, kept) = project(inputs, out_grads, proj_in.T, proj_out.T, devices)
    came_y = [swap(array, core=1) for array in given_y]
    came = swap(given[0], core=1)
    for last, step in zip(steps, steps[1:-1]):
        held, reach = stack(held, came_held), reach + [chip ^ last for chip in reach]
        came_held = swap(held, chip=step)
    across = swap(add_given(kept_y, came_y), chip=1)
    early, early_reach = held, reach
    late, late_reach = came_held, [chip ^ steps[-2] for chip in reach]
    held, reach = stack(early, late), early_reach + late_reach
    came_held = swap(held, chip=1)
    other_early = swap(early, core=1)
    across, came, other_early = together((across, came, other_early))

    parts = list(add_kept(kept, came, across))
    late, parts = together((late, parts))
    other_late = swap(late, core=1)
    parts[1:] = [swap(part, chip=2 * z) for z, part in zip(reversed(range(1, depth)), parts[1:])]
    came_held, other_late, parts = together((came_held, other_late, parts))
    other_came = [swap(half, core=1) for half in halves(came_held)]
    reach_y = [chip ^ 1 for chip in reach]
    queries = [held, other_early, other_late, came_held]
    reaches = [(0, reach), (1, early_reach), (1, late_reach), (0, reach_y)]
    grads, scores = first_scores(parts, queries, reaches, rank)
    return last_scores(grads, scores, *other_came, reach_y)


def solution(mesh):
    return jax.shard_map(
        shards,
        mesh=mesh,
        in_specs=(
            P("ex", "groups"),
            P("ex", "groups"),
            P("ex", None),
            P("ex", None),
            P("ex", None),
        ),
        out_specs=P(("groups", "ex"), None),
        check_vma=False,
    )
```

```python
import functools

import jax
import jax.numpy as jnp
from jax import lax
from jax.experimental import pallas as pl
from jax.experimental.pallas import tpu as pltpu
from jax.sharding import PartitionSpec as P

SEQ = 64
VMEM_BYTES = 32 * 1024 * 1024
LOADED_ROWS = 128
FAR_PAD = 16
LEFT_OVER = 0.36 * 2.0**-8
LANES_BY_LANES = (((1,), (1,)), ((), ()))
HBM_SPEC = pl.BlockSpec(memory_space=pltpu.HBM)
VMEM_SPEC = pl.BlockSpec(memory_space=pltpu.VMEM)
PARAMS = pltpu.CompilerParams(vmem_limit_bytes=VMEM_BYTES)


def project_loaded_kernel(x_hbm, w_hbm, p_in_hbm, p_out_hbm, low_in_ref, low_out_ref, x_buf, w_buf, p_in, p_out, sems, p_sems):
    matrices = [
        pltpu.make_async_copy(p_in_hbm, p_in, p_sems.at[0]),
        pltpu.make_async_copy(p_out_hbm.at[:, pl.ds(0, p_out.shape[1])], p_out, p_sems.at[1]),
    ]
    chunks = []
    for hbm, buf, matrix, low_ref in ((x_hbm, x_buf, p_in, low_in_ref), (w_hbm, w_buf, p_out, low_out_ref)):
        count = buf.shape[0] // LOADED_ROWS if buf.shape[0] % LOADED_ROWS == 0 else 1
        for chunk in range(count):
            part = pl.ds(chunk * (buf.shape[0] // count), buf.shape[0] // count)
            copy = pltpu.make_async_copy(hbm.at[part, :], buf.at[part, :], sems.at[len(chunks)])
            chunks.append((part, buf, matrix, low_ref, copy, chunk == 0))
    for copy in matrices + [chunk[4] for chunk in chunks]:
        copy.start()
    for copy in matrices:
        copy.wait()
    step = min(1024, low_in_ref.shape[1])
    for part, buf, matrix, low_ref, copy, first in chunks:
        copy.wait()
        for column in range(0, low_ref.shape[1], step):
            columns = slice(column, column + step)
            product = jnp.dot(matrix[:, part], buf[part, columns], preferred_element_type=jnp.float32)
            low_ref[:, columns] = product if first else low_ref[:, columns] + product


def project_loaded(inputs, out_grads, proj_in_t, proj_out_t, rows):
    arrays = [pltpu.with_memory_space_constraint(a, pltpu.HBM) for a in (inputs, out_grads, proj_in_t, proj_out_t)]
    rank, tokens = proj_in_t.shape[0], inputs.shape[1]
    chunks = sum(a // LOADED_ROWS if a % LOADED_ROWS == 0 else 1 for a in (inputs.shape[0], rows))
    return pl.pallas_call(
        project_loaded_kernel,
        out_shape=[jax.ShapeDtypeStruct((rank, tokens), jnp.float32)] * 2,
        in_specs=[HBM_SPEC] * 4,
        out_specs=[VMEM_SPEC] * 2,
        scratch_shapes=[
            pltpu.VMEM(inputs.shape, jnp.bfloat16),
            pltpu.VMEM((rows, tokens), jnp.bfloat16),
            pltpu.VMEM(proj_in_t.shape, jnp.bfloat16),
            pltpu.VMEM((rank, max(rows, 128)), jnp.bfloat16),
            pltpu.SemaphoreType.DMA((chunks,)),
            pltpu.SemaphoreType.DMA((2,)),
        ],
        compiler_params=PARAMS,
        cost_estimate=pl.CostEstimate(
            flops=2 * rank * (inputs.shape[0] + rows) * tokens,
            bytes_accessed=2 * (inputs.shape[0] + rows) * tokens,
            transcendentals=0,
        ),
    )(*arrays)


def project_kernel(done, low_in_ref, low_out_ref, p_ref, w_ref, *refs):
    *given, kept_y, kept_here = refs
    given_y, given_here = given[:-1], given[-1:]
    here = lax.axis_index("ex")
    core, chip = lax.rem(here, 2), lax.div(here, 2)
    depth = kept_y.shape[0]
    rank, width = kept_y.shape[1] // 2, kept_y.shape[2]
    for flip, given_refs, kept_ref in ((1, given_y, kept_y), (0, given_here, kept_here)):
        for z in range(depth):
            place = lax.bitwise_xor(chip, 2 * z + flip)
            columns = pl.ds(pl.multiple_of(place * 2 * width, 2 * width), 2 * width)
            low_out = jnp.dot(p_ref[:, done:], w_ref[done:, columns], preferred_element_type=jnp.float32)
            low_out = low_out + low_out_ref[:, columns]
            given_ref = given_refs[z * len(given_refs) // depth]
            for lines, low in ((slice(0, rank), low_in_ref[:, columns]), (slice(rank, 2 * rank), low_out)):
                left, right = low[:, :width], low[:, width:]
                given_ref[z % given_ref.shape[0], lines, :] = jnp.where(core == 0, right, left)
                kept_ref[z, lines, :] = jnp.where(core == 0, left, right)


def project(inputs, out_grads, proj_in_t, proj_out_t, devices):
    rank, width = proj_in_t.shape[0], inputs.shape[1] // devices
    units = out_grads.shape[0]
    rows = LOADED_ROWS if units % LOADED_ROWS == 0 else 16
    lows = project_loaded(inputs, out_grads, proj_in_t, proj_out_t, rows)
    low = jax.ShapeDtypeStruct((devices // 4, 2 * rank, width), jnp.float32)
    half = jax.ShapeDtypeStruct((devices // 8, 2 * rank, width), jnp.float32)
    return pl.pallas_call(
        functools.partial(project_kernel, rows),
        out_shape=[half] * 2 + [low] * 3,
        in_specs=[VMEM_SPEC] * 4,
        out_specs=[VMEM_SPEC] * 5,
        compiler_params=PARAMS,
        cost_estimate=pl.CostEstimate(
            flops=2 * rank * out_grads.size, bytes_accessed=2 * out_grads.size, transcendentals=0
        ),
    )(*lows, proj_out_t, out_grads)


def put_coded(out_ref, low):
    rows = low.shape[0]
    rounded = low.astype(jnp.bfloat16)
    out_ref[:rows, :] = rounded
    above = jnp.where(low > rounded.astype(jnp.float32), 1.0, 0.0)
    part = rows // 8
    word = above[:part, :]
    for index in range(1, 8):
        word = word + 2.0**index * above[index * part : (index + 1) * part, :]
    out_ref[rows : rows + part, :] = word.astype(jnp.bfloat16)


def add_coded(total, rows, ref):
    part = rows // 8
    word = ref[rows : rows + part, :].astype(jnp.float32)
    parts = []
    for index in reversed(range(8)):
        above = jnp.floor(word * 0.5**index)
        word = word - above * 2.0**index
        rounded = ref[index * part : (index + 1) * part, :].astype(jnp.float32)
        left = jnp.abs(rounded) * ((2.0 * LEFT_OVER) * above - LEFT_OVER)
        parts.append((slice(index * part, (index + 1) * part), total(index * part, part) + rounded + left))
    return parts


def add_given_kernel(kept_ref, *refs):
    *came_refs, out_ref = refs
    half = came_refs[0].shape[0]
    for block in range(out_ref.shape[0]):
        put_coded(out_ref.at[block], kept_ref[block] + came_refs[block // half][block % half])


def add_given(kept, came):
    blocks, rows, width = kept.shape
    return pl.pallas_call(
        add_given_kernel,
        out_shape=jax.ShapeDtypeStruct((blocks, rows // 8 * 9, width), jnp.bfloat16),
        compiler_params=PARAMS,
    )(kept, *came)


def add_kept_kernel(kept_ref, came_ref, across_ref, own_ref, *out_refs):
    for z in range(len(out_refs) + 1):
        def here(first, rows):
            return kept_ref[z, first : first + rows, :] + came_ref[z, first : first + rows, :]

        sums = add_coded(here, kept_ref.shape[1], across_ref.at[z])
        if z == 0:
            for rows, total in sums:
                own_ref[rows, :] = total
        else:
            put_coded(out_refs[len(out_refs) - z], jnp.concatenate([total for _, total in reversed(sums)], axis=0))


def add_kept(kept, came, across):
    depth, rows, width = kept.shape
    own = jax.ShapeDtypeStruct((rows, width), jnp.float32)
    heights = [rows // 8 * 9 + (FAR_PAD if z > 2 else 0) for z in reversed(range(1, depth))]
    return pl.pallas_call(
        add_kept_kernel,
        out_shape=[own] + [jax.ShapeDtypeStruct((height, width), jnp.bfloat16) for height in heights],
        compiler_params=PARAMS,
    )(kept, came, across)


def stack_kernel(left_ref, right_ref, out_ref):
    out_ref[: left_ref.shape[0]] = left_ref[...]
    out_ref[left_ref.shape[0] :] = right_ref[...]


def stack(left, right):
    return pl.pallas_call(
        stack_kernel,
        out_shape=jax.ShapeDtypeStruct((2 * left.shape[0],) + left.shape[1:], left.dtype),
        compiler_params=PARAMS,
    )(left, right)


def add_scores(queries_ref, chips, place, grads, sums_ref):
    examples, half_rank, lanes = grads.shape
    held = queries_ref.shape[1]
    step = 4 if len(chips) % 4 == 0 else 2
    here = lax.div(lax.axis_index("ex"), 2)
    for first in range(0, len(chips), step):
        sums = [jnp.zeros((step * held, lanes), jnp.float32) for _ in range(examples)]
        for k in range(half_rank):
            query = queries_ref[first : first + step, :, k * lanes : (k + 1) * lanes].astype(jnp.float32)
            query = query.reshape(step * held, lanes)
            for n in range(examples):
                sums[n] = sums[n] + query * grads[n, k : k + 1, :]
        for part in range(step):
            source = lax.bitwise_xor(here, chips[first + part])
            for n in range(examples):
                sums_ref[n, source, place] = sums[n][part * held : (part + 1) * held, :]


def first_score_kernel(parts_count, held, *refs):
    part_refs, query_refs = refs[:parts_count], refs[parts_count : parts_count + len(held)]
    grads_ref, sums_ref, total_ref = refs[parts_count + len(held) :]
    rank, tokens = total_ref.shape[0] // 2, total_ref.shape[1]
    core = lax.rem(lax.axis_index("ex"), 2)
    total_ref[...] = part_refs[0][...]
    for part_ref in part_refs[1:]:
        for rows, total in add_coded(lambda first, count: total_ref[first : first + count, :], 2 * rank, part_ref):
            total_ref[rows, :] = total
    even = total_ref[pl.ds(rank, rank // 2, stride=2), :]
    odd = total_ref[pl.ds(rank + 1, rank // 2, stride=2), :]
    token = lax.broadcasted_iota(jnp.int32, (rank, tokens), 1)
    for n in range(tokens // SEQ):
        mine = jnp.where((token >= n * SEQ) & (token < (n + 1) * SEQ), total_ref[:rank, :], 0.0)
        for side, rows in enumerate((even, odd)):
            grads_ref[n, :, side * rank : (side + 1) * rank] = lax.dot_general(
                rows, mine, LANES_BY_LANES, precision=lax.Precision.HIGHEST, preferred_element_type=jnp.float32
            )
    sums_ref[...] = jnp.zeros_like(sums_ref)
    for queries_ref, (other, chips) in zip(query_refs, held):
        add_scores(queries_ref, chips, lax.rem(core + other, 2), grads_ref, sums_ref)


def last_score_kernel(chips, grads_ref, before_ref, queries_ref, out_ref, sums_ref):
    core = lax.rem(lax.axis_index("ex"), 2)
    sums_ref[...] = before_ref[...]
    add_scores(queries_ref, chips, lax.rem(core + 1, 2), grads_ref, sums_ref)
    examples, *rows, lanes = sums_ref.shape
    sums = sums_ref[...].reshape(examples * out_ref.shape[1], lanes)
    high = sums.astype(jnp.bfloat16)
    low = (sums - high.astype(jnp.float32)).astype(jnp.bfloat16)
    ones = jnp.ones((16, lanes), jnp.bfloat16)
    row = sum(lax.dot_general(ones, part, LANES_BY_LANES, preferred_element_type=jnp.float32) for part in (high, low))
    for n in range(examples):
        out_ref[n : n + 1, :] = row[0:1, n * out_ref.shape[1] : (n + 1) * out_ref.shape[1]]


def first_scores(parts, queries, held, rank):
    tokens = parts[0].shape[1]
    examples = tokens // SEQ
    chips = 2 * queries[0].shape[0]
    return pl.pallas_call(
        functools.partial(first_score_kernel, len(parts), held),
        out_shape=[
            jax.ShapeDtypeStruct((examples, rank // 2, 2 * rank), jnp.float32),
            jax.ShapeDtypeStruct((examples, chips, 2, queries[0].shape[1], 2 * rank), jnp.float32),
        ],
        scratch_shapes=[pltpu.VMEM((2 * rank, tokens), jnp.float32)],
        compiler_params=PARAMS,
    )(*parts, *queries)


def last_scores(grads, sums, queries, chips):
    examples, all_chips, cores, held, _ = sums.shape
    return pl.pallas_call(
        functools.partial(last_score_kernel, chips),
        out_shape=jax.ShapeDtypeStruct((examples, all_chips * cores * held), jnp.float32),
        scratch_shapes=[pltpu.VMEM(sums.shape, jnp.float32)],
        compiler_params=PARAMS,
    )(grads, sums, queries)


def shards(inputs, out_grads, proj_in, proj_out, queries):
    devices = lax.axis_size("ex")
    chips = devices // 2
    depth = chips // 2
    rank = proj_in.shape[1]
    together = lax.optimization_barrier

    def swap(array, chip=0, core=0):
        distance = 2 * chip + core
        return lax.ppermute(array, "ex", [(i, i ^ distance) for i in range(devices)])

    steps = [1 << bit for bit in reversed(range(chips.bit_length() - 1))]
    held, reach = queries[None], [0]
    came_held = swap(held, chip=steps[0])
    lows = project(inputs, out_grads, proj_in.T, proj_out.T, devices)
    *given_y, given, kept_y, kept = lows
    came_y = [swap(array, core=1) for array in given_y]
    came = swap(given, core=1)
    for last, step in zip(steps, steps[1:-1]):
        held, reach = stack(held, came_held), reach + [chip ^ last for chip in reach]
        came_held = swap(held, chip=step)
    across = swap(add_given(kept_y, came_y), chip=1)
    early, early_reach = held, reach
    late, late_reach = came_held, [chip ^ steps[-2] for chip in reach]
    held, reach = stack(early, late), early_reach + late_reach
    came_held = swap(held, chip=1)
    other_early = swap(early, core=1)
    across, came, other_early = together((across, came, other_early))

    parts = list(add_kept(kept, came, across))
    late, parts = together((late, parts))
    other_late = swap(late, core=1)
    parts[1:] = [swap(part, chip=2 * z) for z, part in zip(reversed(range(1, depth)), parts[1:])]
    came_held, other_late, parts = together((came_held, other_late, parts))
    other_came = swap(came_held, core=1)
    reach_y = [chip ^ 1 for chip in reach]
    queries = [held, other_early, other_late, came_held]
    reaches = [(0, reach), (1, early_reach), (1, late_reach), (0, reach_y)]
    grads, scores = first_scores(parts, queries, reaches, rank)
    return last_scores(grads, scores, other_came, reach_y)


def solution(mesh):
    return jax.shard_map(
        shards,
        mesh=mesh,
        in_specs=(
            P("ex", "groups"),
            P("ex", "groups"),
            P("ex", None),
            P("ex", None),
            P("ex", None),
        ),
        out_specs=P(("groups", "ex"), None),
        check_vma=False,
    )
```

```python
import functools

import jax
import jax.numpy as jnp
from jax import lax
from jax.experimental import pallas as pl
from jax.experimental.pallas import tpu as pltpu
from jax.sharding import PartitionSpec as P

SEQ = 64
VMEM_BYTES = 32 * 1024 * 1024
LOADED_ROWS = 128
FAR_PAD = 16
LEFT_OVER = 0.36 * 2.0**-8
LANES_BY_LANES = (((1,), (1,)), ((), ()))
HBM_SPEC = pl.BlockSpec(memory_space=pltpu.HBM)
VMEM_SPEC = pl.BlockSpec(memory_space=pltpu.VMEM)
PARAMS = pltpu.CompilerParams(vmem_limit_bytes=VMEM_BYTES)


def project_loaded_kernel(x_hbm, w_hbm, p_in_hbm, p_out_hbm, low_in_ref, low_out_ref, x_buf, w_buf, p_in, p_out, sems, p_sems):
    matrices = [
        pltpu.make_async_copy(p_in_hbm, p_in, p_sems.at[0]),
        pltpu.make_async_copy(p_out_hbm.at[:, pl.ds(0, p_out.shape[1])], p_out, p_sems.at[1]),
    ]
    chunks = []
    for hbm, buf, matrix, low_ref in ((x_hbm, x_buf, p_in, low_in_ref), (w_hbm, w_buf, p_out, low_out_ref)):
        count = buf.shape[0] // LOADED_ROWS if buf.shape[0] % LOADED_ROWS == 0 else 1
        for chunk in range(count):
            part = pl.ds(chunk * (buf.shape[0] // count), buf.shape[0] // count)
            copy = pltpu.make_async_copy(hbm.at[part, :], buf.at[part, :], sems.at[len(chunks)])
            chunks.append((part, buf, matrix, low_ref, copy, chunk == 0))
    for copy in matrices + [chunk[4] for chunk in chunks]:
        copy.start()
    for copy in matrices:
        copy.wait()
    step = min(1024, low_in_ref.shape[1])
    for part, buf, matrix, low_ref, copy, first in chunks:
        copy.wait()
        for column in range(0, low_ref.shape[1], step):
            columns = slice(column, column + step)
            product = jnp.dot(matrix[:, part], buf[part, columns], preferred_element_type=jnp.float32)
            low_ref[:, columns] = product if first else low_ref[:, columns] + product


def project_loaded(inputs, out_grads, proj_in_t, proj_out_t, rows):
    arrays = [pltpu.with_memory_space_constraint(a, pltpu.HBM) for a in (inputs, out_grads, proj_in_t, proj_out_t)]
    rank, tokens = proj_in_t.shape[0], inputs.shape[1]
    chunks = sum(a // LOADED_ROWS if a % LOADED_ROWS == 0 else 1 for a in (inputs.shape[0], rows))
    return pl.pallas_call(
        project_loaded_kernel,
        out_shape=[jax.ShapeDtypeStruct((rank, tokens), jnp.float32)] * 2,
        in_specs=[HBM_SPEC] * 4,
        out_specs=[VMEM_SPEC] * 2,
        scratch_shapes=[
            pltpu.VMEM(inputs.shape, jnp.bfloat16),
            pltpu.VMEM((rows, tokens), jnp.bfloat16),
            pltpu.VMEM(proj_in_t.shape, jnp.bfloat16),
            pltpu.VMEM((rank, max(rows, 128)), jnp.bfloat16),
            pltpu.SemaphoreType.DMA((chunks,)),
            pltpu.SemaphoreType.DMA((2,)),
        ],
        compiler_params=PARAMS,
        cost_estimate=pl.CostEstimate(
            flops=2 * rank * (inputs.shape[0] + rows) * tokens,
            bytes_accessed=2 * (inputs.shape[0] + rows) * tokens,
            transcendentals=0,
        ),
    )(*arrays)


def project_kernel(done, low_in_ref, low_out_ref, p_ref, w_ref, *refs):
    *given, kept_y, kept_here = refs
    given_y, given_here = given[:-1], given[-1:]
    here = lax.axis_index("ex")
    core, chip = lax.rem(here, 2), lax.div(here, 2)
    depth = kept_y.shape[0]
    rank, width = kept_y.shape[1] // 2, kept_y.shape[2]
    for flip, given_refs, kept_ref in ((1, given_y, kept_y), (0, given_here, kept_here)):
        for z in range(depth):
            place = lax.bitwise_xor(chip, 2 * z + flip)
            columns = pl.ds(pl.multiple_of(place * 2 * width, 2 * width), 2 * width)
            low_out = jnp.dot(p_ref[:, done:], w_ref[done:, columns], preferred_element_type=jnp.float32)
            low_out = low_out + low_out_ref[:, columns]
            given_ref = given_refs[z * len(given_refs) // depth]
            for lines, low in ((slice(0, rank), low_in_ref[:, columns]), (slice(rank, 2 * rank), low_out)):
                left, right = low[:, :width], low[:, width:]
                given_ref[z % given_ref.shape[0], lines, :] = jnp.where(core == 0, right, left)
                kept_ref[z, lines, :] = jnp.where(core == 0, left, right)


def project(inputs, out_grads, proj_in_t, proj_out_t, devices):
    rank, width = proj_in_t.shape[0], inputs.shape[1] // devices
    units = out_grads.shape[0]
    rows = LOADED_ROWS if units % LOADED_ROWS == 0 else 16
    lows = project_loaded(inputs, out_grads, proj_in_t, proj_out_t, rows)
    low = jax.ShapeDtypeStruct((devices // 4, 2 * rank, width), jnp.float32)
    half = jax.ShapeDtypeStruct((devices // 8, 2 * rank, width), jnp.float32)
    return pl.pallas_call(
        functools.partial(project_kernel, rows),
        out_shape=[half] * 2 + [low] * 3,
        in_specs=[VMEM_SPEC] * 4,
        out_specs=[VMEM_SPEC] * 5,
        compiler_params=PARAMS,
        cost_estimate=pl.CostEstimate(
            flops=2 * rank * out_grads.size, bytes_accessed=2 * out_grads.size, transcendentals=0
        ),
    )(*lows, proj_out_t, out_grads)


def put_coded(out_ref, low):
    rows = low.shape[0]
    rounded = low.astype(jnp.bfloat16)
    out_ref[:rows, :] = rounded
    above = jnp.where(low > rounded.astype(jnp.float32), 1.0, 0.0)
    part = rows // 8
    word = above[:part, :]
    for index in range(1, 8):
        word = word + 2.0**index * above[index * part : (index + 1) * part, :]
    out_ref[rows : rows + part, :] = word.astype(jnp.bfloat16)


def add_coded(total, rows, ref):
    part = rows // 8
    word = ref[rows : rows + part, :].astype(jnp.float32)
    parts = []
    for index in reversed(range(8)):
        above = jnp.floor(word * 0.5**index)
        word = word - above * 2.0**index
        rounded = ref[index * part : (index + 1) * part, :].astype(jnp.float32)
        left = jnp.abs(rounded) * ((2.0 * LEFT_OVER) * above - LEFT_OVER)
        parts.append((slice(index * part, (index + 1) * part), total(index * part, part) + rounded + left))
    return parts


def add_given_kernel(kept_ref, *refs):
    *came_refs, out_ref = refs
    half = came_refs[0].shape[0]
    for block in range(out_ref.shape[0]):
        put_coded(out_ref.at[block], kept_ref[block] + came_refs[block // half][block % half])


def add_given(kept, came):
    blocks, rows, width = kept.shape
    return pl.pallas_call(
        add_given_kernel,
        out_shape=jax.ShapeDtypeStruct((blocks, rows // 8 * 9, width), jnp.bfloat16),
        compiler_params=PARAMS,
    )(kept, *came)


def add_kept_kernel(kept_ref, came_ref, across_ref, own_ref, *out_refs):
    for z in range(len(out_refs) + 1):
        def here(first, rows):
            return kept_ref[z, first : first + rows, :] + came_ref[z, first : first + rows, :]

        sums = add_coded(here, kept_ref.shape[1], across_ref.at[z])
        if z == 0:
            for rows, total in sums:
                own_ref[rows, :] = total
        else:
            put_coded(out_refs[len(out_refs) - z], jnp.concatenate([total for _, total in reversed(sums)], axis=0))


def add_kept(kept, came, across):
    depth, rows, width = kept.shape
    own = jax.ShapeDtypeStruct((rows, width), jnp.float32)
    heights = [rows // 8 * 9 + (FAR_PAD if z > 2 else 0) for z in reversed(range(1, depth))]
    return pl.pallas_call(
        add_kept_kernel,
        out_shape=[own] + [jax.ShapeDtypeStruct((height, width), jnp.bfloat16) for height in heights],
        compiler_params=PARAMS,
    )(kept, came, across)


def stack_kernel(left_ref, right_ref, out_ref):
    out_ref[: left_ref.shape[0]] = left_ref[...]
    out_ref[left_ref.shape[0] :] = right_ref[...]


def stack(left, right):
    return pl.pallas_call(
        stack_kernel,
        out_shape=jax.ShapeDtypeStruct((2 * left.shape[0],) + left.shape[1:], left.dtype),
        compiler_params=PARAMS,
    )(left, right)


def add_scores(queries_ref, chips, place, grads, sums_ref):
    examples, half_rank, lanes = grads.shape
    held = queries_ref.shape[1]
    step = 4 if len(chips) % 4 == 0 else 2
    here = lax.div(lax.axis_index("ex"), 2)
    for first in range(0, len(chips), step):
        sums = [jnp.zeros((step * held, lanes), jnp.float32) for _ in range(examples)]
        for k in range(half_rank):
            query = queries_ref[first : first + step, :, k * lanes : (k + 1) * lanes].astype(jnp.float32)
            query = query.reshape(step * held, lanes)
            for n in range(examples):
                sums[n] = sums[n] + query * grads[n, k : k + 1, :]
        for part in range(step):
            source = lax.bitwise_xor(here, chips[first + part])
            for n in range(examples):
                sums_ref[n, source, place] = sums[n][part * held : (part + 1) * held, :]


def first_score_kernel(parts_count, held, *refs):
    part_refs, query_refs = refs[:parts_count], refs[parts_count : parts_count + len(held)]
    grads_ref, sums_ref, total_ref = refs[parts_count + len(held) :]
    rank, tokens = total_ref.shape[0] // 2, total_ref.shape[1]
    core = lax.rem(lax.axis_index("ex"), 2)
    total_ref[...] = part_refs[0][...]
    for part_ref in part_refs[1:]:
        for rows, total in add_coded(lambda first, count: total_ref[first : first + count, :], 2 * rank, part_ref):
            total_ref[rows, :] = total
    even = total_ref[pl.ds(rank, rank // 2, stride=2), :]
    odd = total_ref[pl.ds(rank + 1, rank // 2, stride=2), :]
    token = lax.broadcasted_iota(jnp.int32, (rank, tokens), 1)
    for n in range(tokens // SEQ):
        mine = jnp.where((token >= n * SEQ) & (token < (n + 1) * SEQ), total_ref[:rank, :], 0.0)
        for side, rows in enumerate((even, odd)):
            grads_ref[n, :, side * rank : (side + 1) * rank] = lax.dot_general(
                rows, mine, LANES_BY_LANES, precision=lax.Precision.HIGHEST, preferred_element_type=jnp.float32
            )
    sums_ref[...] = jnp.zeros_like(sums_ref)
    for queries_ref, (other, chips) in zip(query_refs, held):
        add_scores(queries_ref, chips, lax.rem(core + other, 2), grads_ref, sums_ref)


def last_score_kernel(chips, grads_ref, before_ref, queries_ref, out_ref, sums_ref):
    core = lax.rem(lax.axis_index("ex"), 2)
    sums_ref[...] = before_ref[...]
    add_scores(queries_ref, chips, lax.rem(core + 1, 2), grads_ref, sums_ref)
    examples, *rows, lanes = sums_ref.shape
    sums = sums_ref[...].reshape(examples * out_ref.shape[1], lanes)
    high = sums.astype(jnp.bfloat16)
    low = (sums - high.astype(jnp.float32)).astype(jnp.bfloat16)
    ones = jnp.ones((16, lanes), jnp.bfloat16)
    row = sum(lax.dot_general(ones, part, LANES_BY_LANES, preferred_element_type=jnp.float32) for part in (high, low))
    for n in range(examples):
        out_ref[n : n + 1, :] = row[0:1, n * out_ref.shape[1] : (n + 1) * out_ref.shape[1]]


def first_scores(parts, queries, held, rank):
    tokens = parts[0].shape[1]
    examples = tokens // SEQ
    chips = 2 * queries[0].shape[0]
    return pl.pallas_call(
        functools.partial(first_score_kernel, len(parts), held),
        out_shape=[
            jax.ShapeDtypeStruct((examples, rank // 2, 2 * rank), jnp.float32),
            jax.ShapeDtypeStruct((examples, chips, 2, queries[0].shape[1], 2 * rank), jnp.float32),
        ],
        scratch_shapes=[pltpu.VMEM((2 * rank, tokens), jnp.float32)],
        compiler_params=PARAMS,
    )(*parts, *queries)


def last_scores(grads, sums, queries, chips):
    examples, all_chips, cores, held, _ = sums.shape
    return pl.pallas_call(
        functools.partial(last_score_kernel, chips),
        out_shape=jax.ShapeDtypeStruct((examples, all_chips * cores * held), jnp.float32),
        scratch_shapes=[pltpu.VMEM(sums.shape, jnp.float32)],
        compiler_params=PARAMS,
    )(grads, sums, queries)


def shards(inputs, out_grads, proj_in, proj_out, queries):
    devices = lax.axis_size("ex")
    chips = devices // 2
    depth = chips // 2
    rank = proj_in.shape[1]
    together = lax.optimization_barrier

    def swap(array, chip=0, core=0):
        distance = 2 * chip + core
        return lax.ppermute(array, "ex", [(i, i ^ distance) for i in range(devices)])

    steps = [chips - 2] + [1 << bit for bit in reversed(range(chips.bit_length() - 2))]
    held, reach = queries[None], [0]
    came_held = swap(held, chip=steps[0])
    lows = project(inputs, out_grads, proj_in.T, proj_out.T, devices)
    *given_y, given, kept_y, kept = lows
    came_y = [swap(array, core=1) for array in given_y]
    came = swap(given, core=1)
    for last, step in zip(steps, steps[1:-1]):
        held, reach = stack(held, came_held), reach + [chip ^ last for chip in reach]
        came_held = swap(held, chip=step)
    across = swap(add_given(kept_y, came_y), chip=1)
    early, early_reach = held, reach
    late, late_reach = came_held, [chip ^ steps[-2] for chip in reach]
    held, reach = stack(early, late), early_reach + late_reach
    came_held = swap(held, chip=1)
    other_early = swap(early, core=1)
    across, came, other_early = together((across, came, other_early))

    parts = list(add_kept(kept, came, across))
    late, parts = together((late, parts))
    other_late = swap(late, core=1)
    parts[1:] = [swap(part, chip=2 * z) for z, part in zip(reversed(range(1, depth)), parts[1:])]
    came_held, other_late, parts = together((came_held, other_late, parts))
    other_came = swap(came_held, core=1)
    reach_y = [chip ^ 1 for chip in reach]
    queries = [held, other_early, other_late, came_held]
    reaches = [(0, reach), (1, early_reach), (1, late_reach), (0, reach_y)]
    grads, scores = first_scores(parts, queries, reaches, rank)
    return last_scores(grads, scores, other_came, reach_y)


def solution(mesh):
    return jax.shard_map(
        shards,
        mesh=mesh,
        in_specs=(
            P("ex", "groups"),
            P("ex", "groups"),
            P("ex", None),
            P("ex", None),
            P("ex", None),
        ),
        out_specs=P(("groups", "ex"), None),
        check_vma=False,
    )
```

```python
import functools

import jax
import jax.numpy as jnp
from jax import lax
from jax.experimental import pallas as pl
from jax.experimental.pallas import tpu as pltpu
from jax.sharding import PartitionSpec as P

SEQ = 64
VMEM_BYTES = 32 * 1024 * 1024
LOADED_ROWS = 128
PAD = 16
LEFT_OVER = 0.36 * 2.0**-8
LANES_BY_LANES = (((1,), (1,)), ((), ()))
HBM_SPEC = pl.BlockSpec(memory_space=pltpu.HBM)
VMEM_SPEC = pl.BlockSpec(memory_space=pltpu.VMEM)
PARAMS = pltpu.CompilerParams(vmem_limit_bytes=VMEM_BYTES)


def project_loaded_kernel(x_hbm, w_hbm, p_in_hbm, p_out_hbm, low_in_ref, low_out_ref, x_buf, w_buf, p_in, p_out, sems, p_sems):
    matrices = [
        pltpu.make_async_copy(p_in_hbm, p_in, p_sems.at[0]),
        pltpu.make_async_copy(p_out_hbm.at[:, pl.ds(0, p_out.shape[1])], p_out, p_sems.at[1]),
    ]
    chunks = []
    for hbm, buf, matrix, low_ref in ((x_hbm, x_buf, p_in, low_in_ref), (w_hbm, w_buf, p_out, low_out_ref)):
        count = buf.shape[0] // LOADED_ROWS if buf.shape[0] % LOADED_ROWS == 0 else 1
        for chunk in range(count):
            part = pl.ds(chunk * (buf.shape[0] // count), buf.shape[0] // count)
            copy = pltpu.make_async_copy(hbm.at[part, :], buf.at[part, :], sems.at[len(chunks)])
            chunks.append((part, buf, matrix, low_ref, copy, chunk == 0))
    for copy in matrices + [chunk[4] for chunk in chunks]:
        copy.start()
    for copy in matrices:
        copy.wait()
    step = min(1024, low_in_ref.shape[1])
    for part, buf, matrix, low_ref, copy, first in chunks:
        copy.wait()
        for column in range(0, low_ref.shape[1], step):
            columns = slice(column, column + step)
            product = jnp.dot(matrix[:, part], buf[part, columns], preferred_element_type=jnp.float32)
            low_ref[:, columns] = product if first else low_ref[:, columns] + product


def project_loaded(inputs, out_grads, proj_in_t, proj_out_t, rows):
    arrays = [pltpu.with_memory_space_constraint(a, pltpu.HBM) for a in (inputs, out_grads, proj_in_t, proj_out_t)]
    rank, tokens = proj_in_t.shape[0], inputs.shape[1]
    chunks = sum(a // LOADED_ROWS if a % LOADED_ROWS == 0 else 1 for a in (inputs.shape[0], rows))
    return pl.pallas_call(
        project_loaded_kernel,
        out_shape=[jax.ShapeDtypeStruct((rank, tokens), jnp.float32)] * 2,
        in_specs=[HBM_SPEC] * 4,
        out_specs=[VMEM_SPEC] * 2,
        scratch_shapes=[
            pltpu.VMEM(inputs.shape, jnp.bfloat16),
            pltpu.VMEM((rows, tokens), jnp.bfloat16),
            pltpu.VMEM(proj_in_t.shape, jnp.bfloat16),
            pltpu.VMEM((rank, max(rows, 128)), jnp.bfloat16),
            pltpu.SemaphoreType.DMA((chunks,)),
            pltpu.SemaphoreType.DMA((2,)),
        ],
        compiler_params=PARAMS,
        cost_estimate=pl.CostEstimate(
            flops=2 * rank * (inputs.shape[0] + rows) * tokens,
            bytes_accessed=2 * (inputs.shape[0] + rows) * tokens,
            transcendentals=0,
        ),
    )(*arrays)


def project_kernel(done, low_in_ref, low_out_ref, p_ref, w_ref, *refs):
    *given, kept_y, kept_here = refs
    given_y, given_here = given[:-1], given[-1:]
    here = lax.axis_index("ex")
    core, chip = lax.rem(here, 2), lax.div(here, 2)
    depth = kept_y.shape[0]
    rank, width = kept_y.shape[1] // 2, kept_y.shape[2]
    for flip, given_refs, kept_ref in ((1, given_y, kept_y), (0, given_here, kept_here)):
        for z in range(depth):
            place = lax.bitwise_xor(chip, 2 * z + flip)
            columns = pl.ds(pl.multiple_of(place * 2 * width, 2 * width), 2 * width)
            low_out = jnp.dot(p_ref[:, done:], w_ref[done:, columns], preferred_element_type=jnp.float32)
            low_out = low_out + low_out_ref[:, columns]
            given_ref = given_refs[z * len(given_refs) // depth]
            for lines, low in ((slice(0, rank), low_in_ref[:, columns]), (slice(rank, 2 * rank), low_out)):
                left, right = low[:, :width], low[:, width:]
                given_ref[z % given_ref.shape[0], lines, :] = jnp.where(core == 0, right, left)
                kept_ref[z, lines, :] = jnp.where(core == 0, left, right)


def project(inputs, out_grads, proj_in_t, proj_out_t, devices):
    rank, width = proj_in_t.shape[0], inputs.shape[1] // devices
    units = out_grads.shape[0]
    rows = LOADED_ROWS if units % LOADED_ROWS == 0 else 16
    lows = project_loaded(inputs, out_grads, proj_in_t, proj_out_t, rows)
    low = jax.ShapeDtypeStruct((devices // 4, 2 * rank, width), jnp.float32)
    half = jax.ShapeDtypeStruct((devices // 8, 2 * rank, width), jnp.float32)
    return pl.pallas_call(
        functools.partial(project_kernel, rows),
        out_shape=[half] * 2 + [low] * 3,
        in_specs=[VMEM_SPEC] * 4,
        out_specs=[VMEM_SPEC] * 5,
        compiler_params=PARAMS,
        cost_estimate=pl.CostEstimate(
            flops=2 * rank * out_grads.size, bytes_accessed=2 * out_grads.size, transcendentals=0
        ),
    )(*lows, proj_out_t, out_grads)


def put_coded(out_ref, low):
    rows = low.shape[0]
    rounded = low.astype(jnp.bfloat16)
    out_ref[:rows, :] = rounded
    above = jnp.where(low > rounded.astype(jnp.float32), 1.0, 0.0)
    part = rows // 8
    word = above[:part, :]
    for index in range(1, 8):
        word = word + 2.0**index * above[index * part : (index + 1) * part, :]
    out_ref[rows : rows + part, :] = word.astype(jnp.bfloat16)


def add_coded(total, rows, ref):
    part = rows // 8
    word = ref[rows : rows + part, :].astype(jnp.float32)
    parts = []
    for index in reversed(range(8)):
        above = jnp.floor(word * 0.5**index)
        word = word - above * 2.0**index
        rounded = ref[index * part : (index + 1) * part, :].astype(jnp.float32)
        left = jnp.abs(rounded) * ((2.0 * LEFT_OVER) * above - LEFT_OVER)
        parts.append((slice(index * part, (index + 1) * part), total(index * part, part) + rounded + left))
    return parts


def add_given_kernel(kept_ref, *refs):
    *came_refs, out_ref = refs
    half = came_refs[0].shape[0]
    for block in range(out_ref.shape[0]):
        put_coded(out_ref.at[block], kept_ref[block] + came_refs[block // half][block % half])


def add_given(kept, came):
    blocks, rows, width = kept.shape
    return pl.pallas_call(
        add_given_kernel,
        out_shape=jax.ShapeDtypeStruct((blocks, rows // 8 * 9, width), jnp.bfloat16),
        compiler_params=PARAMS,
    )(kept, *came)


def add_kept_kernel(kept_ref, came_ref, across_ref, own_ref, *out_refs):
    for z in range(len(out_refs) + 1):
        def here(first, rows):
            return kept_ref[z, first : first + rows, :] + came_ref[z, first : first + rows, :]

        sums = add_coded(here, kept_ref.shape[1], across_ref.at[z])
        if z == 0:
            for rows, total in sums:
                own_ref[rows, :] = total
        else:
            put_coded(out_refs[len(out_refs) - z], jnp.concatenate([total for _, total in reversed(sums)], axis=0))


def add_kept(kept, came, across):
    depth, rows, width = kept.shape
    own = jax.ShapeDtypeStruct((rows, width), jnp.float32)
    heights = [rows // 8 * 9 + (2 * PAD if z > 2 else PAD if z == 1 else 0) for z in reversed(range(1, depth))]
    return pl.pallas_call(
        add_kept_kernel,
        out_shape=[own] + [jax.ShapeDtypeStruct((height, width), jnp.bfloat16) for height in heights],
        compiler_params=PARAMS,
    )(kept, came, across)


def stack_kernel(left_ref, right_ref, out_ref):
    out_ref[: left_ref.shape[0]] = left_ref[...]
    out_ref[left_ref.shape[0] :] = right_ref[...]


def stack(left, right):
    return pl.pallas_call(
        stack_kernel,
        out_shape=jax.ShapeDtypeStruct((2 * left.shape[0],) + left.shape[1:], left.dtype),
        compiler_params=PARAMS,
    )(left, right)


def add_scores(queries_ref, chips, place, grads, sums_ref):
    examples, half_rank, lanes = grads.shape
    held = queries_ref.shape[1]
    step = 4 if len(chips) % 4 == 0 else 2
    here = lax.div(lax.axis_index("ex"), 2)
    for first in range(0, len(chips), step):
        sums = [jnp.zeros((step * held, lanes), jnp.float32) for _ in range(examples)]
        for k in range(half_rank):
            query = queries_ref[first : first + step, :, k * lanes : (k + 1) * lanes].astype(jnp.float32)
            query = query.reshape(step * held, lanes)
            for n in range(examples):
                sums[n] = sums[n] + query * grads[n, k : k + 1, :]
        for part in range(step):
            source = lax.bitwise_xor(here, chips[first + part])
            for n in range(examples):
                sums_ref[n, source, place] = sums[n][part * held : (part + 1) * held, :]


def first_score_kernel(parts_count, held, *refs):
    part_refs, query_refs = refs[:parts_count], refs[parts_count : parts_count + len(held)]
    grads_ref, sums_ref, total_ref = refs[parts_count + len(held) :]
    rank, tokens = total_ref.shape[0] // 2, total_ref.shape[1]
    core = lax.rem(lax.axis_index("ex"), 2)
    total_ref[...] = part_refs[0][...]
    for part_ref in part_refs[1:]:
        for rows, total in add_coded(lambda first, count: total_ref[first : first + count, :], 2 * rank, part_ref):
            total_ref[rows, :] = total
    even = total_ref[pl.ds(rank, rank // 2, stride=2), :]
    odd = total_ref[pl.ds(rank + 1, rank // 2, stride=2), :]
    token = lax.broadcasted_iota(jnp.int32, (rank, tokens), 1)
    for n in range(tokens // SEQ):
        mine = jnp.where((token >= n * SEQ) & (token < (n + 1) * SEQ), total_ref[:rank, :], 0.0)
        for side, rows in enumerate((even, odd)):
            grads_ref[n, :, side * rank : (side + 1) * rank] = lax.dot_general(
                rows, mine, LANES_BY_LANES, precision=lax.Precision.HIGHEST, preferred_element_type=jnp.float32
            )
    sums_ref[...] = jnp.zeros_like(sums_ref)
    for queries_ref, (other, chips) in zip(query_refs, held):
        add_scores(queries_ref, chips, lax.rem(core + other, 2), grads_ref, sums_ref)


def last_score_kernel(chips, grads_ref, before_ref, queries_ref, out_ref, sums_ref):
    core = lax.rem(lax.axis_index("ex"), 2)
    sums_ref[...] = before_ref[...]
    add_scores(queries_ref, chips, lax.rem(core + 1, 2), grads_ref, sums_ref)
    examples, *rows, lanes = sums_ref.shape
    sums = sums_ref[...].reshape(examples * out_ref.shape[1], lanes)
    high = sums.astype(jnp.bfloat16)
    low = (sums - high.astype(jnp.float32)).astype(jnp.bfloat16)
    ones = jnp.ones((16, lanes), jnp.bfloat16)
    row = sum(lax.dot_general(ones, part, LANES_BY_LANES, preferred_element_type=jnp.float32) for part in (high, low))
    for n in range(examples):
        out_ref[n : n + 1, :] = row[0:1, n * out_ref.shape[1] : (n + 1) * out_ref.shape[1]]


def first_scores(parts, queries, held, rank):
    tokens = parts[0].shape[1]
    examples = tokens // SEQ
    chips = 2 * queries[0].shape[0]
    return pl.pallas_call(
        functools.partial(first_score_kernel, len(parts), held),
        out_shape=[
            jax.ShapeDtypeStruct((examples, rank // 2, 2 * rank), jnp.float32),
            jax.ShapeDtypeStruct((examples, chips, 2, queries[0].shape[1], 2 * rank), jnp.float32),
        ],
        scratch_shapes=[pltpu.VMEM((2 * rank, tokens), jnp.float32)],
        compiler_params=PARAMS,
    )(*parts, *queries)


def last_scores(grads, sums, queries, chips):
    examples, all_chips, cores, held, _ = sums.shape
    return pl.pallas_call(
        functools.partial(last_score_kernel, chips),
        out_shape=jax.ShapeDtypeStruct((examples, all_chips * cores * held), jnp.float32),
        scratch_shapes=[pltpu.VMEM(sums.shape, jnp.float32)],
        compiler_params=PARAMS,
    )(grads, sums, queries)


def shards(inputs, out_grads, proj_in, proj_out, queries):
    devices = lax.axis_size("ex")
    chips = devices // 2
    depth = chips // 2
    rank = proj_in.shape[1]
    together = lax.optimization_barrier

    def swap(array, chip=0, core=0):
        distance = 2 * chip + core
        return lax.ppermute(array, "ex", [(i, i ^ distance) for i in range(devices)])

    steps = [1 << bit for bit in reversed(range(chips.bit_length() - 1))]
    held, reach = queries[None], [0]
    came_held = swap(held, chip=steps[0])
    lows = project(inputs, out_grads, proj_in.T, proj_out.T, devices)
    *given_y, given, kept_y, kept = lows
    came_y = [swap(array, core=1) for array in given_y]
    came = swap(given, core=1)
    for last, step in zip(steps, steps[1:-1]):
        held, reach = stack(held, came_held), reach + [chip ^ last for chip in reach]
        came_held = swap(held, chip=step)
    across = swap(add_given(kept_y, came_y), chip=1)
    early, early_reach = held, reach
    late, late_reach = came_held, [chip ^ steps[-2] for chip in reach]
    held, reach = stack(early, late), early_reach + late_reach
    came_held = swap(held, chip=1)
    other_early = swap(early, core=1)
    across, came, other_early = together((across, came, other_early))

    parts = list(add_kept(kept, came, across))
    late, parts = together((late, parts))
    other_late = swap(late, core=1)
    parts[1:] = [swap(part, chip=2 * z) for z, part in zip(reversed(range(1, depth)), parts[1:])]
    came_held, other_late, parts = together((came_held, other_late, parts))
    other_came = swap(came_held, core=1)
    reach_y = [chip ^ 1 for chip in reach]
    queries = [held, other_early, other_late, came_held]
    reaches = [(0, reach), (1, early_reach), (1, late_reach), (0, reach_y)]
    grads, scores = first_scores(parts, queries, reaches, rank)
    return last_scores(grads, scores, other_came, reach_y)


def solution(mesh):
    return jax.shard_map(
        shards,
        mesh=mesh,
        in_specs=(
            P("ex", "groups"),
            P("ex", "groups"),
            P("ex", None),
            P("ex", None),
            P("ex", None),
        ),
        out_specs=P(("groups", "ex"), None),
        check_vma=False,
    )
```

```python
import functools

import jax
import jax.numpy as jnp
from jax import lax
from jax.experimental import pallas as pl
from jax.experimental.pallas import tpu as pltpu
from jax.sharding import PartitionSpec as P

SEQ = 64
VMEM_BYTES = 32 * 1024 * 1024
LOADED_ROWS = 128
FAR_PAD = 16
LEFT_OVER = 0.36 * 2.0**-8
LANES_BY_LANES = (((1,), (1,)), ((), ()))
HBM_SPEC = pl.BlockSpec(memory_space=pltpu.HBM)
VMEM_SPEC = pl.BlockSpec(memory_space=pltpu.VMEM)
PARAMS = pltpu.CompilerParams(vmem_limit_bytes=VMEM_BYTES)


def project_loaded_kernel(x_hbm, w_hbm, p_in_hbm, p_out_hbm, low_in_ref, low_out_ref, x_buf, w_buf, p_in, p_out, sems, p_sems):
    matrices = [
        pltpu.make_async_copy(p_in_hbm, p_in, p_sems.at[0]),
        pltpu.make_async_copy(p_out_hbm.at[:, pl.ds(0, p_out.shape[1])], p_out, p_sems.at[1]),
    ]
    chunks = []
    for hbm, buf, matrix, low_ref in ((x_hbm, x_buf, p_in, low_in_ref), (w_hbm, w_buf, p_out, low_out_ref)):
        count = buf.shape[0] // LOADED_ROWS if buf.shape[0] % LOADED_ROWS == 0 else 1
        for chunk in range(count):
            part = pl.ds(chunk * (buf.shape[0] // count), buf.shape[0] // count)
            copy = pltpu.make_async_copy(hbm.at[part, :], buf.at[part, :], sems.at[len(chunks)])
            chunks.append((part, buf, matrix, low_ref, copy, chunk == 0))
    for copy in matrices + [chunk[4] for chunk in chunks]:
        copy.start()
    for copy in matrices:
        copy.wait()
    step = min(1024, low_in_ref.shape[1])
    for part, buf, matrix, low_ref, copy, first in chunks:
        copy.wait()
        for column in range(0, low_ref.shape[1], step):
            columns = slice(column, column + step)
            product = jnp.dot(matrix[:, part], buf[part, columns], preferred_element_type=jnp.float32)
            low_ref[:, columns] = product if first else low_ref[:, columns] + product


def project_loaded(inputs, out_grads, proj_in_t, proj_out_t, rows):
    arrays = [pltpu.with_memory_space_constraint(a, pltpu.HBM) for a in (inputs, out_grads, proj_in_t, proj_out_t)]
    rank, tokens = proj_in_t.shape[0], inputs.shape[1]
    chunks = sum(a // LOADED_ROWS if a % LOADED_ROWS == 0 else 1 for a in (inputs.shape[0], rows))
    return pl.pallas_call(
        project_loaded_kernel,
        out_shape=[jax.ShapeDtypeStruct((rank, tokens), jnp.float32)] * 2,
        in_specs=[HBM_SPEC] * 4,
        out_specs=[VMEM_SPEC] * 2,
        scratch_shapes=[
            pltpu.VMEM(inputs.shape, jnp.bfloat16),
            pltpu.VMEM((rows, tokens), jnp.bfloat16),
            pltpu.VMEM(proj_in_t.shape, jnp.bfloat16),
            pltpu.VMEM((rank, max(rows, 128)), jnp.bfloat16),
            pltpu.SemaphoreType.DMA((chunks,)),
            pltpu.SemaphoreType.DMA((2,)),
        ],
        compiler_params=PARAMS,
        cost_estimate=pl.CostEstimate(
            flops=2 * rank * (inputs.shape[0] + rows) * tokens,
            bytes_accessed=2 * (inputs.shape[0] + rows) * tokens,
            transcendentals=0,
        ),
    )(*arrays)


def project_kernel(done, flip, low_in_ref, low_out_ref, p_ref, w_ref, *refs):
    *given_refs, kept_ref = refs
    here = lax.axis_index("ex")
    core, chip = lax.rem(here, 2), lax.div(here, 2)
    depth = kept_ref.shape[0]
    rank, width = kept_ref.shape[1] // 2, kept_ref.shape[2]
    for z in range(depth):
        place = lax.bitwise_xor(chip, 2 * z + flip)
        columns = pl.ds(pl.multiple_of(place * 2 * width, 2 * width), 2 * width)
        low_out = jnp.dot(p_ref[:, done:], w_ref[done:, columns], preferred_element_type=jnp.float32)
        low_out = low_out + low_out_ref[:, columns]
        given_ref = given_refs[z * len(given_refs) // depth]
        for lines, low in ((slice(0, rank), low_in_ref[:, columns]), (slice(rank, 2 * rank), low_out)):
            left, right = low[:, :width], low[:, width:]
            given_ref[z % given_ref.shape[0], lines, :] = jnp.where(core == 0, right, left)
            kept_ref[z, lines, :] = jnp.where(core == 0, left, right)


def project(inputs, out_grads, proj_in_t, proj_out_t, devices):
    rank, width = proj_in_t.shape[0], inputs.shape[1] // devices
    units = out_grads.shape[0]
    rows = LOADED_ROWS if units % LOADED_ROWS == 0 else 16
    lows = project_loaded(inputs, out_grads, proj_in_t, proj_out_t, rows)

    def part(flip, given_count):
        low = jax.ShapeDtypeStruct((devices // 4, 2 * rank, width), jnp.float32)
        given = jax.ShapeDtypeStruct((devices // 4 // given_count, 2 * rank, width), jnp.float32)
        *given, kept = pl.pallas_call(
            functools.partial(project_kernel, rows, flip),
            out_shape=[given] * given_count + [low],
            in_specs=[VMEM_SPEC] * 4,
            out_specs=[VMEM_SPEC] * (given_count + 1),
            compiler_params=PARAMS,
            cost_estimate=pl.CostEstimate(
                flops=rank * out_grads.size, bytes_accessed=out_grads.size, transcendentals=0
            ),
        )(*lows, proj_out_t, out_grads)
        return given, kept

    return part(1, 2), part(0, 1)


def put_coded(out_ref, low):
    rows = low.shape[0]
    rounded = low.astype(jnp.bfloat16)
    out_ref[:rows, :] = rounded
    above = jnp.where(low > rounded.astype(jnp.float32), 1.0, 0.0)
    part = rows // 8
    word = above[:part, :]
    for index in range(1, 8):
        word = word + 2.0**index * above[index * part : (index + 1) * part, :]
    out_ref[rows : rows + part, :] = word.astype(jnp.bfloat16)


def add_coded(total, rows, ref):
    part = rows // 8
    word = ref[rows : rows + part, :].astype(jnp.float32)
    parts = []
    for index in reversed(range(8)):
        above = jnp.floor(word * 0.5**index)
        word = word - above * 2.0**index
        rounded = ref[index * part : (index + 1) * part, :].astype(jnp.float32)
        left = jnp.abs(rounded) * ((2.0 * LEFT_OVER) * above - LEFT_OVER)
        parts.append((slice(index * part, (index + 1) * part), total(index * part, part) + rounded + left))
    return parts


def add_given_kernel(kept_ref, *refs):
    *came_refs, out_ref = refs
    half = came_refs[0].shape[0]
    for block in range(out_ref.shape[0]):
        put_coded(out_ref.at[block], kept_ref[block] + came_refs[block // half][block % half])


def add_given(kept, came):
    blocks, rows, width = kept.shape
    return pl.pallas_call(
        add_given_kernel,
        out_shape=jax.ShapeDtypeStruct((blocks, rows // 8 * 9, width), jnp.bfloat16),
        compiler_params=PARAMS,
    )(kept, *came)


def add_kept_kernel(kept_ref, came_ref, across_ref, own_ref, *out_refs):
    for z in range(len(out_refs) + 1):
        def here(first, rows):
            return kept_ref[z, first : first + rows, :] + came_ref[z, first : first + rows, :]

        sums = add_coded(here, kept_ref.shape[1], across_ref.at[z])
        if z == 0:
            for rows, total in sums:
                own_ref[rows, :] = total
        else:
            put_coded(out_refs[len(out_refs) - z], jnp.concatenate([total for _, total in reversed(sums)], axis=0))


def add_kept(kept, came, across):
    depth, rows, width = kept.shape
    own = jax.ShapeDtypeStruct((rows, width), jnp.float32)
    heights = [rows // 8 * 9 + (FAR_PAD if z > 2 else 0) for z in reversed(range(1, depth))]
    return pl.pallas_call(
        add_kept_kernel,
        out_shape=[own] + [jax.ShapeDtypeStruct((height, width), jnp.bfloat16) for height in heights],
        compiler_params=PARAMS,
    )(kept, came, across)


def stack_kernel(left_ref, right_ref, out_ref):
    out_ref[: left_ref.shape[0]] = left_ref[...]
    out_ref[left_ref.shape[0] :] = right_ref[...]


def stack(left, right):
    return pl.pallas_call(
        stack_kernel,
        out_shape=jax.ShapeDtypeStruct((2 * left.shape[0],) + left.shape[1:], left.dtype),
        compiler_params=PARAMS,
    )(left, right)


def add_scores(queries_ref, chips, place, grads, sums_ref):
    examples, half_rank, lanes = grads.shape
    held = queries_ref.shape[1]
    step = 4 if len(chips) % 4 == 0 else 2
    here = lax.div(lax.axis_index("ex"), 2)
    for first in range(0, len(chips), step):
        sums = [jnp.zeros((step * held, lanes), jnp.float32) for _ in range(examples)]
        for k in range(half_rank):
            query = queries_ref[first : first + step, :, k * lanes : (k + 1) * lanes].astype(jnp.float32)
            query = query.reshape(step * held, lanes)
            for n in range(examples):
                sums[n] = sums[n] + query * grads[n, k : k + 1, :]
        for part in range(step):
            source = lax.bitwise_xor(here, chips[first + part])
            for n in range(examples):
                sums_ref[n, source, place] = sums[n][part * held : (part + 1) * held, :]


def first_score_kernel(parts_count, held, *refs):
    part_refs, query_refs = refs[:parts_count], refs[parts_count : parts_count + len(held)]
    grads_ref, sums_ref, total_ref = refs[parts_count + len(held) :]
    rank, tokens = total_ref.shape[0] // 2, total_ref.shape[1]
    core = lax.rem(lax.axis_index("ex"), 2)
    total_ref[...] = part_refs[0][...]
    for part_ref in part_refs[1:]:
        for rows, total in add_coded(lambda first, count: total_ref[first : first + count, :], 2 * rank, part_ref):
            total_ref[rows, :] = total
    even = total_ref[pl.ds(rank, rank // 2, stride=2), :]
    odd = total_ref[pl.ds(rank + 1, rank // 2, stride=2), :]
    token = lax.broadcasted_iota(jnp.int32, (rank, tokens), 1)
    for n in range(tokens // SEQ):
        mine = jnp.where((token >= n * SEQ) & (token < (n + 1) * SEQ), total_ref[:rank, :], 0.0)
        for side, rows in enumerate((even, odd)):
            grads_ref[n, :, side * rank : (side + 1) * rank] = lax.dot_general(
                rows, mine, LANES_BY_LANES, precision=lax.Precision.HIGHEST, preferred_element_type=jnp.float32
            )
    sums_ref[...] = jnp.zeros_like(sums_ref)
    for queries_ref, (other, chips) in zip(query_refs, held):
        add_scores(queries_ref, chips, lax.rem(core + other, 2), grads_ref, sums_ref)


def last_score_kernel(chips, grads_ref, before_ref, queries_ref, out_ref, sums_ref):
    core = lax.rem(lax.axis_index("ex"), 2)
    sums_ref[...] = before_ref[...]
    add_scores(queries_ref, chips, lax.rem(core + 1, 2), grads_ref, sums_ref)
    examples, *rows, lanes = sums_ref.shape
    sums = sums_ref[...].reshape(examples * out_ref.shape[1], lanes)
    high = sums.astype(jnp.bfloat16)
    low = (sums - high.astype(jnp.float32)).astype(jnp.bfloat16)
    ones = jnp.ones((16, lanes), jnp.bfloat16)
    row = sum(lax.dot_general(ones, part, LANES_BY_LANES, preferred_element_type=jnp.float32) for part in (high, low))
    for n in range(examples):
        out_ref[n : n + 1, :] = row[0:1, n * out_ref.shape[1] : (n + 1) * out_ref.shape[1]]


def first_scores(parts, queries, held, rank):
    tokens = parts[0].shape[1]
    examples = tokens // SEQ
    chips = 2 * queries[0].shape[0]
    return pl.pallas_call(
        functools.partial(first_score_kernel, len(parts), held),
        out_shape=[
            jax.ShapeDtypeStruct((examples, rank // 2, 2 * rank), jnp.float32),
            jax.ShapeDtypeStruct((examples, chips, 2, queries[0].shape[1], 2 * rank), jnp.float32),
        ],
        scratch_shapes=[pltpu.VMEM((2 * rank, tokens), jnp.float32)],
        compiler_params=PARAMS,
    )(*parts, *queries)


def last_scores(grads, sums, queries, chips):
    examples, all_chips, cores, held, _ = sums.shape
    return pl.pallas_call(
        functools.partial(last_score_kernel, chips),
        out_shape=jax.ShapeDtypeStruct((examples, all_chips * cores * held), jnp.float32),
        scratch_shapes=[pltpu.VMEM(sums.shape, jnp.float32)],
        compiler_params=PARAMS,
    )(grads, sums, queries)


def shards(inputs, out_grads, proj_in, proj_out, queries):
    devices = lax.axis_size("ex")
    chips = devices // 2
    depth = chips // 2
    rank = proj_in.shape[1]
    together = lax.optimization_barrier

    def swap(array, chip=0, core=0):
        distance = 2 * chip + core
        return lax.ppermute(array, "ex", [(i, i ^ distance) for i in range(devices)])

    steps = [1 << bit for bit in reversed(range(chips.bit_length() - 1))]
    held, reach = queries[None], [0]
    came_held = swap(held, chip=steps[0])
    (given_y, kept_y), (given, kept) = project(inputs, out_grads, proj_in.T, proj_out.T, devices)
    came_y = [swap(array, core=1) for array in given_y]
    came = swap(given[0], core=1)
    for last, step in zip(steps, steps[1:-1]):
        held, reach = stack(held, came_held), reach + [chip ^ last for chip in reach]
        came_held = swap(held, chip=step)
    across = swap(add_given(kept_y, came_y), chip=1)
    early, early_reach = held, reach
    late, late_reach = came_held, [chip ^ steps[-2] for chip in reach]
    held, reach = stack(early, late), early_reach + late_reach
    came_held = swap(held, chip=1)
    other_early = swap(early, core=1)
    across, came, other_early = together((across, came, other_early))

    parts = list(add_kept(kept, came, across))
    late, parts = together((late, parts))
    other_late = swap(late, core=1)
    parts[1:] = [swap(part, chip=2 * z) for z, part in zip(reversed(range(1, depth)), parts[1:])]
    came_held, other_late, parts = together((came_held, other_late, parts))
    other_came = swap(came_held, core=1)
    reach_y = [chip ^ 1 for chip in reach]
    queries = [held, other_early, other_late, came_held]
    reaches = [(0, reach), (1, early_reach), (1, late_reach), (0, reach_y)]
    grads, scores = first_scores(parts, queries, reaches, rank)
    return last_scores(grads, scores, other_came, reach_y)


def solution(mesh):
    return jax.shard_map(
        shards,
        mesh=mesh,
        in_specs=(
            P("ex", "groups"),
            P("ex", "groups"),
            P("ex", None),
            P("ex", None),
            P("ex", None),
        ),
        out_specs=P(("groups", "ex"), None),
        check_vma=False,
    )
```

```python
import functools

import jax
import jax.numpy as jnp
from jax import lax
from jax.experimental import pallas as pl
from jax.experimental.pallas import tpu as pltpu
from jax.sharding import PartitionSpec as P

SEQ = 64
VMEM_BYTES = 32 * 1024 * 1024
LOADED_ROWS = 128
FAR_PAD = 16
LEFT_OVER = 0.36 * 2.0**-8
LANES_BY_LANES = (((1,), (1,)), ((), ()))
HBM_SPEC = pl.BlockSpec(memory_space=pltpu.HBM)
VMEM_SPEC = pl.BlockSpec(memory_space=pltpu.VMEM)
PARAMS = pltpu.CompilerParams(vmem_limit_bytes=VMEM_BYTES)


def project_loaded_kernel(x_hbm, w_hbm, p_in_hbm, p_out_hbm, low_in_ref, low_out_ref, x_buf, w_buf, p_in, p_out, sems, p_sems):
    matrices = [
        pltpu.make_async_copy(p_in_hbm, p_in, p_sems.at[0]),
        pltpu.make_async_copy(p_out_hbm.at[:, pl.ds(0, p_out.shape[1])], p_out, p_sems.at[1]),
    ]
    chunks = []
    for hbm, buf, matrix, low_ref in ((x_hbm, x_buf, p_in, low_in_ref), (w_hbm, w_buf, p_out, low_out_ref)):
        count = buf.shape[0] // LOADED_ROWS if buf.shape[0] % LOADED_ROWS == 0 else 1
        for chunk in range(count):
            part = pl.ds(chunk * (buf.shape[0] // count), buf.shape[0] // count)
            copy = pltpu.make_async_copy(hbm.at[part, :], buf.at[part, :], sems.at[len(chunks)])
            chunks.append((part, buf, matrix, low_ref, copy, chunk == 0))
    for copy in matrices + [chunk[4] for chunk in chunks]:
        copy.start()
    for copy in matrices:
        copy.wait()
    step = min(1024, low_in_ref.shape[1])
    for part, buf, matrix, low_ref, copy, first in chunks:
        copy.wait()
        for column in range(0, low_ref.shape[1], step):
            columns = slice(column, column + step)
            product = jnp.dot(matrix[:, part], buf[part, columns], preferred_element_type=jnp.float32)
            low_ref[:, columns] = product if first else low_ref[:, columns] + product


def project_loaded(inputs, out_grads, proj_in_t, proj_out_t, rows):
    arrays = [pltpu.with_memory_space_constraint(a, pltpu.HBM) for a in (inputs, out_grads, proj_in_t, proj_out_t)]
    rank, tokens = proj_in_t.shape[0], inputs.shape[1]
    chunks = sum(a // LOADED_ROWS if a % LOADED_ROWS == 0 else 1 for a in (inputs.shape[0], rows))
    return pl.pallas_call(
        project_loaded_kernel,
        out_shape=[jax.ShapeDtypeStruct((rank, tokens), jnp.float32)] * 2,
        in_specs=[HBM_SPEC] * 4,
        out_specs=[VMEM_SPEC] * 2,
        scratch_shapes=[
            pltpu.VMEM(inputs.shape, jnp.bfloat16),
            pltpu.VMEM((rows, tokens), jnp.bfloat16),
            pltpu.VMEM(proj_in_t.shape, jnp.bfloat16),
            pltpu.VMEM((rank, max(rows, 128)), jnp.bfloat16),
            pltpu.SemaphoreType.DMA((chunks,)),
            pltpu.SemaphoreType.DMA((2,)),
        ],
        compiler_params=PARAMS,
        cost_estimate=pl.CostEstimate(
            flops=2 * rank * (inputs.shape[0] + rows) * tokens,
            bytes_accessed=2 * (inputs.shape[0] + rows) * tokens,
            transcendentals=0,
        ),
    )(*arrays)


def project_kernel(done, low_in_ref, low_out_ref, p_ref, w_ref, *refs):
    *given, kept_y, kept_here = refs
    given_y, given_here = given[:-1], given[-1:]
    here = lax.axis_index("ex")
    core, chip = lax.rem(here, 2), lax.div(here, 2)
    depth = kept_y.shape[0]
    rank, width = kept_y.shape[1] // 2, kept_y.shape[2]
    for flip, given_refs, kept_ref in ((1, given_y, kept_y), (0, given_here, kept_here)):
        for z in range(depth):
            place = lax.bitwise_xor(chip, 2 * z + flip)
            columns = pl.ds(pl.multiple_of(place * 2 * width, 2 * width), 2 * width)
            low_out = jnp.dot(p_ref[:, done:], w_ref[done:, columns], preferred_element_type=jnp.float32)
            low_out = low_out + low_out_ref[:, columns]
            given_ref = given_refs[z * len(given_refs) // depth]
            for lines, low in ((slice(0, rank), low_in_ref[:, columns]), (slice(rank, 2 * rank), low_out)):
                left, right = low[:, :width], low[:, width:]
                given_ref[z % given_ref.shape[0], lines, :] = jnp.where(core == 0, right, left)
                kept_ref[z, lines, :] = jnp.where(core == 0, left, right)


def project(inputs, out_grads, proj_in_t, proj_out_t, devices):
    rank, width = proj_in_t.shape[0], inputs.shape[1] // devices
    units = out_grads.shape[0]
    rows = LOADED_ROWS if units % LOADED_ROWS == 0 else 16
    lows = project_loaded(inputs, out_grads, proj_in_t, proj_out_t, rows)
    low = jax.ShapeDtypeStruct((devices // 4, 2 * rank, width), jnp.float32)
    half = jax.ShapeDtypeStruct((devices // 8, 2 * rank, width), jnp.float32)
    return pl.pallas_call(
        functools.partial(project_kernel, rows),
        out_shape=[half] * 2 + [low] * 3,
        in_specs=[VMEM_SPEC] * 4,
        out_specs=[VMEM_SPEC] * 5,
        compiler_params=PARAMS,
        cost_estimate=pl.CostEstimate(
            flops=2 * rank * out_grads.size, bytes_accessed=2 * out_grads.size, transcendentals=0
        ),
    )(*lows, proj_out_t, out_grads)


def put_coded(out_ref, low):
    rows = low.shape[0]
    rounded = low.astype(jnp.bfloat16)
    out_ref[:rows, :] = rounded
    above = jnp.where(low > rounded.astype(jnp.float32), 1.0, 0.0)
    part = rows // 8
    word = above[:part, :]
    for index in range(1, 8):
        word = word + 2.0**index * above[index * part : (index + 1) * part, :]
    out_ref[rows : rows + part, :] = word.astype(jnp.bfloat16)


def add_coded(total, rows, ref):
    part = rows // 8
    word = ref[rows : rows + part, :].astype(jnp.float32)
    parts = []
    for index in reversed(range(8)):
        above = jnp.floor(word * 0.5**index)
        word = word - above * 2.0**index
        rounded = ref[index * part : (index + 1) * part, :].astype(jnp.float32)
        left = jnp.abs(rounded) * ((2.0 * LEFT_OVER) * above - LEFT_OVER)
        parts.append((slice(index * part, (index + 1) * part), total(index * part, part) + rounded + left))
    return parts


def add_given_kernel(kept_ref, *refs):
    *came_refs, out_ref = refs
    half = came_refs[0].shape[0]
    for block in range(out_ref.shape[0]):
        put_coded(out_ref.at[block], kept_ref[block] + came_refs[block // half][block % half])


def add_given(kept, came):
    blocks, rows, width = kept.shape
    return pl.pallas_call(
        add_given_kernel,
        out_shape=jax.ShapeDtypeStruct((blocks, rows // 8 * 9, width), jnp.bfloat16),
        compiler_params=PARAMS,
    )(kept, *came)


def add_kept_kernel(kept_ref, came_ref, across_ref, own_ref, *out_refs):
    for z in range(len(out_refs) + 1):
        def here(first, rows):
            return kept_ref[z, first : first + rows, :] + came_ref[z, first : first + rows, :]

        sums = add_coded(here, kept_ref.shape[1], across_ref.at[z])
        if z == 0:
            for rows, total in sums:
                own_ref[rows, :] = total
        else:
            put_coded(out_refs[len(out_refs) - z], jnp.concatenate([total for _, total in reversed(sums)], axis=0))


def add_kept(kept, came, across):
    depth, rows, width = kept.shape
    own = jax.ShapeDtypeStruct((rows, width), jnp.float32)
    heights = [rows // 8 * 9 + (FAR_PAD if z > 2 else 0) for z in reversed(range(1, depth))]
    return pl.pallas_call(
        add_kept_kernel,
        out_shape=[own] + [jax.ShapeDtypeStruct((height, width), jnp.bfloat16) for height in heights],
        compiler_params=PARAMS,
    )(kept, came, across)


def stack_kernel(left_ref, right_ref, out_ref):
    out_ref[: left_ref.shape[0]] = left_ref[...]
    out_ref[left_ref.shape[0] :] = right_ref[...]


def stack(left, right):
    return pl.pallas_call(
        stack_kernel,
        out_shape=jax.ShapeDtypeStruct((2 * left.shape[0],) + left.shape[1:], left.dtype),
        compiler_params=PARAMS,
    )(left, right)


def add_scores(queries_ref, chips, place, grads, sums_ref):
    examples, half_rank, lanes = grads.shape
    held = queries_ref.shape[1]
    step = 4 if len(chips) % 4 == 0 else 2
    here = lax.div(lax.axis_index("ex"), 2)
    for first in range(0, len(chips), step):
        sums = [jnp.zeros((step * held, lanes), jnp.float32) for _ in range(examples)]
        for k in range(half_rank):
            query = queries_ref[first : first + step, :, k * lanes : (k + 1) * lanes].astype(jnp.float32)
            query = query.reshape(step * held, lanes)
            for n in range(examples):
                sums[n] = sums[n] + query * grads[n, k : k + 1, :]
        for part in range(step):
            source = lax.bitwise_xor(here, chips[first + part])
            for n in range(examples):
                sums_ref[n, source, place] = sums[n][part * held : (part + 1) * held, :]


def first_score_kernel(parts_count, held, *refs):
    part_refs, query_refs = refs[:parts_count], refs[parts_count : parts_count + len(held)]
    grads_ref, sums_ref, total_ref = refs[parts_count + len(held) :]
    rank, tokens = total_ref.shape[0] // 2, total_ref.shape[1]
    core = lax.rem(lax.axis_index("ex"), 2)
    total_ref[...] = part_refs[0][...]
    for part_ref in part_refs[1:]:
        for rows, total in add_coded(lambda first, count: total_ref[first : first + count, :], 2 * rank, part_ref):
            total_ref[rows, :] = total
    even = total_ref[pl.ds(rank, rank // 2, stride=2), :]
    odd = total_ref[pl.ds(rank + 1, rank // 2, stride=2), :]
    token = lax.broadcasted_iota(jnp.int32, (rank, tokens), 1)
    for n in range(tokens // SEQ):
        mine = jnp.where((token >= n * SEQ) & (token < (n + 1) * SEQ), total_ref[:rank, :], 0.0)
        for side, rows in enumerate((even, odd)):
            grads_ref[n, :, side * rank : (side + 1) * rank] = lax.dot_general(
                rows, mine, LANES_BY_LANES, precision=lax.Precision.HIGHEST, preferred_element_type=jnp.float32
            )
    sums_ref[...] = jnp.zeros_like(sums_ref)
    for queries_ref, (other, chips) in zip(query_refs, held):
        add_scores(queries_ref, chips, lax.rem(core + other, 2), grads_ref, sums_ref)


def last_score_kernel(chips, grads_ref, before_ref, queries_ref, out_ref, sums_ref):
    core = lax.rem(lax.axis_index("ex"), 2)
    sums_ref[...] = before_ref[...]
    add_scores(queries_ref, chips, lax.rem(core + 1, 2), grads_ref, sums_ref)
    examples, *rows, lanes = sums_ref.shape
    sums = sums_ref[...].reshape(examples * out_ref.shape[1], lanes)
    high = sums.astype(jnp.bfloat16)
    low = (sums - high.astype(jnp.float32)).astype(jnp.bfloat16)
    ones = jnp.ones((16, lanes), jnp.bfloat16)
    row = sum(lax.dot_general(ones, part, LANES_BY_LANES, preferred_element_type=jnp.float32) for part in (high, low))
    for n in range(examples):
        out_ref[n : n + 1, :] = row[0:1, n * out_ref.shape[1] : (n + 1) * out_ref.shape[1]]


def first_scores(parts, queries, held, rank):
    tokens = parts[0].shape[1]
    examples = tokens // SEQ
    chips = 2 * queries[0].shape[0]
    return pl.pallas_call(
        functools.partial(first_score_kernel, len(parts), held),
        out_shape=[
            jax.ShapeDtypeStruct((examples, rank // 2, 2 * rank), jnp.float32),
            jax.ShapeDtypeStruct((examples, chips, 2, queries[0].shape[1], 2 * rank), jnp.float32),
        ],
        scratch_shapes=[pltpu.VMEM((2 * rank, tokens), jnp.float32)],
        compiler_params=PARAMS,
    )(*parts, *queries)


def last_scores(grads, sums, queries, chips):
    examples, all_chips, cores, held, _ = sums.shape
    return pl.pallas_call(
        functools.partial(last_score_kernel, chips),
        out_shape=jax.ShapeDtypeStruct((examples, all_chips * cores * held), jnp.float32),
        scratch_shapes=[pltpu.VMEM(sums.shape, jnp.float32)],
        compiler_params=PARAMS,
    )(grads, sums, queries)


def shards(inputs, out_grads, proj_in, proj_out, queries):
    devices = lax.axis_size("ex")
    chips = devices // 2
    depth = chips // 2
    rank = proj_in.shape[1]
    together = lax.optimization_barrier

    def swap(array, chip=0, core=0):
        distance = 2 * chip + core
        return lax.ppermute(array, "ex", [(i, i ^ distance) for i in range(devices)])

    steps = [1 << bit for bit in reversed(range(chips.bit_length() - 1))]
    held, reach = queries[None], [0]
    came_held = swap(held, chip=steps[0])
    lows = project(inputs, out_grads, proj_in.T, proj_out.T, devices)
    *given_y, given, kept_y, kept = lows
    came_y = [swap(array, core=1) for array in given_y]
    came = swap(given, core=1)
    for last, step in zip(steps, steps[1:-1]):
        held, reach = stack(held, came_held), reach + [chip ^ last for chip in reach]
        came_held = swap(held, chip=step)
    across = swap(add_given(kept_y, came_y), chip=1)
    early, early_reach = held, reach
    late, late_reach = came_held, [chip ^ steps[-2] for chip in reach]
    held, reach = stack(early, late), early_reach + late_reach
    came_held = swap(held, chip=1)
    other_early = swap(early, core=1)
    across, came = together((across, came))

    parts = list(add_kept(kept, came, across))
    late, parts = together((late, parts))
    other_late = swap(late, core=1)
    parts[1:] = [swap(part, chip=2 * z) for z, part in zip(reversed(range(1, depth)), parts[1:])]
    came_held, other_late, other_early, parts = together((came_held, other_late, other_early, parts))
    other_came = swap(came_held, core=1)
    reach_y = [chip ^ 1 for chip in reach]
    queries = [held, other_early, other_late, came_held]
    reaches = [(0, reach), (1, early_reach), (1, late_reach), (0, reach_y)]
    grads, scores = first_scores(parts, queries, reaches, rank)
    return last_scores(grads, scores, other_came, reach_y)


def solution(mesh):
    return jax.shard_map(
        shards,
        mesh=mesh,
        in_specs=(
            P("ex", "groups"),
            P("ex", "groups"),
            P("ex", None),
            P("ex", None),
            P("ex", None),
        ),
        out_specs=P(("groups", "ex"), None),
        check_vma=False,
    )
```

```python
import functools

import jax
import jax.numpy as jnp
from jax import lax
from jax.experimental import pallas as pl
from jax.experimental.pallas import tpu as pltpu
from jax.sharding import PartitionSpec as P

SEQ = 64
VMEM_BYTES = 32 * 1024 * 1024
LOADED_ROWS = 128
FAR_PAD = 16
LEFT_OVER = 0.36 * 2.0**-8
LANES_BY_LANES = (((1,), (1,)), ((), ()))
HBM_SPEC = pl.BlockSpec(memory_space=pltpu.HBM)
VMEM_SPEC = pl.BlockSpec(memory_space=pltpu.VMEM)
PARAMS = pltpu.CompilerParams(vmem_limit_bytes=VMEM_BYTES)


def project_loaded_kernel(x_hbm, w_hbm, p_in_hbm, p_out_hbm, low_in_ref, low_out_ref, x_buf, w_buf, p_in, p_out, sems, p_sems):
    matrices = [
        pltpu.make_async_copy(p_in_hbm, p_in, p_sems.at[0]),
        pltpu.make_async_copy(p_out_hbm.at[:, pl.ds(0, p_out.shape[1])], p_out, p_sems.at[1]),
    ]
    chunks = []
    for hbm, buf, matrix, low_ref in ((x_hbm, x_buf, p_in, low_in_ref), (w_hbm, w_buf, p_out, low_out_ref)):
        count = buf.shape[0] // LOADED_ROWS if buf.shape[0] % LOADED_ROWS == 0 else 1
        for chunk in range(count):
            part = pl.ds(chunk * (buf.shape[0] // count), buf.shape[0] // count)
            copy = pltpu.make_async_copy(hbm.at[part, :], buf.at[part, :], sems.at[len(chunks)])
            chunks.append((part, buf, matrix, low_ref, copy, chunk == 0))
    for copy in matrices + [chunk[4] for chunk in chunks]:
        copy.start()
    for copy in matrices:
        copy.wait()
    step = min(1024, low_in_ref.shape[1])
    for part, buf, matrix, low_ref, copy, first in chunks:
        copy.wait()
        for column in range(0, low_ref.shape[1], step):
            columns = slice(column, column + step)
            product = jnp.dot(matrix[:, part], buf[part, columns], preferred_element_type=jnp.float32)
            low_ref[:, columns] = product if first else low_ref[:, columns] + product


def project_loaded(inputs, out_grads, proj_in_t, proj_out_t, rows):
    arrays = [pltpu.with_memory_space_constraint(a, pltpu.HBM) for a in (inputs, out_grads, proj_in_t, proj_out_t)]
    rank, tokens = proj_in_t.shape[0], inputs.shape[1]
    chunks = sum(a // LOADED_ROWS if a % LOADED_ROWS == 0 else 1 for a in (inputs.shape[0], rows))
    return pl.pallas_call(
        project_loaded_kernel,
        out_shape=[jax.ShapeDtypeStruct((rank, tokens), jnp.float32)] * 2,
        in_specs=[HBM_SPEC] * 4,
        out_specs=[VMEM_SPEC] * 2,
        scratch_shapes=[
            pltpu.VMEM(inputs.shape, jnp.bfloat16),
            pltpu.VMEM((rows, tokens), jnp.bfloat16),
            pltpu.VMEM(proj_in_t.shape, jnp.bfloat16),
            pltpu.VMEM((rank, max(rows, 128)), jnp.bfloat16),
            pltpu.SemaphoreType.DMA((chunks,)),
            pltpu.SemaphoreType.DMA((2,)),
        ],
        compiler_params=PARAMS,
        cost_estimate=pl.CostEstimate(
            flops=2 * rank * (inputs.shape[0] + rows) * tokens,
            bytes_accessed=2 * (inputs.shape[0] + rows) * tokens,
            transcendentals=0,
        ),
    )(*arrays)


def project_kernel(done, low_in_ref, low_out_ref, p_ref, w_ref, *refs):
    *given, kept_y, kept_here = refs
    given_y, given_here = given[:-1], given[-1:]
    here = lax.axis_index("ex")
    core, chip = lax.rem(here, 2), lax.div(here, 2)
    depth = kept_y.shape[0]
    rank, width = kept_y.shape[1] // 2, kept_y.shape[2]
    line, y = lax.div(chip, 2), lax.rem(chip, 2)
    for z in range(depth):
        start = lax.bitwise_xor(line, z) * 4 * width
        columns = pl.ds(pl.multiple_of(start, 4 * width), 4 * width)
        low_out = jnp.dot(p_ref[:, done:], w_ref[done:, columns], preferred_element_type=jnp.float32)
        low_out = low_out + low_out_ref[:, columns]
        given_ref = given_y[z * len(given_y) // depth]
        places = ((given_ref, z % given_ref.shape[0], kept_y), (given_here[0], z, kept_here))
        for lines, low in ((slice(0, rank), low_in_ref[:, columns]), (slice(rank, 2 * rank), low_out)):
            lower, upper = low[:, : 2 * width], low[:, 2 * width :]
            sides = (jnp.where(y == 0, upper, lower), jnp.where(y == 0, lower, upper))
            for both, (given, at, kept) in zip(sides, places):
                left, right = both[:, :width], both[:, width:]
                given[at, lines, :] = jnp.where(core == 0, right, left)
                kept[z, lines, :] = jnp.where(core == 0, left, right)


def project(inputs, out_grads, proj_in_t, proj_out_t, devices):
    rank, width = proj_in_t.shape[0], inputs.shape[1] // devices
    units = out_grads.shape[0]
    rows = LOADED_ROWS if units % LOADED_ROWS == 0 else 16
    lows = project_loaded(inputs, out_grads, proj_in_t, proj_out_t, rows)
    low = jax.ShapeDtypeStruct((devices // 4, 2 * rank, width), jnp.float32)
    half = jax.ShapeDtypeStruct((devices // 8, 2 * rank, width), jnp.float32)
    return pl.pallas_call(
        functools.partial(project_kernel, rows),
        out_shape=[half] * 2 + [low] * 3,
        in_specs=[VMEM_SPEC] * 4,
        out_specs=[VMEM_SPEC] * 5,
        compiler_params=PARAMS,
        cost_estimate=pl.CostEstimate(
            flops=2 * rank * out_grads.size, bytes_accessed=2 * out_grads.size, transcendentals=0
        ),
    )(*lows, proj_out_t, out_grads)


def put_coded(out_ref, low):
    rows = low.shape[0]
    rounded = low.astype(jnp.bfloat16)
    out_ref[:rows, :] = rounded
    above = jnp.where(low > rounded.astype(jnp.float32), 1.0, 0.0)
    part = rows // 8
    word = above[:part, :]
    for index in range(1, 8):
        word = word + 2.0**index * above[index * part : (index + 1) * part, :]
    out_ref[rows : rows + part, :] = word.astype(jnp.bfloat16)


def add_coded(total, rows, ref):
    part = rows // 8
    word = ref[rows : rows + part, :].astype(jnp.float32)
    parts = []
    for index in reversed(range(8)):
        above = jnp.floor(word * 0.5**index)
        word = word - above * 2.0**index
        rounded = ref[index * part : (index + 1) * part, :].astype(jnp.float32)
        left = jnp.abs(rounded) * ((2.0 * LEFT_OVER) * above - LEFT_OVER)
        parts.append((slice(index * part, (index + 1) * part), total(index * part, part) + rounded + left))
    return parts


def add_given_kernel(kept_ref, *refs):
    *came_refs, out_ref = refs
    half = came_refs[0].shape[0]
    for block in range(out_ref.shape[0]):
        put_coded(out_ref.at[block], kept_ref[block] + came_refs[block // half][block % half])


def add_given(kept, came):
    blocks, rows, width = kept.shape
    return pl.pallas_call(
        add_given_kernel,
        out_shape=jax.ShapeDtypeStruct((blocks, rows // 8 * 9, width), jnp.bfloat16),
        compiler_params=PARAMS,
    )(kept, *came)


def add_kept_kernel(kept_ref, came_ref, across_ref, own_ref, *out_refs):
    for z in range(len(out_refs) + 1):
        def here(first, rows):
            return kept_ref[z, first : first + rows, :] + came_ref[z, first : first + rows, :]

        sums = add_coded(here, kept_ref.shape[1], across_ref.at[z])
        if z == 0:
            for rows, total in sums:
                own_ref[rows, :] = total
        else:
            put_coded(out_refs[len(out_refs) - z], jnp.concatenate([total for _, total in reversed(sums)], axis=0))


def add_kept(kept, came, across):
    depth, rows, width = kept.shape
    own = jax.ShapeDtypeStruct((rows, width), jnp.float32)
    heights = [rows // 8 * 9 + (FAR_PAD if z > 2 else 0) for z in reversed(range(1, depth))]
    return pl.pallas_call(
        add_kept_kernel,
        out_shape=[own] + [jax.ShapeDtypeStruct((height, width), jnp.bfloat16) for height in heights],
        compiler_params=PARAMS,
    )(kept, came, across)


def stack_kernel(left_ref, right_ref, out_ref):
    out_ref[: left_ref.shape[0]] = left_ref[...]
    out_ref[left_ref.shape[0] :] = right_ref[...]


def stack(left, right):
    return pl.pallas_call(
        stack_kernel,
        out_shape=jax.ShapeDtypeStruct((2 * left.shape[0],) + left.shape[1:], left.dtype),
        compiler_params=PARAMS,
    )(left, right)


def add_scores(queries_ref, chips, place, grads, sums_ref):
    examples, half_rank, lanes = grads.shape
    held = queries_ref.shape[1]
    step = 4 if len(chips) % 4 == 0 else 2
    here = lax.div(lax.axis_index("ex"), 2)
    for first in range(0, len(chips), step):
        sums = [jnp.zeros((step * held, lanes), jnp.float32) for _ in range(examples)]
        for k in range(half_rank):
            query = queries_ref[first : first + step, :, k * lanes : (k + 1) * lanes].astype(jnp.float32)
            query = query.reshape(step * held, lanes)
            for n in range(examples):
                sums[n] = sums[n] + query * grads[n, k : k + 1, :]
        for part in range(step):
            source = lax.bitwise_xor(here, chips[first + part])
            for n in range(examples):
                sums_ref[n, source, place] = sums[n][part * held : (part + 1) * held, :]


def first_score_kernel(parts_count, held, *refs):
    part_refs, query_refs = refs[:parts_count], refs[parts_count : parts_count + len(held)]
    grads_ref, sums_ref, total_ref = refs[parts_count + len(held) :]
    rank, tokens = total_ref.shape[0] // 2, total_ref.shape[1]
    core = lax.rem(lax.axis_index("ex"), 2)
    total_ref[...] = part_refs[0][...]
    for part_ref in part_refs[1:]:
        for rows, total in add_coded(lambda first, count: total_ref[first : first + count, :], 2 * rank, part_ref):
            total_ref[rows, :] = total
    even = total_ref[pl.ds(rank, rank // 2, stride=2), :]
    odd = total_ref[pl.ds(rank + 1, rank // 2, stride=2), :]
    token = lax.broadcasted_iota(jnp.int32, (rank, tokens), 1)
    for n in range(tokens // SEQ):
        mine = jnp.where((token >= n * SEQ) & (token < (n + 1) * SEQ), total_ref[:rank, :], 0.0)
        for side, rows in enumerate((even, odd)):
            grads_ref[n, :, side * rank : (side + 1) * rank] = lax.dot_general(
                rows, mine, LANES_BY_LANES, precision=lax.Precision.HIGHEST, preferred_element_type=jnp.float32
            )
    sums_ref[...] = jnp.zeros_like(sums_ref)
    for queries_ref, (other, chips) in zip(query_refs, held):
        add_scores(queries_ref, chips, lax.rem(core + other, 2), grads_ref, sums_ref)


def last_score_kernel(chips, grads_ref, before_ref, queries_ref, out_ref, sums_ref):
    core = lax.rem(lax.axis_index("ex"), 2)
    sums_ref[...] = before_ref[...]
    add_scores(queries_ref, chips, lax.rem(core + 1, 2), grads_ref, sums_ref)
    examples, *rows, lanes = sums_ref.shape
    sums = sums_ref[...].reshape(examples * out_ref.shape[1], lanes)
    high = sums.astype(jnp.bfloat16)
    low = (sums - high.astype(jnp.float32)).astype(jnp.bfloat16)
    ones = jnp.ones((16, lanes), jnp.bfloat16)
    row = sum(lax.dot_general(ones, part, LANES_BY_LANES, preferred_element_type=jnp.float32) for part in (high, low))
    for n in range(examples):
        out_ref[n : n + 1, :] = row[0:1, n * out_ref.shape[1] : (n + 1) * out_ref.shape[1]]


def first_scores(parts, queries, held, rank):
    tokens = parts[0].shape[1]
    examples = tokens // SEQ
    chips = 2 * queries[0].shape[0]
    return pl.pallas_call(
        functools.partial(first_score_kernel, len(parts), held),
        out_shape=[
            jax.ShapeDtypeStruct((examples, rank // 2, 2 * rank), jnp.float32),
            jax.ShapeDtypeStruct((examples, chips, 2, queries[0].shape[1], 2 * rank), jnp.float32),
        ],
        scratch_shapes=[pltpu.VMEM((2 * rank, tokens), jnp.float32)],
        compiler_params=PARAMS,
    )(*parts, *queries)


def last_scores(grads, sums, queries, chips):
    examples, all_chips, cores, held, _ = sums.shape
    return pl.pallas_call(
        functools.partial(last_score_kernel, chips),
        out_shape=jax.ShapeDtypeStruct((examples, all_chips * cores * held), jnp.float32),
        scratch_shapes=[pltpu.VMEM(sums.shape, jnp.float32)],
        compiler_params=PARAMS,
    )(grads, sums, queries)


def shards(inputs, out_grads, proj_in, proj_out, queries):
    devices = lax.axis_size("ex")
    chips = devices // 2
    depth = chips // 2
    rank = proj_in.shape[1]
    together = lax.optimization_barrier

    def swap(array, chip=0, core=0):
        distance = 2 * chip + core
        return lax.ppermute(array, "ex", [(i, i ^ distance) for i in range(devices)])

    steps = [1 << bit for bit in reversed(range(chips.bit_length() - 1))]
    held, reach = queries[None], [0]
    came_held = swap(held, chip=steps[0])
    lows = project(inputs, out_grads, proj_in.T, proj_out.T, devices)
    *given_y, given, kept_y, kept = lows
    came_y = [swap(array, core=1) for array in given_y]
    came = swap(given, core=1)
    for last, step in zip(steps, steps[1:-1]):
        held, reach = stack(held, came_held), reach + [chip ^ last for chip in reach]
        came_held = swap(held, chip=step)
    across = swap(add_given(kept_y, came_y), chip=1)
    early, early_reach = held, reach
    late, late_reach = came_held, [chip ^ steps[-2] for chip in reach]
    held, reach = stack(early, late), early_reach + late_reach
    came_held = swap(held, chip=1)
    other_early = swap(early, core=1)
    across, came, other_early = together((across, came, other_early))

    parts = list(add_kept(kept, came, across))
    late, parts = together((late, parts))
    other_late = swap(late, core=1)
    parts[1:] = [swap(part, chip=2 * z) for z, part in zip(reversed(range(1, depth)), parts[1:])]
    came_held, other_late, parts = together((came_held, other_late, parts))
    other_came = swap(came_held, core=1)
    reach_y = [chip ^ 1 for chip in reach]
    queries = [held, other_early, other_late, came_held]
    reaches = [(0, reach), (1, early_reach), (1, late_reach), (0, reach_y)]
    grads, scores = first_scores(parts, queries, reaches, rank)
    return last_scores(grads, scores, other_came, reach_y)


def solution(mesh):
    return jax.shard_map(
        shards,
        mesh=mesh,
        in_specs=(
            P("ex", "groups"),
            P("ex", "groups"),
            P("ex", None),
            P("ex", None),
            P("ex", None),
        ),
        out_specs=P(("groups", "ex"), None),
        check_vma=False,
    )
```

```python
import functools

import jax
import jax.numpy as jnp
from jax import lax
from jax.experimental import pallas as pl
from jax.experimental.pallas import tpu as pltpu
from jax.sharding import PartitionSpec as P

SEQ = 64
VMEM_BYTES = 32 * 1024 * 1024
LOADED_ROWS = 128
CHUNK_ROWS = 256
FAR_PAD = 16
LEFT_OVER = 0.36 * 2.0**-8
LANES_BY_LANES = (((1,), (1,)), ((), ()))
HBM_SPEC = pl.BlockSpec(memory_space=pltpu.HBM)
VMEM_SPEC = pl.BlockSpec(memory_space=pltpu.VMEM)
PARAMS = pltpu.CompilerParams(vmem_limit_bytes=VMEM_BYTES)


def project_loaded_kernel(x_hbm, w_hbm, p_in_hbm, p_out_hbm, low_in_ref, low_out_ref, x_buf, w_buf, p_in, p_out, sems, p_sems):
    matrices = [
        pltpu.make_async_copy(p_in_hbm, p_in, p_sems.at[0]),
        pltpu.make_async_copy(p_out_hbm.at[:, pl.ds(0, p_out.shape[1])], p_out, p_sems.at[1]),
    ]
    chunks = []
    for hbm, buf, matrix, low_ref in ((x_hbm, x_buf, p_in, low_in_ref), (w_hbm, w_buf, p_out, low_out_ref)):
        count = buf.shape[0] // CHUNK_ROWS if buf.shape[0] % CHUNK_ROWS == 0 else 1
        for chunk in range(count):
            part = pl.ds(chunk * (buf.shape[0] // count), buf.shape[0] // count)
            copy = pltpu.make_async_copy(hbm.at[part, :], buf.at[part, :], sems.at[len(chunks)])
            chunks.append((part, buf, matrix, low_ref, copy, chunk == 0))
    for copy in matrices + [chunk[4] for chunk in chunks]:
        copy.start()
    for copy in matrices:
        copy.wait()
    step = min(1024, low_in_ref.shape[1])
    for part, buf, matrix, low_ref, copy, first in chunks:
        copy.wait()
        for column in range(0, low_ref.shape[1], step):
            columns = slice(column, column + step)
            product = jnp.dot(matrix[:, part], buf[part, columns], preferred_element_type=jnp.float32)
            low_ref[:, columns] = product if first else low_ref[:, columns] + product


def project_loaded(inputs, out_grads, proj_in_t, proj_out_t, rows):
    arrays = [pltpu.with_memory_space_constraint(a, pltpu.HBM) for a in (inputs, out_grads, proj_in_t, proj_out_t)]
    rank, tokens = proj_in_t.shape[0], inputs.shape[1]
    chunks = sum(a // CHUNK_ROWS if a % CHUNK_ROWS == 0 else 1 for a in (inputs.shape[0], rows))
    return pl.pallas_call(
        project_loaded_kernel,
        out_shape=[jax.ShapeDtypeStruct((rank, tokens), jnp.float32)] * 2,
        in_specs=[HBM_SPEC] * 4,
        out_specs=[VMEM_SPEC] * 2,
        scratch_shapes=[
            pltpu.VMEM(inputs.shape, jnp.bfloat16),
            pltpu.VMEM((rows, tokens), jnp.bfloat16),
            pltpu.VMEM(proj_in_t.shape, jnp.bfloat16),
            pltpu.VMEM((rank, max(rows, 128)), jnp.bfloat16),
            pltpu.SemaphoreType.DMA((chunks,)),
            pltpu.SemaphoreType.DMA((2,)),
        ],
        compiler_params=PARAMS,
        cost_estimate=pl.CostEstimate(
            flops=2 * rank * (inputs.shape[0] + rows) * tokens,
            bytes_accessed=2 * (inputs.shape[0] + rows) * tokens,
            transcendentals=0,
        ),
    )(*arrays)


def project_kernel(done, low_in_ref, low_out_ref, p_ref, w_ref, *refs):
    *given, kept_y, kept_here = refs
    given_y, given_here = given[:-1], given[-1:]
    here = lax.axis_index("ex")
    core, chip = lax.rem(here, 2), lax.div(here, 2)
    depth = kept_y.shape[0]
    rank, width = kept_y.shape[1] // 2, kept_y.shape[2]
    line, y = lax.div(chip, 2), lax.rem(chip, 2)
    for z in range(depth):
        start = lax.bitwise_xor(line, z) * 4 * width
        columns = pl.ds(pl.multiple_of(start, 4 * width), 4 * width)
        low_out = jnp.dot(p_ref[:, done:], w_ref[done:, columns], preferred_element_type=jnp.float32)
        low_out = low_out + low_out_ref[:, columns]
        given_ref = given_y[z * len(given_y) // depth]
        places = ((given_ref, z % given_ref.shape[0], kept_y), (given_here[0], z, kept_here))
        for lines, low in ((slice(0, rank), low_in_ref[:, columns]), (slice(rank, 2 * rank), low_out)):
            lower, upper = low[:, : 2 * width], low[:, 2 * width :]
            sides = (jnp.where(y == 0, upper, lower), jnp.where(y == 0, lower, upper))
            for both, (given, at, kept) in zip(sides, places):
                left, right = both[:, :width], both[:, width:]
                given[at, lines, :] = jnp.where(core == 0, right, left)
                kept[z, lines, :] = jnp.where(core == 0, left, right)


def project(inputs, out_grads, proj_in_t, proj_out_t, devices):
    rank, width = proj_in_t.shape[0], inputs.shape[1] // devices
    units = out_grads.shape[0]
    rows = LOADED_ROWS if units % LOADED_ROWS == 0 else 16
    lows = project_loaded(inputs, out_grads, proj_in_t, proj_out_t, rows)
    low = jax.ShapeDtypeStruct((devices // 4, 2 * rank, width), jnp.float32)
    half = jax.ShapeDtypeStruct((devices // 8, 2 * rank, width), jnp.float32)
    return pl.pallas_call(
        functools.partial(project_kernel, rows),
        out_shape=[half] * 2 + [low] * 3,
        in_specs=[VMEM_SPEC] * 4,
        out_specs=[VMEM_SPEC] * 5,
        compiler_params=PARAMS,
        cost_estimate=pl.CostEstimate(
            flops=2 * rank * out_grads.size, bytes_accessed=2 * out_grads.size, transcendentals=0
        ),
    )(*lows, proj_out_t, out_grads)


def put_coded(out_ref, low):
    rows = low.shape[0]
    rounded = low.astype(jnp.bfloat16)
    out_ref[:rows, :] = rounded
    above = jnp.where(low > rounded.astype(jnp.float32), 1.0, 0.0)
    part = rows // 8
    word = above[:part, :]
    for index in range(1, 8):
        word = word + 2.0**index * above[index * part : (index + 1) * part, :]
    out_ref[rows : rows + part, :] = word.astype(jnp.bfloat16)


def add_coded(total, rows, ref):
    part = rows // 8
    word = ref[rows : rows + part, :].astype(jnp.float32)
    parts = []
    for index in reversed(range(8)):
        above = jnp.floor(word * 0.5**index)
        word = word - above * 2.0**index
        rounded = ref[index * part : (index + 1) * part, :].astype(jnp.float32)
        left = jnp.abs(rounded) * ((2.0 * LEFT_OVER) * above - LEFT_OVER)
        parts.append((slice(index * part, (index + 1) * part), total(index * part, part) + rounded + left))
    return parts


def add_given_kernel(kept_ref, *refs):
    *came_refs, out_ref = refs
    half = came_refs[0].shape[0]
    for block in range(out_ref.shape[0]):
        put_coded(out_ref.at[block], kept_ref[block] + came_refs[block // half][block % half])


def add_given(kept, came):
    blocks, rows, width = kept.shape
    return pl.pallas_call(
        add_given_kernel,
        out_shape=jax.ShapeDtypeStruct((blocks, rows // 8 * 9, width), jnp.bfloat16),
        compiler_params=PARAMS,
    )(kept, *came)


def add_kept_kernel(kept_ref, came_ref, across_ref, own_ref, *out_refs):
    for z in range(len(out_refs) + 1):
        def here(first, rows):
            return kept_ref[z, first : first + rows, :] + came_ref[z, first : first + rows, :]

        sums = add_coded(here, kept_ref.shape[1], across_ref.at[z])
        if z == 0:
            for rows, total in sums:
                own_ref[rows, :] = total
        else:
            put_coded(out_refs[len(out_refs) - z], jnp.concatenate([total for _, total in reversed(sums)], axis=0))


def add_kept(kept, came, across):
    depth, rows, width = kept.shape
    own = jax.ShapeDtypeStruct((rows, width), jnp.float32)
    heights = [rows // 8 * 9 + (FAR_PAD if z > 2 else 0) for z in reversed(range(1, depth))]
    return pl.pallas_call(
        add_kept_kernel,
        out_shape=[own] + [jax.ShapeDtypeStruct((height, width), jnp.bfloat16) for height in heights],
        compiler_params=PARAMS,
    )(kept, came, across)


def stack_kernel(left_ref, right_ref, out_ref):
    out_ref[: left_ref.shape[0]] = left_ref[...]
    out_ref[left_ref.shape[0] :] = right_ref[...]


def stack(left, right):
    return pl.pallas_call(
        stack_kernel,
        out_shape=jax.ShapeDtypeStruct((2 * left.shape[0],) + left.shape[1:], left.dtype),
        compiler_params=PARAMS,
    )(left, right)


def add_scores(queries_ref, chips, place, grads, sums_ref):
    examples, half_rank, lanes = grads.shape
    held = queries_ref.shape[1]
    step = 4 if len(chips) % 4 == 0 else 2
    here = lax.div(lax.axis_index("ex"), 2)
    for first in range(0, len(chips), step):
        sums = [jnp.zeros((step * held, lanes), jnp.float32) for _ in range(examples)]
        for k in range(half_rank):
            query = queries_ref[first : first + step, :, k * lanes : (k + 1) * lanes].astype(jnp.float32)
            query = query.reshape(step * held, lanes)
            for n in range(examples):
                sums[n] = sums[n] + query * grads[n, k : k + 1, :]
        for part in range(step):
            source = lax.bitwise_xor(here, chips[first + part])
            for n in range(examples):
                sums_ref[n, source, place] = sums[n][part * held : (part + 1) * held, :]


def first_score_kernel(parts_count, held, *refs):
    part_refs, query_refs = refs[:parts_count], refs[parts_count : parts_count + len(held)]
    grads_ref, sums_ref, total_ref = refs[parts_count + len(held) :]
    rank, tokens = total_ref.shape[0] // 2, total_ref.shape[1]
    core = lax.rem(lax.axis_index("ex"), 2)
    total_ref[...] = part_refs[0][...]
    for part_ref in part_refs[1:]:
        for rows, total in add_coded(lambda first, count: total_ref[first : first + count, :], 2 * rank, part_ref):
            total_ref[rows, :] = total
    even = total_ref[pl.ds(rank, rank // 2, stride=2), :]
    odd = total_ref[pl.ds(rank + 1, rank // 2, stride=2), :]
    token = lax.broadcasted_iota(jnp.int32, (rank, tokens), 1)
    for n in range(tokens // SEQ):
        mine = jnp.where((token >= n * SEQ) & (token < (n + 1) * SEQ), total_ref[:rank, :], 0.0)
        for side, rows in enumerate((even, odd)):
            grads_ref[n, :, side * rank : (side + 1) * rank] = lax.dot_general(
                rows, mine, LANES_BY_LANES, precision=lax.Precision.HIGHEST, preferred_element_type=jnp.float32
            )
    sums_ref[...] = jnp.zeros_like(sums_ref)
    for queries_ref, (other, chips) in zip(query_refs, held):
        add_scores(queries_ref, chips, lax.rem(core + other, 2), grads_ref, sums_ref)


def last_score_kernel(chips, grads_ref, before_ref, queries_ref, out_ref, sums_ref):
    core = lax.rem(lax.axis_index("ex"), 2)
    sums_ref[...] = before_ref[...]
    add_scores(queries_ref, chips, lax.rem(core + 1, 2), grads_ref, sums_ref)
    examples, *rows, lanes = sums_ref.shape
    sums = sums_ref[...].reshape(examples * out_ref.shape[1], lanes)
    high = sums.astype(jnp.bfloat16)
    low = (sums - high.astype(jnp.float32)).astype(jnp.bfloat16)
    ones = jnp.ones((16, lanes), jnp.bfloat16)
    row = sum(lax.dot_general(ones, part, LANES_BY_LANES, preferred_element_type=jnp.float32) for part in (high, low))
    for n in range(examples):
        out_ref[n : n + 1, :] = row[0:1, n * out_ref.shape[1] : (n + 1) * out_ref.shape[1]]


def first_scores(parts, queries, held, rank):
    tokens = parts[0].shape[1]
    examples = tokens // SEQ
    chips = 2 * queries[0].shape[0]
    return pl.pallas_call(
        functools.partial(first_score_kernel, len(parts), held),
        out_shape=[
            jax.ShapeDtypeStruct((examples, rank // 2, 2 * rank), jnp.float32),
            jax.ShapeDtypeStruct((examples, chips, 2, queries[0].shape[1], 2 * rank), jnp.float32),
        ],
        scratch_shapes=[pltpu.VMEM((2 * rank, tokens), jnp.float32)],
        compiler_params=PARAMS,
    )(*parts, *queries)


def last_scores(grads, sums, queries, chips):
    examples, all_chips, cores, held, _ = sums.shape
    return pl.pallas_call(
        functools.partial(last_score_kernel, chips),
        out_shape=jax.ShapeDtypeStruct((examples, all_chips * cores * held), jnp.float32),
        scratch_shapes=[pltpu.VMEM(sums.shape, jnp.float32)],
        compiler_params=PARAMS,
    )(grads, sums, queries)


def shards(inputs, out_grads, proj_in, proj_out, queries):
    devices = lax.axis_size("ex")
    chips = devices // 2
    depth = chips // 2
    rank = proj_in.shape[1]
    together = lax.optimization_barrier

    def swap(array, chip=0, core=0):
        distance = 2 * chip + core
        return lax.ppermute(array, "ex", [(i, i ^ distance) for i in range(devices)])

    steps = [1 << bit for bit in reversed(range(chips.bit_length() - 1))]
    held, reach = queries[None], [0]
    came_held = swap(held, chip=steps[0])
    lows = project(inputs, out_grads, proj_in.T, proj_out.T, devices)
    *given_y, given, kept_y, kept = lows
    came_y = [swap(array, core=1) for array in given_y]
    came = swap(given, core=1)
    for last, step in zip(steps, steps[1:-1]):
        held, reach = stack(held, came_held), reach + [chip ^ last for chip in reach]
        came_held = swap(held, chip=step)
    across = swap(add_given(kept_y, came_y), chip=1)
    early, early_reach = held, reach
    late, late_reach = came_held, [chip ^ steps[-2] for chip in reach]
    held, reach = stack(early, late), early_reach + late_reach
    came_held = swap(held, chip=1)
    other_early = swap(early, core=1)
    across, came, other_early = together((across, came, other_early))

    parts = list(add_kept(kept, came, across))
    late, parts = together((late, parts))
    other_late = swap(late, core=1)
    parts[1:] = [swap(part, chip=2 * z) for z, part in zip(reversed(range(1, depth)), parts[1:])]
    came_held, other_late, parts = together((came_held, other_late, parts))
    other_came = swap(came_held, core=1)
    reach_y = [chip ^ 1 for chip in reach]
    queries = [held, other_early, other_late, came_held]
    reaches = [(0, reach), (1, early_reach), (1, late_reach), (0, reach_y)]
    grads, scores = first_scores(parts, queries, reaches, rank)
    return last_scores(grads, scores, other_came, reach_y)


def solution(mesh):
    return jax.shard_map(
        shards,
        mesh=mesh,
        in_specs=(
            P("ex", "groups"),
            P("ex", "groups"),
            P("ex", None),
            P("ex", None),
            P("ex", None),
        ),
        out_specs=P(("groups", "ex"), None),
        check_vma=False,
    )
```

```python
import functools

import jax
import jax.numpy as jnp
from jax import lax
from jax.experimental import pallas as pl
from jax.experimental.pallas import tpu as pltpu
from jax.sharding import PartitionSpec as P

SEQ = 64
VMEM_BYTES = 32 * 1024 * 1024
LOADED_ROWS = 256
CHUNK_ROWS = 256
FAR_PAD = 16
LEFT_OVER = 0.36 * 2.0**-8
LANES_BY_LANES = (((1,), (1,)), ((), ()))
HBM_SPEC = pl.BlockSpec(memory_space=pltpu.HBM)
VMEM_SPEC = pl.BlockSpec(memory_space=pltpu.VMEM)
PARAMS = pltpu.CompilerParams(vmem_limit_bytes=VMEM_BYTES)


def project_loaded_kernel(x_hbm, w_hbm, p_in_hbm, p_out_hbm, low_in_ref, low_out_ref, x_buf, w_buf, p_in, p_out, sems, p_sems):
    matrices = [
        pltpu.make_async_copy(p_in_hbm, p_in, p_sems.at[0]),
        pltpu.make_async_copy(p_out_hbm.at[:, pl.ds(0, p_out.shape[1])], p_out, p_sems.at[1]),
    ]
    chunks = []
    for hbm, buf, matrix, low_ref in ((x_hbm, x_buf, p_in, low_in_ref), (w_hbm, w_buf, p_out, low_out_ref)):
        count = buf.shape[0] // CHUNK_ROWS if buf.shape[0] % CHUNK_ROWS == 0 else 1
        for chunk in range(count):
            part = pl.ds(chunk * (buf.shape[0] // count), buf.shape[0] // count)
            copy = pltpu.make_async_copy(hbm.at[part, :], buf.at[part, :], sems.at[len(chunks)])
            chunks.append((part, buf, matrix, low_ref, copy, chunk == 0))
    for copy in matrices + [chunk[4] for chunk in chunks]:
        copy.start()
    for copy in matrices:
        copy.wait()
    step = min(1024, low_in_ref.shape[1])
    for part, buf, matrix, low_ref, copy, first in chunks:
        copy.wait()
        for column in range(0, low_ref.shape[1], step):
            columns = slice(column, column + step)
            product = jnp.dot(matrix[:, part], buf[part, columns], preferred_element_type=jnp.float32)
            low_ref[:, columns] = product if first else low_ref[:, columns] + product


def project_loaded(inputs, out_grads, proj_in_t, proj_out_t, rows):
    arrays = [pltpu.with_memory_space_constraint(a, pltpu.HBM) for a in (inputs, out_grads, proj_in_t, proj_out_t)]
    rank, tokens = proj_in_t.shape[0], inputs.shape[1]
    chunks = sum(a // CHUNK_ROWS if a % CHUNK_ROWS == 0 else 1 for a in (inputs.shape[0], rows))
    return pl.pallas_call(
        project_loaded_kernel,
        out_shape=[jax.ShapeDtypeStruct((rank, tokens), jnp.float32)] * 2,
        in_specs=[HBM_SPEC] * 4,
        out_specs=[VMEM_SPEC] * 2,
        scratch_shapes=[
            pltpu.VMEM(inputs.shape, jnp.bfloat16),
            pltpu.VMEM((rows, tokens), jnp.bfloat16),
            pltpu.VMEM(proj_in_t.shape, jnp.bfloat16),
            pltpu.VMEM((rank, max(rows, 128)), jnp.bfloat16),
            pltpu.SemaphoreType.DMA((chunks,)),
            pltpu.SemaphoreType.DMA((2,)),
        ],
        compiler_params=PARAMS,
        cost_estimate=pl.CostEstimate(
            flops=2 * rank * (inputs.shape[0] + rows) * tokens,
            bytes_accessed=2 * (inputs.shape[0] + rows) * tokens,
            transcendentals=0,
        ),
    )(*arrays)


def project_kernel(done, low_in_ref, low_out_ref, p_ref, w_ref, *refs):
    *given, kept_y, kept_here = refs
    given_y, given_here = given[:-1], given[-1:]
    here = lax.axis_index("ex")
    core, chip = lax.rem(here, 2), lax.div(here, 2)
    depth = kept_y.shape[0]
    rank, width = kept_y.shape[1] // 2, kept_y.shape[2]
    line, y = lax.div(chip, 2), lax.rem(chip, 2)
    for z in range(depth):
        start = lax.bitwise_xor(line, z) * 4 * width
        columns = pl.ds(pl.multiple_of(start, 4 * width), 4 * width)
        low_out = jnp.dot(p_ref[:, done:], w_ref[done:, columns], preferred_element_type=jnp.float32)
        low_out = low_out + low_out_ref[:, columns]
        given_ref = given_y[z * len(given_y) // depth]
        places = ((given_ref, z % given_ref.shape[0], kept_y), (given_here[0], z, kept_here))
        for lines, low in ((slice(0, rank), low_in_ref[:, columns]), (slice(rank, 2 * rank), low_out)):
            lower, upper = low[:, : 2 * width], low[:, 2 * width :]
            sides = (jnp.where(y == 0, upper, lower), jnp.where(y == 0, lower, upper))
            for both, (given, at, kept) in zip(sides, places):
                left, right = both[:, :width], both[:, width:]
                given[at, lines, :] = jnp.where(core == 0, right, left)
                kept[z, lines, :] = jnp.where(core == 0, left, right)


def project(inputs, out_grads, proj_in_t, proj_out_t, devices):
    rank, width = proj_in_t.shape[0], inputs.shape[1] // devices
    units = out_grads.shape[0]
    rows = LOADED_ROWS if units % LOADED_ROWS == 0 else 16
    lows = project_loaded(inputs, out_grads, proj_in_t, proj_out_t, rows)
    low = jax.ShapeDtypeStruct((devices // 4, 2 * rank, width), jnp.float32)
    half = jax.ShapeDtypeStruct((devices // 8, 2 * rank, width), jnp.float32)
    return pl.pallas_call(
        functools.partial(project_kernel, rows),
        out_shape=[half] * 2 + [low] * 3,
        in_specs=[VMEM_SPEC] * 4,
        out_specs=[VMEM_SPEC] * 5,
        compiler_params=PARAMS,
        cost_estimate=pl.CostEstimate(
            flops=2 * rank * out_grads.size, bytes_accessed=2 * out_grads.size, transcendentals=0
        ),
    )(*lows, proj_out_t, out_grads)


def put_coded(out_ref, low):
    rows = low.shape[0]
    rounded = low.astype(jnp.bfloat16)
    out_ref[:rows, :] = rounded
    above = jnp.where(low > rounded.astype(jnp.float32), 1.0, 0.0)
    part = rows // 8
    word = above[:part, :]
    for index in range(1, 8):
        word = word + 2.0**index * above[index * part : (index + 1) * part, :]
    out_ref[rows : rows + part, :] = word.astype(jnp.bfloat16)


def add_coded(total, rows, ref):
    part = rows // 8
    word = ref[rows : rows + part, :].astype(jnp.float32)
    parts = []
    for index in reversed(range(8)):
        above = jnp.floor(word * 0.5**index)
        word = word - above * 2.0**index
        rounded = ref[index * part : (index + 1) * part, :].astype(jnp.float32)
        left = jnp.abs(rounded) * ((2.0 * LEFT_OVER) * above - LEFT_OVER)
        parts.append((slice(index * part, (index + 1) * part), total(index * part, part) + rounded + left))
    return parts


def add_given_kernel(kept_ref, *refs):
    *came_refs, out_ref = refs
    half = came_refs[0].shape[0]
    for block in range(out_ref.shape[0]):
        put_coded(out_ref.at[block], kept_ref[block] + came_refs[block // half][block % half])


def add_given(kept, came):
    blocks, rows, width = kept.shape
    return pl.pallas_call(
        add_given_kernel,
        out_shape=jax.ShapeDtypeStruct((blocks, rows // 8 * 9, width), jnp.bfloat16),
        compiler_params=PARAMS,
    )(kept, *came)


def add_kept_kernel(kept_ref, came_ref, across_ref, own_ref, *out_refs):
    for z in range(len(out_refs) + 1):
        def here(first, rows):
            return kept_ref[z, first : first + rows, :] + came_ref[z, first : first + rows, :]

        sums = add_coded(here, kept_ref.shape[1], across_ref.at[z])
        if z == 0:
            for rows, total in sums:
                own_ref[rows, :] = total
        else:
            put_coded(out_refs[len(out_refs) - z], jnp.concatenate([total for _, total in reversed(sums)], axis=0))


def add_kept(kept, came, across):
    depth, rows, width = kept.shape
    own = jax.ShapeDtypeStruct((rows, width), jnp.float32)
    heights = [rows // 8 * 9 + (FAR_PAD if z > 2 else 0) for z in reversed(range(1, depth))]
    return pl.pallas_call(
        add_kept_kernel,
        out_shape=[own] + [jax.ShapeDtypeStruct((height, width), jnp.bfloat16) for height in heights],
        compiler_params=PARAMS,
    )(kept, came, across)


def stack_kernel(left_ref, right_ref, out_ref):
    out_ref[: left_ref.shape[0]] = left_ref[...]
    out_ref[left_ref.shape[0] :] = right_ref[...]


def stack(left, right):
    return pl.pallas_call(
        stack_kernel,
        out_shape=jax.ShapeDtypeStruct((2 * left.shape[0],) + left.shape[1:], left.dtype),
        compiler_params=PARAMS,
    )(left, right)


def add_scores(queries_ref, chips, place, grads, sums_ref):
    examples, half_rank, lanes = grads.shape
    held = queries_ref.shape[1]
    step = 4 if len(chips) % 4 == 0 else 2
    here = lax.div(lax.axis_index("ex"), 2)
    for first in range(0, len(chips), step):
        sums = [jnp.zeros((step * held, lanes), jnp.float32) for _ in range(examples)]
        for k in range(half_rank):
            query = queries_ref[first : first + step, :, k * lanes : (k + 1) * lanes].astype(jnp.float32)
            query = query.reshape(step * held, lanes)
            for n in range(examples):
                sums[n] = sums[n] + query * grads[n, k : k + 1, :]
        for part in range(step):
            source = lax.bitwise_xor(here, chips[first + part])
            for n in range(examples):
                sums_ref[n, source, place] = sums[n][part * held : (part + 1) * held, :]


def first_score_kernel(parts_count, held, *refs):
    part_refs, query_refs = refs[:parts_count], refs[parts_count : parts_count + len(held)]
    grads_ref, sums_ref, total_ref = refs[parts_count + len(held) :]
    rank, tokens = total_ref.shape[0] // 2, total_ref.shape[1]
    core = lax.rem(lax.axis_index("ex"), 2)
    total_ref[...] = part_refs[0][...]
    for part_ref in part_refs[1:]:
        for rows, total in add_coded(lambda first, count: total_ref[first : first + count, :], 2 * rank, part_ref):
            total_ref[rows, :] = total
    even = total_ref[pl.ds(rank, rank // 2, stride=2), :]
    odd = total_ref[pl.ds(rank + 1, rank // 2, stride=2), :]
    token = lax.broadcasted_iota(jnp.int32, (rank, tokens), 1)
    for n in range(tokens // SEQ):
        mine = jnp.where((token >= n * SEQ) & (token < (n + 1) * SEQ), total_ref[:rank, :], 0.0)
        for side, rows in enumerate((even, odd)):
            grads_ref[n, :, side * rank : (side + 1) * rank] = lax.dot_general(
                rows, mine, LANES_BY_LANES, precision=lax.Precision.HIGHEST, preferred_element_type=jnp.float32
            )
    sums_ref[...] = jnp.zeros_like(sums_ref)
    for queries_ref, (other, chips) in zip(query_refs, held):
        add_scores(queries_ref, chips, lax.rem(core + other, 2), grads_ref, sums_ref)


def last_score_kernel(chips, grads_ref, before_ref, queries_ref, out_ref, sums_ref):
    core = lax.rem(lax.axis_index("ex"), 2)
    sums_ref[...] = before_ref[...]
    add_scores(queries_ref, chips, lax.rem(core + 1, 2), grads_ref, sums_ref)
    examples, *rows, lanes = sums_ref.shape
    sums = sums_ref[...].reshape(examples * out_ref.shape[1], lanes)
    high = sums.astype(jnp.bfloat16)
    low = (sums - high.astype(jnp.float32)).astype(jnp.bfloat16)
    ones = jnp.ones((16, lanes), jnp.bfloat16)
    row = sum(lax.dot_general(ones, part, LANES_BY_LANES, preferred_element_type=jnp.float32) for part in (high, low))
    for n in range(examples):
        out_ref[n : n + 1, :] = row[0:1, n * out_ref.shape[1] : (n + 1) * out_ref.shape[1]]


def first_scores(parts, queries, held, rank):
    tokens = parts[0].shape[1]
    examples = tokens // SEQ
    chips = 2 * queries[0].shape[0]
    return pl.pallas_call(
        functools.partial(first_score_kernel, len(parts), held),
        out_shape=[
            jax.ShapeDtypeStruct((examples, rank // 2, 2 * rank), jnp.float32),
            jax.ShapeDtypeStruct((examples, chips, 2, queries[0].shape[1], 2 * rank), jnp.float32),
        ],
        scratch_shapes=[pltpu.VMEM((2 * rank, tokens), jnp.float32)],
        compiler_params=PARAMS,
    )(*parts, *queries)


def last_scores(grads, sums, queries, chips):
    examples, all_chips, cores, held, _ = sums.shape
    return pl.pallas_call(
        functools.partial(last_score_kernel, chips),
        out_shape=jax.ShapeDtypeStruct((examples, all_chips * cores * held), jnp.float32),
        scratch_shapes=[pltpu.VMEM(sums.shape, jnp.float32)],
        compiler_params=PARAMS,
    )(grads, sums, queries)


def shards(inputs, out_grads, proj_in, proj_out, queries):
    devices = lax.axis_size("ex")
    chips = devices // 2
    depth = chips // 2
    rank = proj_in.shape[1]
    together = lax.optimization_barrier

    def swap(array, chip=0, core=0):
        distance = 2 * chip + core
        return lax.ppermute(array, "ex", [(i, i ^ distance) for i in range(devices)])

    steps = [1 << bit for bit in reversed(range(chips.bit_length() - 1))]
    held, reach = queries[None], [0]
    came_held = swap(held, chip=steps[0])
    lows = project(inputs, out_grads, proj_in.T, proj_out.T, devices)
    *given_y, given, kept_y, kept = lows
    came_y = [swap(array, core=1) for array in given_y]
    came = swap(given, core=1)
    for last, step in zip(steps, steps[1:-1]):
        held, reach = stack(held, came_held), reach + [chip ^ last for chip in reach]
        came_held = swap(held, chip=step)
    across = swap(add_given(kept_y, came_y), chip=1)
    early, early_reach = held, reach
    late, late_reach = came_held, [chip ^ steps[-2] for chip in reach]
    held, reach = stack(early, late), early_reach + late_reach
    came_held = swap(held, chip=1)
    other_early = swap(early, core=1)
    across, came, other_early = together((across, came, other_early))

    parts = list(add_kept(kept, came, across))
    late, parts = together((late, parts))
    other_late = swap(late, core=1)
    parts[1:] = [swap(part, chip=2 * z) for z, part in zip(reversed(range(1, depth)), parts[1:])]
    came_held, other_late, parts = together((came_held, other_late, parts))
    other_came = swap(came_held, core=1)
    reach_y = [chip ^ 1 for chip in reach]
    queries = [held, other_early, other_late, came_held]
    reaches = [(0, reach), (1, early_reach), (1, late_reach), (0, reach_y)]
    grads, scores = first_scores(parts, queries, reaches, rank)
    return last_scores(grads, scores, other_came, reach_y)


def solution(mesh):
    return jax.shard_map(
        shards,
        mesh=mesh,
        in_specs=(
            P("ex", "groups"),
            P("ex", "groups"),
            P("ex", None),
            P("ex", None),
            P("ex", None),
        ),
        out_specs=P(("groups", "ex"), None),
        check_vma=False,
    )
```
